256 devices in a mesh: tgt: 8 (over z_hi, core), row: 8 (over z_lo, x), col: 4 (over y).
Axes of the slice: x: 4, y: 4, z: 8 (z_hi: 4, z_lo: 2; z = z_hi * 2 + z_lo), core: 2. Of those that a mesh axis runs over, the one named last changes fastest.
Arguments:
- homolog_activation_matrix: bfloat16 [8, 128, 512, 256], P('tgt', None, ('row', 'col')), may hold values from -80 to 80
- standardizer_multiplier: float32 [256], replicated, may hold values from 0.5 to 1.5
- standardizer_offset: float32 [256], replicated, may hold values from -3 to 3
- side_mapping_matrices: bfloat16 [256, 64], replicated, may hold values from -0.375 to 0.375
- side_mapping_offsets: float32 [64], replicated, may hold values from -3 to 3
- final_channel_matrix: bfloat16 [1024, 128], replicated, may hold values from -0.1875 to 0.1875
- residue_couple_cotangent: bfloat16 [8, 512, 512, 128], P('tgt', 'row', 'col'), may hold values from -32.4 to 32.4
Outputs:
- sequence_stack_cotangent: bfloat16 [8, 128, 512, 256], P('tgt', None, ('row', 'col'))
- proj_weight_grad: float32 [256, 64], replicated
- proj_bias_grad: float32 [64], replicated
- ln_gain_grad: float32 [256], replicated
- ln_bias_grad: float32 [256], replicated
- out_weight_grad: float32 [1024, 128], replicated
- out_bias_grad: float32 [128], replicated
The draws below stay inside these ranges and needn't reach their ends.
All inputs are finite; a program needn't handle non-finite values.
Results may differ from the reference program's by a relative error of at most 0.0069.
Values may be sent and summed in bfloat16 or wider, within the bound.
A program may use at most 128 MiB of HBM per device.

```python
import math
import jax
import jax.numpy as jnp
from jax import lax

CM = 256
CH = 32
CZ = 128
S = 128
NT = 8
R = 512


def draw_homolog_activation_matrix(key, part):
    key = jax.random.fold_in(key, 11)
    keys = jax.random.split(key, 3)
    row_scale = jnp.exp(jax.random.uniform(keys[1], (NT, S, R, 1), jnp.float32) * math.log(10.0))
    col_scale = jnp.exp(jax.random.uniform(keys[2], (1, 1, 1, CM), jnp.float32, -math.log(2.0), math.log(2.0)))
    base = jnp.clip(jax.random.normal(keys[0], (NT, S, R, CM), jnp.float32), -4.0, 4.0)
    return (base * row_scale * col_scale).astype(jnp.bfloat16)


def draw_residue_couple_cotangent(key, part):
    key = jax.random.fold_in(key, 7)
    keys = jax.random.split(key, 1)
    target_pos = jnp.arange(NT, dtype=jnp.float32) / max(NT - 1, 1)
    res_pos = jnp.arange(R, dtype=jnp.float32) / max(R - 1, 1)
    rise = target_pos[:, None, None, None] + res_pos[None, :, None, None] + res_pos[None, None, :, None]
    scale = jnp.exp(math.log(3.0) * rise)
    base = 0.3 * jnp.clip(jax.random.normal(keys[0], (NT, R, R, CZ), jnp.float32), -4.0, 4.0)
    return (base * scale).astype(jnp.bfloat16)


def gaussian(own_key, shape, spread, most, kind=jnp.bfloat16):
    array = jax.random.normal(own_key, shape, jnp.float32) * spread
    return jnp.minimum(jnp.maximum(array, -most), most).astype(kind)


def setup_inputs(seed: int = 0) -> dict:
    key_list = jax.random.split(jax.random.key(seed), 8)
    return {
        "homolog_activation_matrix": draw_homolog_activation_matrix(jax.random.fold_in(key_list[7], 71), 0),
        "standardizer_multiplier": jnp.clip(jax.random.uniform(key_list[1], (CM,), jnp.float32, 0.5, 1.5), 0.5, 1.5),
        "standardizer_offset": gaussian(key_list[2], (CM,), 0.5, 3.0, jnp.float32),
        "side_mapping_matrices": gaussian(key_list[3], (CM, 2 * CH), CM ** -0.5, 0.375),
        "side_mapping_offsets": gaussian(key_list[4], (2 * CH,), 0.5, 3.0, jnp.float32),
        "final_channel_matrix": gaussian(key_list[5], (CH * CH, CZ), (CH * CH) ** -0.5, 0.1875),
        "residue_couple_cotangent": draw_residue_couple_cotangent(jax.random.fold_in(key_list[7], 71), 0),
    }


def layer_normalize(raw, standardizer_multiplier, standardizer_offset):
    values = raw.astype(jnp.float32)
    centre = lax.optimization_barrier(jnp.mean(values, -1, keepdims=True))
    centred = values - centre
    inverse_deviation = lax.rsqrt(lax.optimization_barrier(jnp.mean(centred * centred, -1, keepdims=True)) + 1e-05)
    normalized_input = centred * inverse_deviation
    norm_result = (normalized_input * standardizer_multiplier + standardizer_offset).astype(jnp.bfloat16)
    return (normalized_input, inverse_deviation, norm_result)

def reference(homolog_activation_matrix, standardizer_multiplier, standardizer_offset, side_mapping_matrices, side_mapping_offsets, final_channel_matrix, residue_couple_cotangent):
    wide_weight = final_channel_matrix.astype(jnp.float32)
    block_rows = math.gcd(R, 64)

    def lone_destination(partial_pieces):
        single_alignment, single_gradient = partial_pieces
        normalized_input, inverse_deviation, norm_result = layer_normalize(single_alignment, standardizer_multiplier, standardizer_offset)
        flat_out = norm_result.reshape(S * R, CM)
        projected = (jnp.dot(flat_out, side_mapping_matrices, preferred_element_type=jnp.float32) + side_mapping_offsets).astype(jnp.bfloat16)
        projected = projected.reshape(S, R, 2 * CH)
        left_feats = projected[..., :CH].astype(jnp.float32)
        right_feats = projected[..., CH:].astype(jnp.float32)

        def block_step(running, row_start):
            right_acc, wide_accumulator = running
            grad_block = lax.dynamic_slice_in_dim(single_gradient, row_start, block_rows, 0).astype(jnp.float32)
            left_block = lax.dynamic_slice_in_dim(left_feats, row_start, block_rows, 1)
            pair_back = jnp.einsum('ije,ke->ijk', grad_block, wide_weight).astype(jnp.bfloat16)
            pair_back = lax.optimization_barrier(pair_back).astype(jnp.float32).reshape(block_rows, R, CH, CH)
            row_grad = jnp.einsum('ijcd,sjd->sic', pair_back, right_feats) / S
            right_acc = right_acc + jnp.einsum('ijcd,sic->sjd', pair_back, left_block)
            outer = (jnp.einsum('sic,sjd->ijcd', left_block, right_feats) / S).astype(jnp.bfloat16)
            outer = lax.optimization_barrier(outer).astype(jnp.float32).reshape(block_rows, R, CH * CH)
            wide_accumulator = wide_accumulator + jnp.einsum('ijk,ije->ke', outer, grad_block)
            return ((right_acc, wide_accumulator), row_grad)
        starts = jnp.arange(R // block_rows, dtype=jnp.int32) * block_rows
        initial = (jnp.zeros((S, R, CH), jnp.float32), jnp.zeros((CH * CH, CZ), jnp.float32))
        (right_acc, wide_accumulator), row_blocks = lax.scan(block_step, initial, starts)
        left_grad = jnp.moveaxis(row_blocks, 0, 1).reshape(S, R, CH)
        side_grad = jnp.concatenate([left_grad, right_acc / S], -1)
        side_round = side_grad.astype(jnp.bfloat16)
        flat_side = side_round.reshape(S * R, 2 * CH)
        norm_out_grad = jnp.dot(flat_side, side_mapping_matrices.T, preferred_element_type=jnp.float32).reshape(S, R, CM)
        weight_component = jnp.dot(flat_out.T, flat_side, preferred_element_type=jnp.float32)
        bias_component = lax.optimization_barrier(jnp.sum(side_grad, (0, 1)))
        gain_component = lax.optimization_barrier(jnp.sum(norm_out_grad * normalized_input, (0, 1)))
        shift_component = lax.optimization_barrier(jnp.sum(norm_out_grad, (0, 1)))
        scaled_values = norm_out_grad * standardizer_multiplier
        sequence_stack_cotangent = inverse_deviation * (scaled_values - lax.optimization_barrier(jnp.mean(scaled_values, -1, keepdims=True)) - normalized_input * lax.optimization_barrier(jnp.mean(scaled_values * normalized_input, -1, keepdims=True)))
        output_bias_component = lax.optimization_barrier(jnp.sum(single_gradient.astype(jnp.float32), (0, 1)))
        return (sequence_stack_cotangent.astype(jnp.bfloat16), (weight_component, bias_component, gain_component, shift_component, wide_accumulator, output_bias_component))
    sequence_stack_cotangent, addend_contributions = lax.map(lone_destination, (homolog_activation_matrix, residue_couple_cotangent))
    factor = 1.0 / (NT * R)
    running_totals = [lax.optimization_barrier(jnp.sum(term, 0)) * factor for term in addend_contributions]
    return (sequence_stack_cotangent, running_totals[0], running_totals[1], running_totals[2], running_totals[3], running_totals[4], running_totals[5])
```

```python
import functools

import jax
import jax.numpy as jnp
from jax import lax
from jax.experimental import pallas as pl
from jax.experimental.pallas import tpu as pltpu
from jax.sharding import PartitionSpec as P

CM = 256
CH = 32
CZ = 128
S = 128
F32 = jnp.float32
BF16 = jnp.bfloat16
NT_DIMS = (((1,), (1,)), ((), ()))
NN_DIMS = (((1,), (0,)), ((), ()))


def mm(a, b, dims=NN_DIMS):
    return lax.dot_general(a, b, dims, preferred_element_type=F32)


def axis_sizes():
    return lax.axis_size("tgt"), lax.axis_size("row"), lax.axis_size("col")


def axis_places():
    return lax.axis_index("tgt"), lax.axis_index("row"), lax.axis_index("col")


def descriptor(src, dst, send, recv, where):
    return pltpu.make_async_remote_copy(
        src_ref=src,
        dst_ref=dst,
        send_sem=send,
        recv_sem=recv,
        device_id=where,
        device_id_type=pl.DeviceIdType.MESH,
    )


def push(*args):
    descriptor(*args).start()


def sent(*args):
    descriptor(*args).wait_send()


def arrived(*args):
    descriptor(*args).wait_recv()


def greet(nt, nr, nc, t, r, c):
    barrier = pltpu.get_barrier_semaphore()
    flat = r * nc + c
    for k in range(1, nr * nc):
        other = lax.rem(flat + k, nr * nc)
        pl.semaphore_signal(
            barrier,
            inc=1,
            device_id={"row": other // nc, "col": lax.rem(other, nc)},
            device_id_type=pl.DeviceIdType.MESH,
        )
    for k in range(1, nt):
        pl.semaphore_signal(
            barrier,
            inc=1,
            device_id={"tgt": lax.rem(t + k, nt)},
            device_id_type=pl.DeviceIdType.MESH,
        )


def meet(nt, nr, nc):
    pl.semaphore_wait(pltpu.get_barrier_semaphore(), nr * nc - 1 + nt - 1)


def kernel(
    sizes,
    h_ref,
    mult_ref,
    off_ref,
    pm_ref,
    pb_ref,
    w_ref,
    g_ref,
    dx_out,
    pw_out,
    pbias_out,
    gain_out,
    shift_out,
    ow_out,
    ob_out,
    h,
    g,
    nrm,
    inv,
    no,
    lt,
    lmat,
    rt,
    rown,
    rf,
    wf,
    wp,
    pair,
    rp,
    lp,
    rr,
    lr,
    side,
    on,
    dw,
    obacc,
    a1,
    s1,
    a2,
    a3,
    a4,
    a5,
    pwt,
    vec,
    acc,
    sb,
    b1,
    b2,
    b3,
    b4,
    local_sem,
    gl_send,
    gl_recv,
    gr_send,
    gr_recv,
    sl_send,
    sl_recv,
    sr_send,
    sr_recv,
    a_row_send,
    a_row_recv,
    a_col_send,
    a_col_recv,
    a_tgt_send,
    a_tgt_recv,
    a_col2_send,
    a_col2_recv,
    a_row2_send,
    a_row2_recv,
    b_row_send,
    b_row_recv,
    b_col_send,
    b_col_recv,
    b_tgt_send,
    b_tgt_recv,
    b_row2_send,
    b_row2_recv,
):
    nt, nr, nc, rl = sizes
    rpc = nr // nc
    ni, nj = rl * nc, rl * nr
    lrows = rl * CH
    t, r, c = axis_places()
    home = lax.div(r, rpc)
    block = lax.rem(r, rpc) * nc + c
    mine = c == home

    h_in = pltpu.make_async_copy(h_ref, h, local_sem.at[0])
    h_in.start()
    g_in = pltpu.make_async_copy(g_ref, g, local_sem.at[1])
    g_in.start()
    greet(nt, nr, nc, t, r, c)

    mult = mult_ref[...]
    off = off_ref[...]
    pt32 = pm_ref[...].astype(F32).T
    pt = pt32.astype(BF16)
    bias = jnp.broadcast_to(pb_ref[...], (S, 2 * CH)).T

    wf[...] = w_ref[...].astype(F32)

    def reorder(d, _):
        rows = wf[pl.ds(d, CH, stride=CH), :]
        wp[pl.ds(pl.multiple_of(d * CH, CH), CH), :] = rows.astype(BF16)
        return 0

    lax.fori_loop(0, CH, reorder, 0)
    h_in.wait()

    def normalise(k, _):
        rows = pl.ds(pl.multiple_of(k * 128, 128), 128)
        x = h[rows, :].astype(F32)
        centred = x - jnp.mean(x, -1, keepdims=True)
        scale = lax.rsqrt(jnp.mean(centred * centred, -1, keepdims=True) + 1e-05)
        x = centred * scale
        nrm[0, rows, :] = x[:, :128]
        nrm[1, rows, :] = x[:, 128:]
        inv[rows, :] = jnp.broadcast_to(scale, (128, 128))
        return 0

    lax.fori_loop(0, S * rl // 128, normalise, 0)

    def project(k, _):
        at = pl.ds(k, S, stride=rl)
        x = jnp.concatenate([nrm[0, at, :], nrm[1, at, :]], 1)
        row = (x * mult + off).astype(BF16)
        no[pl.ds(pl.multiple_of(k * S, S), S), :] = row
        y = (mm(pt, row, NT_DIMS) + bias).astype(BF16)
        lt[pl.ds(pl.multiple_of(c * lrows + k * CH, CH), CH), :] = y[:CH]
        rf[pl.ds(pl.multiple_of(k * CH, CH), CH), :] = y[CH:].astype(F32)
        return 0

    lax.fori_loop(0, rl, project, 0)

    def turn(d, _):
        rown[d] = rf[pl.ds(d, rl, stride=CH), :].astype(BF16)
        return 0

    lax.fori_loop(0, CH, turn, 0)
    meet(nt, nr, nc)

    def left_block(k):
        return lt.at[pl.ds(pl.multiple_of(k * lrows, lrows), lrows), :]

    def right_block(k):
        return rt.at[:, pl.ds(pl.multiple_of(k * rl, rl), rl), :]

    def gather_left(k):
        q = lax.rem(c + k, nc)
        return left_block(c), left_block(c), gl_send.at[k], gl_recv.at[c], {"col": q}

    def gather_left_in(k):
        q = lax.rem(c + k, nc)
        return left_block(q), left_block(q), gl_send.at[k], gl_recv.at[q], {"col": q}

    def gather_right(k):
        q = lax.rem(r + k, nr)
        where = {"row": q, "col": home}
        return rown, right_block(block), gr_send.at[k], gr_recv.at[block], where

    def gather_right_in(k):
        where = {"row": rpc * c + k // nc, "col": k % nc}
        return rown, right_block(k), gr_send.at[0], gr_recv.at[k], where

    for k in range(1, nc):
        push(*gather_left(k))
    for k in range(1, nr):
        push(*gather_right(k))

    @pl.when(jnp.logical_not(mine))
    def _():
        push(*gather_right(0))

    @pl.when(mine)
    def _():
        rt[:, pl.ds(pl.multiple_of(block * rl, rl), rl), :] = rown[...]

    g_in.wait()
    obacc[...] = jnp.zeros_like(obacc)

    def back(k, _):
        rows = g[pl.ds(pl.multiple_of(k * 2 * nj, 2 * nj), 2 * nj), :]
        y = mm(wp[...], rows, NT_DIMS).astype(BF16)
        for q in range(2):
            at = pl.ds(pl.multiple_of((2 * k + q) * CH, CH), CH)
            for d in range(CH):
                pair[at, d * nj : (d + 1) * nj] = y[d * CH : (d + 1) * CH, q * nj : (q + 1) * nj]
        obacc[...] += jnp.sum(rows.astype(F32).reshape(2 * nj // 8, 8, CZ), 0)
        return 0

    lax.fori_loop(0, ni // 2, back, 0)

    for k in range(1, nc):
        arrived(*gather_left_in(k))

    def flip(k, _):
        at = pl.ds(pl.multiple_of(k * 128, 128), 128)
        lmat[:, at] = lt[at, :].T
        return 0

    lax.fori_loop(0, ni * CH // 128, flip, 0)

    def right_step(k, _):
        lanes = pl.ds(pl.multiple_of(k * 2 * nj, 2 * nj), 2 * nj)
        y = mm(lmat[...], pair[:, lanes]).T
        rp[pl.ds(2 * k, 2)] = y.reshape(2, nj, S).astype(BF16)
        return 0

    lax.fori_loop(0, CH // 2, right_step, 0)

    def scatter_right(k):
        where = {"row": rpc * c + k // nc, "col": k % nc}
        return rp.at[:, pl.ds(k * rl, rl), :], rr.at[r], sr_send.at[k], sr_recv.at[r], where

    def scatter_right_in(k):
        q = lax.rem(r + k, nr)
        where = {"row": q, "col": home}
        return rp.at[:, pl.ds(0, rl), :], rr.at[q], sr_send.at[0], sr_recv.at[q], where

    for k in range(nr):
        own = jnp.logical_and(mine, block == k)

        @pl.when(jnp.logical_not(own))
        def _():
            push(*scatter_right(k))

        @pl.when(own)
        def _():
            rr[r] = rp[:, k * rl : (k + 1) * rl, :]

    for k in range(nr):
        own = jnp.logical_and(mine, block == k)

        @pl.when(jnp.logical_not(own))
        def _():
            arrived(*gather_right_in(k))

    def left_rows(k):
        return pl.ds(pl.multiple_of(k * lrows, lrows), lrows)

    def scatter_left(k):
        q = lax.rem(c + k, nc)
        return lp.at[k], lr.at[c], sl_send.at[k], sl_recv.at[c], {"col": q}

    def scatter_left_in(k):
        q = lax.rem(c + k, nc)
        return lp.at[k], lr.at[q], sl_send.at[k], sl_recv.at[q], {"col": q}

    for k in range(1, nc + 1):
        q = lax.rem(c + k, nc)
        right_all = rt[...].reshape(CH * nj, S)
        y = mm(pair[left_rows(q), :], right_all).astype(BF16)
        if k < nc:
            lp[k] = y
            push(*scatter_left(k))
        else:
            lr[c] = y

    dw[...] = jnp.zeros_like(dw)

    def weigh(k, _):
        rows = lt[pl.ds(pl.multiple_of(k * 8 * CH, 8 * CH), 8 * CH), :]
        for v in range(8):
            part = rt[v * 4 : (v + 1) * 4].reshape(4 * nj, S)
            y = mm(rows, part, NT_DIMS).astype(BF16)
            for q in range(8):
                for d in range(4):
                    on[(v * 4 + d) * CH : (v * 4 + d + 1) * CH, q * nj : (q + 1) * nj] = y[
                        q * CH : (q + 1) * CH, d * nj : (d + 1) * nj
                    ]
        dw[...] += mm(on[...], g[pl.ds(pl.multiple_of(k * 8 * nj, 8 * nj), 8 * nj), :])
        return 0

    lax.fori_loop(0, ni // 8, weigh, 0)

    ar = CH * CH // nr
    ac = ar // nc

    def a_row(k):
        q = lax.rem(r + k, nr)
        src = dw.at[pl.ds(pl.multiple_of(q * ar, ar), ar), :]
        return src, a1.at[r], a_row_send.at[k], a_row_recv.at[r], {"row": q}

    def a_row_in(k):
        q = lax.rem(r + k, nr)
        src = dw.at[pl.ds(0, ar), :]
        return src, a1.at[q], a_row_send.at[k], a_row_recv.at[q], {"row": q}

    for k in range(1, nr):
        push(*a_row(k))
    a1[r] = dw[pl.ds(pl.multiple_of(r * ar, ar), ar), :]

    for k in range(1, nc):
        arrived(*scatter_left_in(k))
    for k in range(1, nr):
        arrived(*scatter_right_in(k))

    @pl.when(jnp.logical_not(mine))
    def _():
        arrived(*scatter_right_in(0))

    def sum_left(k, _):
        at = pl.ds(pl.multiple_of(k * 128, 128), 128)
        total = lr[0, at, :].astype(F32)
        for q in range(1, nc):
            total += lr[q, at, :].astype(F32)
        side[at, :] = total * (1.0 / S)
        return 0

    lax.fori_loop(0, lrows // 128, sum_left, 0)

    def sum_right(k, _):
        at = pl.ds(k * 8, 8)
        total = rr[0, at].astype(F32)
        for q in range(1, nr):
            total += rr[q, at].astype(F32)
        to = pl.ds(pl.multiple_of(lrows + k * 8 * rl, 8 * rl), 8 * rl)
        side[to, :] = total.reshape(8 * rl, S) * (1.0 / S)
        return 0

    lax.fori_loop(0, CH // 8, sum_right, 0)

    for k in range(1, nr):
        arrived(*a_row_in(k))
    total = a1[0]
    for q in range(1, nr):
        total += a1[q]
    s1[...] = total

    def a_col(k):
        q = lax.rem(c + k, nc)
        src = s1.at[pl.ds(pl.multiple_of(q * ac, ac), ac), :]
        return src, a2.at[c], a_col_send.at[k], a_col_recv.at[c], {"col": q}

    def a_col_in(k):
        q = lax.rem(c + k, nc)
        return s1.at[pl.ds(0, ac), :], a2.at[q], a_col_send.at[k], a_col_recv.at[q], {"col": q}

    for k in range(1, nc):
        push(*a_col(k))
    a2[c] = s1[pl.ds(pl.multiple_of(c * ac, ac), ac), :]

    pwt[...] = jnp.zeros_like(pwt)
    acc[...] = jnp.zeros_like(acc)

    def finish(k, _):
        left = side[pl.ds(pl.multiple_of(k * CH, CH), CH), :]
        right = side[pl.ds(lrows + k, CH, stride=rl), :]
        both = jnp.concatenate([left, right], 0)
        rounded = both.astype(BF16)
        turned = both.T
        acc[:, 2 * CM : 2 * CM + 2 * CH] += jnp.sum(turned.reshape(S // 8, 8, 2 * CH), 0)
        grad = mm(turned.astype(BF16), pt)
        pwt[...] += mm(rounded, no[pl.ds(pl.multiple_of(k * S, S), S), :])
        at = pl.ds(k, S, stride=rl)
        x = jnp.concatenate([nrm[0, at, :], nrm[1, at, :]], 1)
        scale = inv[at, :]
        acc[:, :CM] += jnp.sum((grad * x).reshape(S // 8, 8, CM), 0)
        acc[:, CM : 2 * CM] += jnp.sum(grad.reshape(S // 8, 8, CM), 0)
        scaled = grad * mult
        dx = scaled - jnp.mean(scaled, -1, keepdims=True) - x * jnp.mean(scaled * x, -1, keepdims=True)
        nrm[0, at, :] = dx[:, :128] * scale
        nrm[1, at, :] = dx[:, 128:] * scale
        return 0

    lax.fori_loop(0, rl, finish, 0)

    pr = 2 * 2 * CH // nr
    vr = 8 // nr
    vec[...] = jnp.zeros_like(vec)
    small = jnp.sum(acc[...], 0, keepdims=True)
    vec[0:1, : 2 * CH] = small[:, 2 * CM : 2 * CM + 2 * CH]
    for k in range(4):
        vec[1 + k : 2 + k, :] = small[:, k * 128 : (k + 1) * 128]
    vec[5:6, :] = jnp.sum(obacc[...], 0, keepdims=True)
    weights = pwt[...]
    stacked = jnp.concatenate([weights[:, :128], weights[:, 128:]], 0)
    sb[...] = jnp.zeros_like(sb)
    for q in range(nr):
        sb[q, :pr, :] = stacked[q * pr : (q + 1) * pr]
        sb[q, pr : pr + vr, :] = vec[q * vr : (q + 1) * vr, :]

    def b_row(k):
        q = lax.rem(r + k, nr)
        return sb.at[q], b1.at[r], b_row_send.at[k], b_row_recv.at[r], {"row": q}

    def b_row_in(k):
        q = lax.rem(r + k, nr)
        return sb.at[q], b1.at[q], b_row_send.at[k], b_row_recv.at[q], {"row": q}

    for k in range(1, nr):
        push(*b_row(k))
    b1[r] = sb[r]

    for k in range(1, nc):
        arrived(*a_col_in(k))
    total = a2[0]
    for q in range(1, nc):
        total += a2[q]
    a3[t] = total

    def a_tgt(k):
        q = lax.rem(t + k, nt)
        return a3.at[t], a3.at[t], a_tgt_send.at[k], a_tgt_recv.at[t], {"tgt": q}

    def a_tgt_in(k):
        q = lax.rem(t + k, nt)
        return a3.at[q], a3.at[q], a_tgt_send.at[k], a_tgt_recv.at[q], {"tgt": q}

    for k in range(1, nt):
        push(*a_tgt(k))

    def emit(k, _):
        rows = pl.ds(pl.multiple_of(k * 128, 128), 128)
        h[rows, :128] = nrm[0, rows, :].astype(BF16)
        h[rows, 128:] = nrm[1, rows, :].astype(BF16)
        return 0

    lax.fori_loop(0, S * rl // 128, emit, 0)
    dx_copy = pltpu.make_async_copy(h, dx_out, local_sem.at[2])
    dx_copy.start()

    for k in range(1, nr):
        arrived(*b_row_in(k))
    total = b1[0]
    for q in range(1, nr):
        total += b1[q]
    b2[c] = total

    def b_col(k):
        q = lax.rem(c + k, nc)
        return b2.at[c], b2.at[c], b_col_send.at[k], b_col_recv.at[c], {"col": q}

    def b_col_in(k):
        q = lax.rem(c + k, nc)
        return b2.at[q], b2.at[q], b_col_send.at[k], b_col_recv.at[q], {"col": q}

    for k in range(1, nc):
        push(*b_col(k))

    for k in range(1, nt):
        arrived(*a_tgt_in(k))
    total = a3[0]
    for q in range(1, nt):
        total += a3[q]
    a4[c] = total

    def a_col2(k):
        q = lax.rem(c + k, nc)
        return a4.at[c], a4.at[c], a_col2_send.at[k], a_col2_recv.at[c], {"col": q}

    def a_col2_in(k):
        q = lax.rem(c + k, nc)
        return a4.at[q], a4.at[q], a_col2_send.at[k], a_col2_recv.at[q], {"col": q}

    for k in range(1, nc):
        push(*a_col2(k))

    for k in range(1, nc):
        arrived(*b_col_in(k))
    total = b2[0]
    for q in range(1, nc):
        total += b2[q]
    b3[t] = total

    def b_tgt(k):
        q = lax.rem(t + k, nt)
        return b3.at[t], b3.at[t], b_tgt_send.at[k], b_tgt_recv.at[t], {"tgt": q}

    def b_tgt_in(k):
        q = lax.rem(t + k, nt)
        return b3.at[q], b3.at[q], b_tgt_send.at[k], b_tgt_recv.at[q], {"tgt": q}

    for k in range(1, nt):
        push(*b_tgt(k))

    for k in range(1, nc):
        arrived(*a_col2_in(k))
    a5[r] = a4[...].reshape(ar, CZ)

    def a_row2(k):
        q = lax.rem(r + k, nr)
        return a5.at[r], a5.at[r], a_row2_send.at[k], a_row2_recv.at[r], {"row": q}

    def a_row2_in(k):
        q = lax.rem(r + k, nr)
        return a5.at[q], a5.at[q], a_row2_send.at[k], a_row2_recv.at[q], {"row": q}

    for k in range(1, nr):
        push(*a_row2(k))

    for k in range(1, nt):
        arrived(*b_tgt_in(k))
    total = b3[0]
    for q in range(1, nt):
        total += b3[q]
    b4[r] = total

    def b_row2(k):
        q = lax.rem(r + k, nr)
        return b4.at[r], b4.at[r], b_row2_send.at[k], b_row2_recv.at[r], {"row": q}

    def b_row2_in(k):
        q = lax.rem(r + k, nr)
        return b4.at[q], b4.at[q], b_row2_send.at[k], b_row2_recv.at[q], {"row": q}

    for k in range(1, nr):
        push(*b_row2(k))

    factor = 1.0 / (nt * nr * nc * rl)
    for k in range(1, nr):
        arrived(*a_row2_in(k))

    def place(d, _):
        at = pl.multiple_of(d * CH, CH)
        rows = a5[lax.div(at, ar), pl.ds(pl.multiple_of(lax.rem(at, ar), CH), CH), :]
        ow_out[pl.ds(d, CH, stride=CH), :] = rows * (factor / S)
        return 0

    lax.fori_loop(0, CH, place, 0)

    for k in range(1, nr):
        arrived(*b_row2_in(k))
    whole = b4[:, :pr, :].reshape(4 * CH, 128) * factor
    pw_out[:128, :] = whole[: 2 * CH].T
    pw_out[128:, :] = whole[2 * CH :].T
    for q in range(nr):
        vec[q * vr : (q + 1) * vr, :] = b4[q, pr : pr + vr, :] * factor
    pbias_out[...] = vec[0:1, : 2 * CH]
    gain_out[...] = jnp.concatenate([vec[1:2, :], vec[2:3, :]], 1)
    shift_out[...] = jnp.concatenate([vec[3:4, :], vec[4:5, :]], 1)
    ob_out[...] = vec[5:6, :]

    dx_copy.wait()
    for k in range(1, nc):
        sent(*gather_left(k))
        sent(*scatter_left(k))
        sent(*a_col(k))
        sent(*a_col2(k))
        sent(*b_col(k))
    for k in range(1, nr):
        sent(*gather_right(k))
        sent(*a_row(k))
        sent(*a_row2(k))
        sent(*b_row(k))
        sent(*b_row2(k))
    for k in range(1, nt):
        sent(*a_tgt(k))
        sent(*b_tgt(k))

    @pl.when(jnp.logical_not(mine))
    def _():
        sent(*gather_right(0))

    for k in range(nr):
        own = jnp.logical_and(mine, block == k)

        @pl.when(jnp.logical_not(own))
        def _():
            sent(*scatter_right(k))


def per_device(
    homolog_activation_matrix,
    standardizer_multiplier,
    standardizer_offset,
    side_mapping_matrices,
    side_mapping_offsets,
    final_channel_matrix,
    residue_couple_cotangent,
):
    nt, nr, nc = axis_sizes()
    rl = homolog_activation_matrix.shape[2]
    ni, nj = rl * nc, rl * nr
    ar = CH * CH // nr
    pr = 4 * CH // nr + 8
    vmem = functools.partial(pl.BlockSpec, memory_space=pltpu.VMEM)
    hbm = functools.partial(pl.BlockSpec, memory_space=pl.ANY)

    def sems(n):
        return [pltpu.SemaphoreType.DMA((n,)), pltpu.SemaphoreType.DMA((n,))]

    results = pl.pallas_call(
        functools.partial(kernel, (nt, nr, nc, rl)),
        out_shape=(
            jax.ShapeDtypeStruct((S * rl, CM), BF16),
            jax.ShapeDtypeStruct((CM, 2 * CH), F32),
            jax.ShapeDtypeStruct((1, 2 * CH), F32),
            jax.ShapeDtypeStruct((1, CM), F32),
            jax.ShapeDtypeStruct((1, CM), F32),
            jax.ShapeDtypeStruct((CH * CH, CZ), F32),
            jax.ShapeDtypeStruct((1, CZ), F32),
        ),
        in_specs=[hbm(), vmem(), vmem(), vmem(), vmem(), vmem(), hbm()],
        out_specs=(hbm(), vmem(), vmem(), vmem(), vmem(), vmem(), vmem()),
        scratch_shapes=[
            pltpu.VMEM((S * rl, CM), BF16),
            pltpu.VMEM((ni * nj, CZ), BF16),
            pltpu.VMEM((2, S * rl, 128), F32),
            pltpu.VMEM((S * rl, 128), F32),
            pltpu.VMEM((S * rl, CM), BF16),
            pltpu.VMEM((ni * CH, S), BF16),
            pltpu.VMEM((S, ni * CH), BF16),
            pltpu.VMEM((CH, nj, S), BF16),
            pltpu.VMEM((CH, rl, S), BF16),
            pltpu.VMEM((rl * CH, S), F32),
            pltpu.VMEM((CH * CH, CZ), F32),
            pltpu.VMEM((CH * CH, CZ), BF16),
            pltpu.VMEM((ni * CH, CH * nj), BF16),
            pltpu.VMEM((CH, nj, S), BF16),
            pltpu.VMEM((nc, rl * CH, S), BF16),
            pltpu.VMEM((nr, CH, rl, S), BF16),
            pltpu.VMEM((nc, rl * CH, S), BF16),
            pltpu.VMEM((2 * rl * CH, S), F32),
            pltpu.VMEM((CH * CH, 8 * nj), BF16),
            pltpu.VMEM((CH * CH, CZ), F32),
            pltpu.VMEM((8, CZ), F32),
            pltpu.VMEM((nr, ar, CZ), F32),
            pltpu.VMEM((ar, CZ), F32),
            pltpu.VMEM((nc, ar // nc, CZ), F32),
            pltpu.VMEM((nt, ar // nc, CZ), F32),
            pltpu.VMEM((nc, ar // nc, CZ), F32),
            pltpu.VMEM((nr, ar, CZ), F32),
            pltpu.VMEM((2 * CH, CM), F32),
            pltpu.VMEM((8, 128), F32),
            pltpu.VMEM((8, 2 * CM + 128), F32),
            pltpu.VMEM((nr, pr, 128), F32),
            pltpu.VMEM((nr, pr, 128), F32),
            pltpu.VMEM((nc, pr, 128), F32),
            pltpu.VMEM((nt, pr, 128), F32),
            pltpu.VMEM((nr, pr, 128), F32),
            pltpu.SemaphoreType.DMA((3,)),
        ]
        + sems(nc)
        + sems(nr)
        + sems(nc)
        + sems(nr)
        + sems(nr)
        + sems(nc)
        + sems(nt)
        + sems(nc)
        + sems(nr)
        + sems(nr)
        + sems(nc)
        + sems(nt)
        + sems(nr),
        compiler_params=pltpu.CompilerParams(
            collective_id=0, has_side_effects=True, vmem_limit_bytes=56 * 1024 * 1024
        ),
        cost_estimate=pl.CostEstimate(
            flops=10 * ni * nj * CH * CH * CZ, bytes_accessed=5 * 1024 * 1024, transcendentals=0
        ),
    )(
        homolog_activation_matrix.reshape(S * rl, CM),
        standardizer_multiplier.reshape(1, CM),
        standardizer_offset.reshape(1, CM),
        side_mapping_matrices,
        side_mapping_offsets.reshape(1, 2 * CH),
        final_channel_matrix,
        residue_couple_cotangent.reshape(ni * nj, CZ),
    )
    return (
        results[0].reshape(1, S, rl, CM),
        results[1],
        results[2].reshape(2 * CH),
        results[3].reshape(CM),
        results[4].reshape(CM),
        results[5],
        results[6].reshape(CZ),
    )


def solution(mesh):
    placed = (
        P("tgt", None, ("row", "col"), None),
        P(),
        P(),
        P(),
        P(),
        P(),
        P("tgt", "row", "col", None),
    )
    return jax.shard_map(
        per_device,
        mesh=mesh,
        in_specs=placed,
        out_specs=(P("tgt", None, ("row", "col"), None), P(), P(), P(), P(), P(), P()),
        check_vma=False,
    )
```

```python
import functools

import jax
import jax.numpy as jnp
from jax import lax
from jax.experimental import pallas as pl
from jax.experimental.pallas import tpu as pltpu
from jax.sharding import PartitionSpec as P

CM = 256
CH = 32
CZ = 128
S = 128
F32 = jnp.float32
BF16 = jnp.bfloat16
NT_DIMS = (((1,), (1,)), ((), ()))
NN_DIMS = (((1,), (0,)), ((), ()))


def mm(a, b, dims=NN_DIMS):
    return lax.dot_general(a, b, dims, preferred_element_type=F32)


def axis_sizes():
    return lax.axis_size("tgt"), lax.axis_size("row"), lax.axis_size("col")


def axis_places():
    return lax.axis_index("tgt"), lax.axis_index("row"), lax.axis_index("col")


def descriptor(src, dst, send, recv, where):
    return pltpu.make_async_remote_copy(
        src_ref=src,
        dst_ref=dst,
        send_sem=send,
        recv_sem=recv,
        device_id=where,
        device_id_type=pl.DeviceIdType.MESH,
    )


def push(*args):
    descriptor(*args).start()


def sent(*args):
    descriptor(*args).wait_send()


def arrived(*args):
    descriptor(*args).wait_recv()


def greet(nt, nr, nc, t, r, c):
    barrier = pltpu.get_barrier_semaphore()
    flat = r * nc + c
    for k in range(1, nr * nc):
        other = lax.rem(flat + k, nr * nc)
        pl.semaphore_signal(
            barrier,
            inc=1,
            device_id={"row": other // nc, "col": lax.rem(other, nc)},
            device_id_type=pl.DeviceIdType.MESH,
        )
    for k in range(1, nt):
        pl.semaphore_signal(
            barrier,
            inc=1,
            device_id={"tgt": lax.rem(t + k, nt)},
            device_id_type=pl.DeviceIdType.MESH,
        )


def meet(nt, nr, nc):
    pl.semaphore_wait(pltpu.get_barrier_semaphore(), nr * nc - 1 + nt - 1)


def kernel(
    sizes,
    h_ref,
    mult_ref,
    off_ref,
    pm_ref,
    pb_ref,
    w_ref,
    g_ref,
    dx_out,
    pw_out,
    pbias_out,
    gain_out,
    shift_out,
    ow_out,
    ob_out,
    h,
    g,
    nrm,
    inv,
    no,
    lt,
    lmat,
    rt,
    rown,
    rf,
    wf,
    wp,
    pair,
    rp,
    lp,
    ra,
    rb,
    ms,
    rr,
    la,
    lb,
    side,
    on,
    dw,
    dwb,
    obacc,
    a1,
    s1,
    a2,
    a3,
    a4,
    a5,
    pwt,
    vec,
    acc,
    sb,
    b1,
    b2,
    b3,
    b4,
    local_sem,
    gl_send,
    gl_recv,
    gl2_send,
    gl2_recv,
    gr1_send,
    gr1_recv,
    gr_send,
    gr_recv,
    gr2_send,
    gr2_recv,
    sr1_send,
    sr1_recv,
    sr2_send,
    sr2_recv,
    sr3_send,
    sr3_recv,
    sl1_send,
    sl1_recv,
    sl2_send,
    sl2_recv,
    a_row_send,
    a_row_recv,
    a_col_send,
    a_col_recv,
    a_tgt_send,
    a_tgt_recv,
    a_col2_send,
    a_col2_recv,
    a_row2_send,
    a_row2_recv,
    b_row_send,
    b_row_recv,
    b_col_send,
    b_col_recv,
    b_tgt_send,
    b_tgt_recv,
    b_row2_send,
    b_row2_recv,
):
    nt, nr, nc, rl = sizes
    rpc = nr // nc
    nx = nr // rpc
    assert nx == nc == 4 and rpc == 2
    ni, nj = rl * nc, rl * nr
    lrows = rl * CH
    t, r, c = axis_places()
    home = lax.div(r, rpc)
    z, x_at, q_at = lax.div(r, nx), lax.rem(r, nx), lax.rem(r, rpc)
    own = jnp.logical_and(x_at == c, home == c)
    half, lhalf = CH // 2, lrows // 2

    h_in = pltpu.make_async_copy(h_ref, h, local_sem.at[0])
    h_in.start()
    g_in = pltpu.make_async_copy(g_ref, g, local_sem.at[1])
    g_in.start()
    greet(nt, nr, nc, t, r, c)

    mult = mult_ref[...]
    off = off_ref[...]
    pt = pm_ref[...]
    bias = jnp.broadcast_to(pb_ref[...], (S, 2 * CH)).T

    wf[...] = w_ref[...].astype(F32)

    def reorder(d, _):
        rows = wf[pl.ds(d, CH, stride=CH), :]
        wp[pl.ds(pl.multiple_of(d * CH, CH), CH), :] = rows.astype(BF16)
        return 0

    lax.fori_loop(0, CH, reorder, 0)
    h_in.wait()

    def normalise(k, _):
        rows = pl.ds(pl.multiple_of(k * 128, 128), 128)
        x = h[rows, :].astype(F32)
        centred = x - jnp.mean(x, -1, keepdims=True)
        scale = lax.rsqrt(jnp.mean(centred * centred, -1, keepdims=True) + 1e-05)
        x = centred * scale
        nrm[0, rows, :] = x[:, :128]
        nrm[1, rows, :] = x[:, 128:]
        inv[rows, :] = jnp.broadcast_to(scale, (128, 128))
        return 0

    lax.fori_loop(0, S * rl // 128, normalise, 0)

    def project(k, _):
        at = pl.ds(k, S, stride=rl)
        x = jnp.concatenate([nrm[0, at, :], nrm[1, at, :]], 1)
        row = (x * mult + off).astype(BF16)
        no[pl.ds(pl.multiple_of(k * S, S), S), :] = row
        y = (mm(pt, row, NT_DIMS) + bias).astype(BF16)
        lt[pl.ds(pl.multiple_of(c * lrows + k * CH, CH), CH), :] = y[:CH]
        rf[pl.ds(pl.multiple_of(k * CH, CH), CH), :] = y[CH:].astype(F32)
        return 0

    lax.fori_loop(0, rl, project, 0)

    def turn(d, _):
        rown[d] = rf[pl.ds(d, rl, stride=CH), :].astype(BF16)
        return 0

    lax.fori_loop(0, CH, turn, 0)
    meet(nt, nr, nc)

    def xs(k):
        return lax.rem(x_at + k, nx)

    def cs(k):
        return lax.rem(c + k, nc)

    def to_x(k):
        return {"row": z * nx + xs(1 if k == 0 else nx - 1)}

    def to_c(k):
        return {"col": cs(1 if k == 0 else nc - 1)}

    back_of = (3, 1)

    def left_block(k, part=None):
        at, size = (k * lrows, lrows) if part is None else (k * lrows + part * lhalf, lhalf)
        return lt.at[pl.ds(pl.multiple_of(at, lhalf), size), :]

    def right_block(k, part=None):
        at = pl.ds(pl.multiple_of(k * rl, rl), rl)
        if part is None:
            return rt.at[:, :, at, :]
        return rt.at[part * half : (part + 1) * half, :, at, :]

    def gather_left(k):
        return left_block(c), left_block(c), gl_send.at[k], gl_recv.at[k], to_c(k)

    def gather_left_in(k):
        at = left_block(cs(back_of[k]))
        return at, at, gl_send.at[k], gl_recv.at[k], to_c(k)

    def relay_left(k):
        at = left_block(cs(back_of[k]), k)
        return at, at, gl2_send.at[k], gl2_recv.at[k], to_c(k)

    def relay_left_in(k):
        at = left_block(cs(2), k)
        return at, at, gl2_send.at[k], gl2_recv.at[k], to_c(k)

    def first_right(k):
        to = rt.at[:, q_at, pl.ds(pl.multiple_of(c * rl, rl), rl), :]
        return rown, to, gr1_send.at[k], gr1_recv.at[q_at], {"row": k * nx + c, "col": home}

    def first_right_in(k):
        to = rt.at[:, k, pl.ds(pl.multiple_of(x_at * rl, rl), rl), :]
        return rown, to, gr1_send.at[k], gr1_recv.at[k], {"row": rpc * c + k, "col": x_at}

    def gather_right(k):
        at = right_block(x_at)
        return at, at, gr_send.at[k], gr_recv.at[k], to_x(k)

    def gather_right_in(k):
        at = right_block(xs(back_of[k]))
        return at, at, gr_send.at[k], gr_recv.at[k], to_x(k)

    def relay_right(k):
        at = right_block(xs(back_of[k]), k)
        return at, at, gr2_send.at[k], gr2_recv.at[k], to_x(k)

    def relay_right_in(k):
        at = right_block(xs(2), k)
        return at, at, gr2_send.at[k], gr2_recv.at[k], to_x(k)

    def unless(same, act):
        pl.when(jnp.logical_not(jnp.logical_and(own, same)))(act)

    for k in range(rpc):
        unless(z == k, lambda: push(*first_right(k)))

    @pl.when(own)
    def _():
        rt[:, q_at, pl.ds(pl.multiple_of(c * rl, rl), rl), :] = rown[...]

    for k in range(2):
        push(*gather_left(k))

    g_in.wait()
    obacc[...] = jnp.zeros_like(obacc)

    def back(k, _):
        rows = g[pl.ds(pl.multiple_of(k * 2 * nj, 2 * nj), 2 * nj), :]
        y = mm(wp[...], rows, NT_DIMS).astype(BF16)
        for q in range(2):
            at = pl.ds(pl.multiple_of((2 * k + q) * CH, CH), CH)
            for d in range(CH):
                pair[at, d * nj : (d + 1) * nj] = y[d * CH : (d + 1) * CH, q * nj : (q + 1) * nj]
        obacc[...] += jnp.sum(rows.astype(F32).reshape(2 * nj // 8, 8, CZ), 0)
        return 0

    lax.fori_loop(0, ni // 4, back, 0)
    for k in range(rpc):
        unless(q_at == k, lambda: arrived(*first_right_in(k)))
    for k in range(2):
        push(*gather_right(k))
    for k in range(2):
        arrived(*gather_left_in(k))
    for k in range(2):
        push(*relay_left(k))
    lax.fori_loop(ni // 4, ni // 2, back, 0)

    for k in range(2):
        arrived(*gather_right_in(k))
    for k in range(2):
        push(*relay_right(k))
    for k in range(2):
        arrived(*relay_left_in(k))

    def flip(k, _):
        at = pl.ds(pl.multiple_of(k * 128, 128), 128)
        lmat[:, at] = lt[at, :].T
        return 0

    lax.fori_loop(0, ni * CH // 128, flip, 0)

    def right_step(k, _):
        lanes = pl.ds(pl.multiple_of(k * 2 * nj, 2 * nj), 2 * nj)
        y = mm(lmat[...], pair[:, lanes]).T
        rp[pl.ds(2 * k, 2)] = y.reshape(2, rpc, nj // rpc, S).astype(BF16)
        return 0

    lax.fori_loop(0, CH // 2, right_step, 0)

    def right_sum(k, part=None):
        at = pl.ds(pl.multiple_of(k * rl, rl), rl)
        if part is None:
            return rp.at[:, :, at, :]
        return rp.at[part * half : (part + 1) * half, :, at, :]

    def far_right(k):
        return right_sum(xs(2), k), ra.at[k], sr1_send.at[k], sr1_recv.at[k], to_x(k)

    def near_right(k):
        at = right_sum(xs(1 if k == 0 else 3))
        return at, rb.at[k], sr2_send.at[k], sr2_recv.at[k], to_x(k)

    def scatter_right(k):
        where = {"row": rpc * c + k, "col": x_at}
        return ms.at[k], rr.at[z], sr3_send.at[k], sr3_recv.at[z], where

    def scatter_right_in(k):
        where = {"row": k * nx + c, "col": home}
        return ms.at[k], rr.at[k], sr3_send.at[k], sr3_recv.at[k], where

    for k in range(2):
        push(*far_right(k))

    for k in range(2):
        arrived(*relay_right_in(k))

    def left_rows(k):
        return pl.ds(pl.multiple_of(k * lrows, lrows), lrows)

    def far_left(k):
        at = lp.at[cs(2), k * lhalf : (k + 1) * lhalf]
        return at, la.at[k], sl1_send.at[k], sl1_recv.at[k], to_c(k)

    def near_left(k):
        at = lp.at[cs(1 if k == 0 else 3)]
        return at, lb.at[k], sl2_send.at[k], sl2_recv.at[k], to_c(k)

    def left_step(k, _):
        right_all = rt[...].reshape(CH * nj, S)
        lp[k] = mm(pair[left_rows(k), :], right_all).astype(BF16)
        return 0

    left_step(cs(2), 0)
    for k in range(2):
        push(*far_left(k))
    left_step(cs(1), 0)
    for k in range(2):
        arrived(*far_right(k))
    for k in range(2):
        at = right_sum(xs(1 if k == 0 else 3), k)
        at[...] = (at[...].astype(F32) + ra[k].astype(F32)).astype(BF16)
        push(*near_right(k))
    left_step(cs(3), 0)
    for k in range(2):
        arrived(*far_left(k))
    for k in range(2):
        at = lp.at[cs(1 if k == 0 else 3), k * lhalf : (k + 1) * lhalf]
        at[...] = (at[...].astype(F32) + la[k].astype(F32)).astype(BF16)
        push(*near_left(k))
    left_step(c, 0)

    dw[...] = jnp.zeros_like(dw)

    def weigh(k, _):
        rows = lt[pl.ds(pl.multiple_of(k * 8 * CH, 8 * CH), 8 * CH), :]
        for v in range(8):
            part = rt[v * 4 : (v + 1) * 4].reshape(4 * nj, S)
            y = mm(rows, part, NT_DIMS).astype(BF16)
            for q in range(8):
                for d in range(4):
                    on[(v * 4 + d) * CH : (v * 4 + d + 1) * CH, q * nj : (q + 1) * nj] = y[
                        q * CH : (q + 1) * CH, d * nj : (d + 1) * nj
                    ]
        dw[...] += mm(on[...], g[pl.ds(pl.multiple_of(k * 8 * nj, 8 * nj), 8 * nj), :])
        return 0

    lax.fori_loop(0, ni // 16, weigh, 0)
    for k in range(2):
        arrived(*near_right(k))
    for k in range(rpc):
        at = pl.ds(pl.multiple_of(x_at * rl, rl), rl)
        total = rp[:, k, at, :].astype(F32)
        total += rb[0, :, k].astype(F32)
        total += rb[1, :, k].astype(F32)
        ms[k] = total.astype(BF16)
    for k in range(rpc):
        unless(q_at == k, lambda: push(*scatter_right(k)))

    @pl.when(own)
    def _():
        rr[z] = ms[q_at]

    lax.fori_loop(ni // 16, ni // 8, weigh, 0)

    ar = CH * CH // nr
    ac = ar // nc

    def a_row(k):
        q = lax.rem(r + k, nr)
        src = dwb.at[pl.ds(pl.multiple_of(q * ar, ar), ar), :]
        return src, a1.at[r], a_row_send.at[k], a_row_recv.at[r], {"row": q}

    def a_row_in(k):
        q = lax.rem(r + k, nr)
        src = dwb.at[pl.ds(0, ar), :]
        return src, a1.at[q], a_row_send.at[k], a_row_recv.at[q], {"row": q}

    dwb[...] = dw[...].astype(BF16)
    for k in range(1, nr):
        push(*a_row(k))
    a1[r] = dwb[pl.ds(pl.multiple_of(r * ar, ar), ar), :]

    for k in range(2):
        arrived(*near_left(k))
    for k in range(rpc):
        unless(z == k, lambda: arrived(*scatter_right_in(k)))

    def sum_left(k, _):
        at = pl.ds(pl.multiple_of(k * 128, 128), 128)
        total = lp[c, at, :].astype(F32)
        for q in range(2):
            total += lb[q, at, :].astype(F32)
        side[at, :] = total * (1.0 / S)
        return 0

    lax.fori_loop(0, lrows // 128, sum_left, 0)

    def sum_right(k, _):
        at = pl.ds(k * 8, 8)
        total = rr[0, at].astype(F32)
        for q in range(1, rpc):
            total += rr[q, at].astype(F32)
        to = pl.ds(pl.multiple_of(lrows + k * 8 * rl, 8 * rl), 8 * rl)
        side[to, :] = total.reshape(8 * rl, S) * (1.0 / S)
        return 0

    lax.fori_loop(0, CH // 8, sum_right, 0)

    for k in range(1, nr):
        arrived(*a_row_in(k))
    total = a1[0].astype(F32)
    for q in range(1, nr):
        total += a1[q].astype(F32)
    s1[...] = total

    def a_col(k):
        q = lax.rem(c + k, nc)
        src = s1.at[pl.ds(pl.multiple_of(q * ac, ac), ac), :]
        return src, a2.at[c], a_col_send.at[k], a_col_recv.at[c], {"col": q}

    def a_col_in(k):
        q = lax.rem(c + k, nc)
        return s1.at[pl.ds(0, ac), :], a2.at[q], a_col_send.at[k], a_col_recv.at[q], {"col": q}

    for k in range(1, nc):
        push(*a_col(k))
    a2[c] = s1[pl.ds(pl.multiple_of(c * ac, ac), ac), :]

    pwt[...] = jnp.zeros_like(pwt)
    acc[...] = jnp.zeros_like(acc)

    def finish(k, _):
        left = side[pl.ds(pl.multiple_of(k * CH, CH), CH), :]
        right = side[pl.ds(lrows + k, CH, stride=rl), :]
        both = jnp.concatenate([left, right], 0)
        rounded = both.astype(BF16)
        turned = both.T
        acc[:, 2 * CM : 2 * CM + 2 * CH] += jnp.sum(turned.reshape(S // 8, 8, 2 * CH), 0)
        grad = mm(turned.astype(BF16), pt)
        pwt[...] += mm(rounded, no[pl.ds(pl.multiple_of(k * S, S), S), :])
        at = pl.ds(k, S, stride=rl)
        x = jnp.concatenate([nrm[0, at, :], nrm[1, at, :]], 1)
        scale = inv[at, :]
        acc[:, :CM] += jnp.sum((grad * x).reshape(S // 8, 8, CM), 0)
        acc[:, CM : 2 * CM] += jnp.sum(grad.reshape(S // 8, 8, CM), 0)
        scaled = grad * mult
        dx = scaled - jnp.mean(scaled, -1, keepdims=True) - x * jnp.mean(scaled * x, -1, keepdims=True)
        nrm[0, at, :] = dx[:, :128] * scale
        nrm[1, at, :] = dx[:, 128:] * scale
        return 0

    lax.fori_loop(0, rl, finish, 0)

    pr = 2 * 2 * CH // nr
    vr = 8 // nr
    vec[...] = jnp.zeros_like(vec)
    small = jnp.sum(acc[...], 0, keepdims=True)
    vec[0:1, : 2 * CH] = small[:, 2 * CM : 2 * CM + 2 * CH]
    for k in range(4):
        vec[1 + k : 2 + k, :] = small[:, k * 128 : (k + 1) * 128]
    vec[5:6, :] = jnp.sum(obacc[...], 0, keepdims=True)
    weights = pwt[...]
    stacked = jnp.concatenate([weights[:, :128], weights[:, 128:]], 0)
    sb[...] = jnp.zeros_like(sb)
    for q in range(nr):
        sb[q, :pr, :] = stacked[q * pr : (q + 1) * pr]
        sb[q, pr : pr + vr, :] = vec[q * vr : (q + 1) * vr, :]

    def b_row(k):
        q = lax.rem(r + k, nr)
        return sb.at[q], b1.at[r], b_row_send.at[k], b_row_recv.at[r], {"row": q}

    def b_row_in(k):
        q = lax.rem(r + k, nr)
        return sb.at[q], b1.at[q], b_row_send.at[k], b_row_recv.at[q], {"row": q}

    for k in range(1, nr):
        push(*b_row(k))
    b1[r] = sb[r]

    for k in range(1, nc):
        arrived(*a_col_in(k))
    total = a2[0]
    for q in range(1, nc):
        total += a2[q]
    a3[t] = total

    def a_tgt(k):
        q = lax.rem(t + k, nt)
        return a3.at[t], a3.at[t], a_tgt_send.at[k], a_tgt_recv.at[t], {"tgt": q}

    def a_tgt_in(k):
        q = lax.rem(t + k, nt)
        return a3.at[q], a3.at[q], a_tgt_send.at[k], a_tgt_recv.at[q], {"tgt": q}

    for k in range(1, nt):
        push(*a_tgt(k))

    def emit(k, _):
        rows = pl.ds(pl.multiple_of(k * 128, 128), 128)
        h[rows, :128] = nrm[0, rows, :].astype(BF16)
        h[rows, 128:] = nrm[1, rows, :].astype(BF16)
        return 0

    lax.fori_loop(0, S * rl // 128, emit, 0)
    dx_copy = pltpu.make_async_copy(h, dx_out, local_sem.at[2])
    dx_copy.start()

    for k in range(1, nr):
        arrived(*b_row_in(k))
    total = b1[0]
    for q in range(1, nr):
        total += b1[q]
    b2[c] = total

    def b_col(k):
        q = lax.rem(c + k, nc)
        return b2.at[c], b2.at[c], b_col_send.at[k], b_col_recv.at[c], {"col": q}

    def b_col_in(k):
        q = lax.rem(c + k, nc)
        return b2.at[q], b2.at[q], b_col_send.at[k], b_col_recv.at[q], {"col": q}

    for k in range(1, nc):
        push(*b_col(k))

    for k in range(1, nt):
        arrived(*a_tgt_in(k))
    total = a3[0]
    for q in range(1, nt):
        total += a3[q]
    a4[c] = total.astype(BF16)

    def a_col2(k):
        q = lax.rem(c + k, nc)
        return a4.at[c], a4.at[c], a_col2_send.at[k], a_col2_recv.at[c], {"col": q}

    def a_col2_in(k):
        q = lax.rem(c + k, nc)
        return a4.at[q], a4.at[q], a_col2_send.at[k], a_col2_recv.at[q], {"col": q}

    for k in range(1, nc):
        push(*a_col2(k))

    for k in range(1, nc):
        arrived(*b_col_in(k))
    total = b2[0]
    for q in range(1, nc):
        total += b2[q]
    b3[t] = total

    def b_tgt(k):
        q = lax.rem(t + k, nt)
        return b3.at[t], b3.at[t], b_tgt_send.at[k], b_tgt_recv.at[t], {"tgt": q}

    def b_tgt_in(k):
        q = lax.rem(t + k, nt)
        return b3.at[q], b3.at[q], b_tgt_send.at[k], b_tgt_recv.at[q], {"tgt": q}

    for k in range(1, nt):
        push(*b_tgt(k))

    for k in range(1, nc):
        arrived(*a_col2_in(k))
    a5[r] = a4[...].reshape(ar, CZ)

    def a_row2(k):
        q = lax.rem(r + k, nr)
        return a5.at[r], a5.at[r], a_row2_send.at[k], a_row2_recv.at[r], {"row": q}

    def a_row2_in(k):
        q = lax.rem(r + k, nr)
        return a5.at[q], a5.at[q], a_row2_send.at[k], a_row2_recv.at[q], {"row": q}

    for k in range(1, nr):
        push(*a_row2(k))

    for k in range(1, nt):
        arrived(*b_tgt_in(k))
    total = b3[0]
    for q in range(1, nt):
        total += b3[q]
    b4[r] = total

    def b_row2(k):
        q = lax.rem(r + k, nr)
        return b4.at[r], b4.at[r], b_row2_send.at[k], b_row2_recv.at[r], {"row": q}

    def b_row2_in(k):
        q = lax.rem(r + k, nr)
        return b4.at[q], b4.at[q], b_row2_send.at[k], b_row2_recv.at[q], {"row": q}

    for k in range(1, nr):
        push(*b_row2(k))

    factor = 1.0 / (nt * nr * nc * rl)
    for k in range(1, nr):
        arrived(*a_row2_in(k))

    def place(d, _):
        at = pl.multiple_of(d * CH, CH)
        rows = a5[lax.div(at, ar), pl.ds(pl.multiple_of(lax.rem(at, ar), CH), CH), :]
        ow_out[pl.ds(d, CH, stride=CH), :] = rows.astype(F32) * (factor / S)
        return 0

    lax.fori_loop(0, CH, place, 0)

    for k in range(1, nr):
        arrived(*b_row2_in(k))
    whole = b4[:, :pr, :].reshape(4 * CH, 128) * factor
    pw_out[:, :128] = whole[: 2 * CH]
    pw_out[:, 128:] = whole[2 * CH :]
    for q in range(nr):
        vec[q * vr : (q + 1) * vr, :] = b4[q, pr : pr + vr, :] * factor
    pbias_out[...] = vec[0:1, : 2 * CH]
    gain_out[...] = jnp.concatenate([vec[1:2, :], vec[2:3, :]], 1)
    shift_out[...] = jnp.concatenate([vec[3:4, :], vec[4:5, :]], 1)
    ob_out[...] = vec[5:6, :]

    dx_copy.wait()
    for k in range(2):
        sent(*gather_left(k))
        sent(*relay_left(k))
        sent(*gather_right(k))
        sent(*relay_right(k))
        sent(*far_right(k))
        sent(*near_right(k))
        sent(*far_left(k))
        sent(*near_left(k))
    for k in range(rpc):
        unless(z == k, lambda: sent(*first_right(k)))
        unless(q_at == k, lambda: sent(*scatter_right(k)))
    for k in range(1, nc):
        sent(*a_col(k))
        sent(*a_col2(k))
        sent(*b_col(k))
    for k in range(1, nr):
        sent(*a_row(k))
        sent(*a_row2(k))
        sent(*b_row(k))
        sent(*b_row2(k))
    for k in range(1, nt):
        sent(*a_tgt(k))
        sent(*b_tgt(k))


def per_device(
    homolog_activation_matrix,
    standardizer_multiplier,
    standardizer_offset,
    side_mapping_matrices,
    side_mapping_offsets,
    final_channel_matrix,
    residue_couple_cotangent,
):
    nt, nr, nc = axis_sizes()
    rl = homolog_activation_matrix.shape[2]
    ni, nj = rl * nc, rl * nr
    ar = CH * CH // nr
    pr = 4 * CH // nr + 8
    vmem = functools.partial(pl.BlockSpec, memory_space=pltpu.VMEM)
    hbm = functools.partial(pl.BlockSpec, memory_space=pl.ANY)

    def sems(n):
        return [pltpu.SemaphoreType.DMA((n,)), pltpu.SemaphoreType.DMA((n,))]

    results = pl.pallas_call(
        functools.partial(kernel, (nt, nr, nc, rl)),
        out_shape=(
            jax.ShapeDtypeStruct((S * rl, CM), BF16),
            jax.ShapeDtypeStruct((2 * CH, CM), F32),
            jax.ShapeDtypeStruct((1, 2 * CH), F32),
            jax.ShapeDtypeStruct((1, CM), F32),
            jax.ShapeDtypeStruct((1, CM), F32),
            jax.ShapeDtypeStruct((CH * CH, CZ), F32),
            jax.ShapeDtypeStruct((1, CZ), F32),
        ),
        in_specs=[hbm(), vmem(), vmem(), vmem(), vmem(), vmem(), hbm()],
        out_specs=(hbm(), vmem(), vmem(), vmem(), vmem(), vmem(), vmem()),
        scratch_shapes=[
            pltpu.VMEM((S * rl, CM), BF16),
            pltpu.VMEM((ni * nj, CZ), BF16),
            pltpu.VMEM((2, S * rl, 128), F32),
            pltpu.VMEM((S * rl, 128), F32),
            pltpu.VMEM((S * rl, CM), BF16),
            pltpu.VMEM((ni * CH, S), BF16),
            pltpu.VMEM((S, ni * CH), BF16),
            pltpu.VMEM((CH, 2, nj // 2, S), BF16),
            pltpu.VMEM((CH, rl, S), BF16),
            pltpu.VMEM((rl * CH, S), F32),
            pltpu.VMEM((CH * CH, CZ), F32),
            pltpu.VMEM((CH * CH, CZ), BF16),
            pltpu.VMEM((ni * CH, CH * nj), BF16),
            pltpu.VMEM((CH, 2, nj // 2, S), BF16),
            pltpu.VMEM((nc, rl * CH, S), BF16),
            pltpu.VMEM((2, CH // 2, 2, rl, S), BF16),
            pltpu.VMEM((2, CH, 2, rl, S), BF16),
            pltpu.VMEM((2, CH, rl, S), BF16),
            pltpu.VMEM((2, CH, rl, S), BF16),
            pltpu.VMEM((2, rl * CH // 2, S), BF16),
            pltpu.VMEM((2, rl * CH, S), BF16),
            pltpu.VMEM((2 * rl * CH, S), F32),
            pltpu.VMEM((CH * CH, 8 * nj), BF16),
            pltpu.VMEM((CH * CH, CZ), F32),
            pltpu.VMEM((CH * CH, CZ), BF16),
            pltpu.VMEM((8, CZ), F32),
            pltpu.VMEM((nr, ar, CZ), BF16),
            pltpu.VMEM((ar, CZ), F32),
            pltpu.VMEM((nc, ar // nc, CZ), F32),
            pltpu.VMEM((nt, ar // nc, CZ), F32),
            pltpu.VMEM((nc, ar // nc, CZ), BF16),
            pltpu.VMEM((nr, ar, CZ), BF16),
            pltpu.VMEM((2 * CH, CM), F32),
            pltpu.VMEM((8, 128), F32),
            pltpu.VMEM((8, 2 * CM + 128), F32),
            pltpu.VMEM((nr, pr, 128), F32),
            pltpu.VMEM((nr, pr, 128), F32),
            pltpu.VMEM((nc, pr, 128), F32),
            pltpu.VMEM((nt, pr, 128), F32),
            pltpu.VMEM((nr, pr, 128), F32),
            pltpu.SemaphoreType.DMA((3,)),
        ]
        + 10 * sems(2)
        + sems(nr)
        + sems(nc)
        + sems(nt)
        + sems(nc)
        + sems(nr)
        + sems(nr)
        + sems(nc)
        + sems(nt)
        + sems(nr),
        compiler_params=pltpu.CompilerParams(
            collective_id=0, has_side_effects=True, vmem_limit_bytes=56 * 1024 * 1024
        ),
        cost_estimate=pl.CostEstimate(
            flops=10 * ni * nj * CH * CH * CZ, bytes_accessed=5 * 1024 * 1024, transcendentals=0
        ),
    )(
        homolog_activation_matrix.reshape(S * rl, CM),
        standardizer_multiplier.reshape(1, CM),
        standardizer_offset.reshape(1, CM),
        side_mapping_matrices.T,
        side_mapping_offsets.reshape(1, 2 * CH),
        final_channel_matrix,
        residue_couple_cotangent.reshape(ni * nj, CZ),
    )
    return (
        results[0].reshape(1, S, rl, CM),
        results[1].T,
        results[2].reshape(2 * CH),
        results[3].reshape(CM),
        results[4].reshape(CM),
        results[5],
        results[6].reshape(CZ),
    )


def solution(mesh):
    placed = (
        P("tgt", None, ("row", "col"), None),
        P(),
        P(),
        P(),
        P(),
        P(),
        P("tgt", "row", "col", None),
    )
    return jax.shard_map(
        per_device,
        mesh=mesh,
        in_specs=placed,
        out_specs=(P("tgt", None, ("row", "col"), None), P(), P(), P(), P(), P(), P()),
        check_vma=False,
    )
```

```python
import functools

import jax
import jax.numpy as jnp
from jax import lax
from jax.experimental import pallas as pl
from jax.experimental.pallas import tpu as pltpu
from jax.sharding import PartitionSpec as P

CM = 256
CH = 32
CZ = 128
S = 128
F32 = jnp.float32
BF16 = jnp.bfloat16
NT_DIMS = (((1,), (1,)), ((), ()))
NN_DIMS = (((1,), (0,)), ((), ()))


def mm(a, b, dims=NN_DIMS):
    return lax.dot_general(a, b, dims, preferred_element_type=F32)


def axis_sizes():
    return lax.axis_size("tgt"), lax.axis_size("row"), lax.axis_size("col")


def axis_places():
    return lax.axis_index("tgt"), lax.axis_index("row"), lax.axis_index("col")


def descriptor(src, dst, send, recv, where):
    return pltpu.make_async_remote_copy(
        src_ref=src,
        dst_ref=dst,
        send_sem=send,
        recv_sem=recv,
        device_id=where,
        device_id_type=pl.DeviceIdType.MESH,
    )


def push(*args):
    descriptor(*args).start()


def sent(*args):
    descriptor(*args).wait_send()


def arrived(*args):
    descriptor(*args).wait_recv()


def greet(nt, nr, nc, t, r, c):
    barrier = pltpu.get_barrier_semaphore()
    flat = r * nc + c
    for k in range(1, nr * nc):
        other = lax.rem(flat + k, nr * nc)
        pl.semaphore_signal(
            barrier,
            inc=1,
            device_id={"row": other // nc, "col": lax.rem(other, nc)},
            device_id_type=pl.DeviceIdType.MESH,
        )
    for k in range(1, nt):
        pl.semaphore_signal(
            barrier,
            inc=1,
            device_id={"tgt": lax.rem(t + k, nt)},
            device_id_type=pl.DeviceIdType.MESH,
        )


def meet(nt, nr, nc):
    pl.semaphore_wait(pltpu.get_barrier_semaphore(), nr * nc - 1 + nt - 1)


def kernel(
    sizes,
    h_ref,
    mult_ref,
    off_ref,
    pm_ref,
    pb_ref,
    w_ref,
    g_ref,
    dx_out,
    pw_out,
    pbias_out,
    gain_out,
    shift_out,
    ow_out,
    ob_out,
    h,
    g,
    nrm,
    inv,
    no,
    lt,
    lmat,
    rt,
    rown,
    rf,
    wf,
    wp,
    pair,
    rp,
    lp,
    ra,
    rb,
    ms,
    rr,
    la,
    lb,
    side,
    on,
    dw,
    dwb,
    obacc,
    a1,
    a3,
    a5,
    grads,
    pwt,
    vec,
    acc,
    sb,
    b1,
    b2,
    b3,
    b4,
    local_sem,
    gl_send,
    gl_recv,
    gl2_send,
    gl2_recv,
    gr1_send,
    gr1_recv,
    gr_send,
    gr_recv,
    gr2_send,
    gr2_recv,
    sr1_send,
    sr1_recv,
    sr2_send,
    sr2_recv,
    sr3_send,
    sr3_recv,
    sl1_send,
    sl1_recv,
    sl2_send,
    sl2_recv,
    a_part_send,
    a_part_recv,
    a_tgt_send,
    a_tgt_recv,
    a_whole_send,
    a_whole_recv,
    b_row_send,
    b_row_recv,
    b_col_send,
    b_col_recv,
    b_tgt_send,
    b_tgt_recv,
    b_row2_send,
    b_row2_recv,
):
    nt, nr, nc, rl = sizes
    rpc = nr // nc
    nx = nr // rpc
    assert nx == nc == 4 and rpc == 2
    ni, nj = rl * nc, rl * nr
    lrows = rl * CH
    t, r, c = axis_places()
    home = lax.div(r, rpc)
    z, x_at, q_at = lax.div(r, nx), lax.rem(r, nx), lax.rem(r, rpc)
    own = jnp.logical_and(x_at == c, home == c)
    half, lhalf = CH // 2, lrows // 2

    h_in = pltpu.make_async_copy(h_ref, h, local_sem.at[0])
    h_in.start()
    g_in = pltpu.make_async_copy(g_ref, g, local_sem.at[1])
    g_in.start()
    greet(nt, nr, nc, t, r, c)

    mult = mult_ref[...]
    off = off_ref[...]
    pt = pm_ref[...]
    bias = jnp.broadcast_to(pb_ref[...], (S, 2 * CH)).T

    wf[...] = w_ref[...].astype(F32)

    def reorder(d, _):
        rows = wf[pl.ds(d, CH, stride=CH), :]
        wp[pl.ds(pl.multiple_of(d * CH, CH), CH), :] = rows.astype(BF16)
        return 0

    lax.fori_loop(0, CH, reorder, 0)
    h_in.wait()

    def normalise(k, _):
        rows = pl.ds(pl.multiple_of(k * 128, 128), 128)
        x = h[rows, :].astype(F32)
        centred = x - jnp.mean(x, -1, keepdims=True)
        scale = lax.rsqrt(jnp.mean(centred * centred, -1, keepdims=True) + 1e-05)
        x = centred * scale
        nrm[0, rows, :] = x[:, :128]
        nrm[1, rows, :] = x[:, 128:]
        inv[rows, :] = jnp.broadcast_to(scale, (128, 128))
        return 0

    lax.fori_loop(0, S * rl // 128, normalise, 0)

    def project(k, _):
        at = pl.ds(k, S, stride=rl)
        x = jnp.concatenate([nrm[0, at, :], nrm[1, at, :]], 1)
        row = (x * mult + off).astype(BF16)
        no[pl.ds(pl.multiple_of(k * S, S), S), :] = row
        y = (mm(pt, row, NT_DIMS) + bias).astype(BF16)
        lt[pl.ds(pl.multiple_of(c * lrows + k * CH, CH), CH), :] = y[:CH]
        rf[pl.ds(pl.multiple_of(k * CH, CH), CH), :] = y[CH:].astype(F32)
        return 0

    lax.fori_loop(0, rl, project, 0)

    def turn(d, _):
        rown[d] = rf[pl.ds(d, rl, stride=CH), :].astype(BF16)
        return 0

    lax.fori_loop(0, CH, turn, 0)
    meet(nt, nr, nc)

    def xs(k):
        return lax.rem(x_at + k, nx)

    def cs(k):
        return lax.rem(c + k, nc)

    def to_x(k):
        return {"row": z * nx + xs(1 if k == 0 else nx - 1)}

    def to_c(k):
        return {"col": cs(1 if k == 0 else nc - 1)}

    back_of = (3, 1)

    def left_block(k, part=None):
        at, size = (k * lrows, lrows) if part is None else (k * lrows + part * lhalf, lhalf)
        return lt.at[pl.ds(pl.multiple_of(at, lhalf), size), :]

    def right_block(k, part=None):
        at = pl.ds(pl.multiple_of(k * rl, rl), rl)
        if part is None:
            return rt.at[:, :, at, :]
        return rt.at[part * half : (part + 1) * half, :, at, :]

    def gather_left(k):
        return left_block(c), left_block(c), gl_send.at[k], gl_recv.at[k], to_c(k)

    def gather_left_in(k):
        at = left_block(cs(back_of[k]))
        return at, at, gl_send.at[k], gl_recv.at[k], to_c(k)

    def relay_left(k):
        at = left_block(cs(back_of[k]), k)
        return at, at, gl2_send.at[k], gl2_recv.at[k], to_c(k)

    def relay_left_in(k):
        at = left_block(cs(2), k)
        return at, at, gl2_send.at[k], gl2_recv.at[k], to_c(k)

    def first_right(k, part):
        at = pl.ds(pl.multiple_of(c * rl, rl), rl)
        rows = slice(part * half, (part + 1) * half)
        to = rt.at[rows, q_at, at, :]
        where = {"row": k * nx + c, "col": home}
        return rown.at[rows], to, gr1_send.at[k, part], gr1_recv.at[q_at, part], where

    def first_right_in(k, part):
        at = pl.ds(pl.multiple_of(x_at * rl, rl), rl)
        rows = slice(part * half, (part + 1) * half)
        to = rt.at[rows, k, at, :]
        where = {"row": rpc * c + k, "col": x_at}
        return rown.at[rows], to, gr1_send.at[k, part], gr1_recv.at[k, part], where

    def gather_right(k, part):
        at = right_block(x_at, part)
        return at, at, gr_send.at[k, part], gr_recv.at[k, part], to_x(k)

    def gather_right_in(k, part):
        at = right_block(xs(back_of[k]), part)
        return at, at, gr_send.at[k, part], gr_recv.at[k, part], to_x(k)

    def relay_right(k):
        at = right_block(xs(back_of[k]), k)
        return at, at, gr2_send.at[k], gr2_recv.at[k], to_x(k)

    def relay_right_in(k):
        at = right_block(xs(2), k)
        return at, at, gr2_send.at[k], gr2_recv.at[k], to_x(k)

    def unless(same, act):
        pl.when(jnp.logical_not(jnp.logical_and(own, same)))(act)

    for part in range(2):
        for k in range(rpc):
            unless(z == k, lambda: push(*first_right(k, part)))

    @pl.when(own)
    def _():
        rt[:, q_at, pl.ds(pl.multiple_of(c * rl, rl), rl), :] = rown[...]

    for k in range(2):
        push(*gather_left(k))

    g_in.wait()
    obacc[...] = jnp.zeros_like(obacc)

    def back(k, _):
        rows = g[pl.ds(pl.multiple_of(k * 2 * nj, 2 * nj), 2 * nj), :]
        y = mm(wp[...], rows, NT_DIMS).astype(BF16)
        for q in range(2):
            at = pl.ds(pl.multiple_of((2 * k + q) * CH, CH), CH)
            for d in range(CH):
                pair[at, d * nj : (d + 1) * nj] = y[d * CH : (d + 1) * CH, q * nj : (q + 1) * nj]
        obacc[...] += jnp.sum(rows.astype(F32).reshape(2 * nj // 8, 8, CZ), 0)
        return 0

    lax.fori_loop(0, 6 * ni // 32, back, 0, unroll=2)
    for k in range(2):
        arrived(*gather_left_in(k))
        push(*relay_left(k))
    lax.fori_loop(6 * ni // 32, 9 * ni // 32, back, 0, unroll=2)
    for k in range(rpc):
        unless(q_at == k, lambda: arrived(*first_right_in(k, 0)))
    for k in range(2):
        push(*gather_right(k, 0))
    lax.fori_loop(9 * ni // 32, 11 * ni // 32, back, 0, unroll=2)
    for k in range(rpc):
        unless(q_at == k, lambda: arrived(*first_right_in(k, 1)))
    for k in range(2):
        push(*gather_right(1 - k, 1))
    lax.fori_loop(11 * ni // 32, ni // 2, back, 0, unroll=2)
    arrived(*gather_right_in(0, 0))
    push(*relay_right(0))

    for k in range(2):
        arrived(*relay_left_in(k))
    def flip(k, _):
        at = pl.ds(pl.multiple_of(k * 128, 128), 128)
        lmat[:, at] = lt[at, :].T
        return 0

    lax.fori_loop(0, ni * CH // 128, flip, 0)

    def right_step(k, _):
        lanes = pl.ds(pl.multiple_of(k * 8 * nj, 8 * nj), 8 * nj)
        y = mm(lmat[...], pair[:, lanes]).T
        rp[pl.ds(8 * k, 8)] = y.reshape(8, rpc, nj // rpc, S).astype(BF16)
        return 0

    def right_sum(k, part=None):
        at = pl.ds(pl.multiple_of(k * rl, rl), rl)
        if part is None:
            return rp.at[:, :, at, :]
        return rp.at[part * half : (part + 1) * half, :, at, :]

    def far_right(k):
        return right_sum(xs(2), k), ra.at[k], sr1_send.at[k], sr1_recv.at[k], to_x(k)

    def near_right(k, part):
        at = right_sum(xs(1 if k == 0 else 3), part)
        to = rb.at[k, part * half : (part + 1) * half]
        return at, to, sr2_send.at[k, part], sr2_recv.at[k, part], to_x(k)

    def scatter_right(k):
        where = {"row": rpc * c + k, "col": x_at}
        return ms.at[k], rr.at[z], sr3_send.at[k], sr3_recv.at[z], where

    def scatter_right_in(k):
        where = {"row": k * nx + c, "col": home}
        return ms.at[k], rr.at[k], sr3_send.at[k], sr3_recv.at[k], where

    lax.fori_loop(0, CH // 16, right_step, 0)
    push(*far_right(0))
    push(*near_right(1, 0))
    arrived(*gather_right_in(1, 1))
    push(*relay_right(1))
    lax.fori_loop(CH // 16, CH // 8, right_step, 0)
    push(*far_right(1))
    push(*near_right(0, 1))

    for k in range(2):
        arrived(*gather_right_in(k, 1 - k))
    for k in range(2):
        arrived(*relay_right_in(k))

    def left_rows(k):
        return pl.ds(pl.multiple_of(k * lrows, lrows), lrows)

    def far_left(k):
        at = lp.at[cs(2), k * lhalf : (k + 1) * lhalf]
        return at, la.at[k], sl1_send.at[k], sl1_recv.at[k], to_c(k)

    def near_left(k):
        at = lp.at[cs(1 if k == 0 else 3)]
        return at, lb.at[k], sl2_send.at[k], sl2_recv.at[k], to_c(k)

    def left_step(k, _):
        right_all = rt[...].reshape(CH * nj, S)
        lp[k] = mm(pair[left_rows(k), :], right_all).astype(BF16)
        return 0

    left_step(cs(2), 0)
    for k in range(2):
        push(*far_left(k))
    left_step(cs(1), 0)
    for k in range(2):
        arrived(*far_right(k))
        at = right_sum(xs(1 if k == 0 else 3), k)
        at[...] = (at[...].astype(F32) + ra[k].astype(F32)).astype(BF16)
        push(*near_right(k, k))
    left_step(cs(3), 0)
    for k in range(2):
        arrived(*far_left(k))
    for k in range(2):
        at = lp.at[cs(1 if k == 0 else 3), k * lhalf : (k + 1) * lhalf]
        at[...] = (at[...].astype(F32) + la[k].astype(F32)).astype(BF16)
        push(*near_left(k))
    left_step(c, 0)

    dw[...] = jnp.zeros_like(dw)

    def weigh(k, _):
        rows = lt[pl.ds(pl.multiple_of(k * 8 * CH, 8 * CH), 8 * CH), :]
        for v in range(8):
            part = rt[v * 4 : (v + 1) * 4].reshape(4 * nj, S)
            y = mm(rows, part, NT_DIMS).astype(BF16)
            for q in range(8):
                for d in range(4):
                    on[(v * 4 + d) * CH : (v * 4 + d + 1) * CH, q * nj : (q + 1) * nj] = y[
                        q * CH : (q + 1) * CH, d * nj : (d + 1) * nj
                    ]
        dw[...] += mm(on[...], g[pl.ds(pl.multiple_of(k * 8 * nj, 8 * nj), 8 * nj), :])
        return 0

    lax.fori_loop(0, ni // 32, weigh, 0)
    for k in range(2):
        for part in range(2):
            arrived(*near_right(k, part))
    for k in range(rpc):
        at = pl.ds(pl.multiple_of(x_at * rl, rl), rl)
        total = rp[:, k, at, :].astype(F32)
        total += rb[0, :, k].astype(F32)
        total += rb[1, :, k].astype(F32)
        ms[k] = total.astype(BF16)
    for k in range(rpc):
        unless(q_at == k, lambda: push(*scatter_right(k)))

    @pl.when(own)
    def _():
        rr[z] = ms[q_at]

    lax.fori_loop(ni // 32, ni // 8, weigh, 0)

    group = nr * nc
    flat = r * nc + c

    def member(k):
        f = lax.rem(flat + k, group)
        return f, {"row": lax.div(f, nc), "col": lax.rem(f, nc)}

    def a_part(k):
        f, where = member(k)
        src = dwb.at[pl.ds(pl.multiple_of(f * CH, CH), CH), :]
        return src, a1.at[flat], a_part_send.at[k], a_part_recv.at[flat], where

    def a_part_in(k):
        f, where = member(k)
        src = dwb.at[pl.ds(pl.multiple_of(flat * CH, CH), CH), :]
        return src, a1.at[f], a_part_send.at[k], a_part_recv.at[f], where

    def a_whole(k):
        _, where = member(k)
        return a5.at[flat], a5.at[flat], a_whole_send.at[k], a_whole_recv.at[flat], where

    def a_whole_in(k):
        f, where = member(k)
        return a5.at[f], a5.at[f], a_whole_send.at[k], a_whole_recv.at[f], where

    def every(act, copy):
        def step(k, _):
            act(*copy(k))
            return 0

        lax.fori_loop(1, group, step, 0)

    dwb[...] = dw[...].astype(BF16)
    every(push, a_part)
    a1[flat] = dwb[pl.ds(pl.multiple_of(flat * CH, CH), CH), :]

    for k in range(2):
        arrived(*near_left(k))
    for k in range(rpc):
        unless(z == k, lambda: arrived(*scatter_right_in(k)))

    def sum_left(k, _):
        at = pl.ds(pl.multiple_of(k * 128, 128), 128)
        total = lp[c, at, :].astype(F32)
        for q in range(2):
            total += lb[q, at, :].astype(F32)
        side[at, :] = total * (1.0 / S)
        return 0

    lax.fori_loop(0, lrows // 128, sum_left, 0)

    def sum_right(k, _):
        at = pl.ds(k * 8, 8)
        total = rr[0, at].astype(F32)
        for q in range(1, rpc):
            total += rr[q, at].astype(F32)
        to = pl.ds(pl.multiple_of(lrows + k * 8 * rl, 8 * rl), 8 * rl)
        side[to, :] = total.reshape(8 * rl, S) * (1.0 / S)
        return 0

    lax.fori_loop(0, CH // 8, sum_right, 0)

    pwt[...] = jnp.zeros_like(pwt)
    acc[...] = jnp.zeros_like(acc)

    def finish(k, _):
        left = side[pl.ds(pl.multiple_of(k * CH, CH), CH), :]
        right = side[pl.ds(lrows + k, CH, stride=rl), :]
        both = jnp.concatenate([left, right], 0)
        rounded = both.astype(BF16)
        turned = both.T
        acc[:, 2 * CM : 2 * CM + 2 * CH] += jnp.sum(turned.reshape(S // 8, 8, 2 * CH), 0)
        grad = mm(turned.astype(BF16), pt)
        grads[pl.ds(pl.multiple_of(k * S, S), S), :] = grad
        pwt[...] += mm(rounded, no[pl.ds(pl.multiple_of(k * S, S), S), :])
        at = pl.ds(k, S, stride=rl)
        x = jnp.concatenate([nrm[0, at, :], nrm[1, at, :]], 1)
        acc[:, :CM] += jnp.sum((grad * x).reshape(S // 8, 8, CM), 0)
        acc[:, CM : 2 * CM] += jnp.sum(grad.reshape(S // 8, 8, CM), 0)
        return 0

    lax.fori_loop(0, rl, finish, 0)

    pr = 2 * 2 * CH // nr
    vr = 8 // nr
    vec[...] = jnp.zeros_like(vec)
    small = jnp.sum(acc[...], 0, keepdims=True)
    vec[0:1, : 2 * CH] = small[:, 2 * CM : 2 * CM + 2 * CH]
    for k in range(4):
        vec[1 + k : 2 + k, :] = small[:, k * 128 : (k + 1) * 128]
    vec[5:6, :] = jnp.sum(obacc[...], 0, keepdims=True)
    weights = pwt[...]
    stacked = jnp.concatenate([weights[:, :128], weights[:, 128:]], 0)
    sb[...] = jnp.zeros_like(sb)
    for q in range(nr):
        sb[q, :pr, :] = stacked[q * pr : (q + 1) * pr]
        sb[q, pr : pr + vr, :] = vec[q * vr : (q + 1) * vr, :]

    def b_row(k):
        q = lax.rem(r + k, nr)
        return sb.at[q], b1.at[r], b_row_send.at[k], b_row_recv.at[r], {"row": q}

    def b_row_in(k):
        q = lax.rem(r + k, nr)
        return sb.at[q], b1.at[q], b_row_send.at[k], b_row_recv.at[q], {"row": q}

    for k in range(1, nr):
        push(*b_row(k))
    b1[r] = sb[r]

    every(arrived, a_part_in)
    total = a1[0].astype(F32)
    for q in range(1, group):
        total += a1[q].astype(F32)
    a3[t] = total

    def a_tgt(k):
        q = lax.rem(t + k, nt)
        return a3.at[t], a3.at[t], a_tgt_send.at[k], a_tgt_recv.at[t], {"tgt": q}

    def a_tgt_in(k):
        q = lax.rem(t + k, nt)
        return a3.at[q], a3.at[q], a_tgt_send.at[k], a_tgt_recv.at[q], {"tgt": q}

    for k in range(1, nt):
        push(*a_tgt(k))

    def descend(k, _):
        grad = grads[pl.ds(pl.multiple_of(k * S, S), S), :]
        at = pl.ds(k, S, stride=rl)
        x = jnp.concatenate([nrm[0, at, :], nrm[1, at, :]], 1)
        scale = inv[at, :]
        scaled = grad * mult
        dx = scaled - jnp.mean(scaled, -1, keepdims=True) - x * jnp.mean(scaled * x, -1, keepdims=True)
        nrm[0, at, :] = dx[:, :128] * scale
        nrm[1, at, :] = dx[:, 128:] * scale
        return 0

    lax.fori_loop(0, rl // 2, descend, 0)

    for k in range(1, nr):
        arrived(*b_row_in(k))
    total = b1[0]
    for q in range(1, nr):
        total += b1[q]
    b2[c] = total

    def b_col(k):
        q = lax.rem(c + k, nc)
        return b2.at[c], b2.at[c], b_col_send.at[k], b_col_recv.at[c], {"col": q}

    def b_col_in(k):
        q = lax.rem(c + k, nc)
        return b2.at[q], b2.at[q], b_col_send.at[k], b_col_recv.at[q], {"col": q}

    for k in range(1, nc):
        push(*b_col(k))

    lax.fori_loop(rl // 2, rl, descend, 0)

    def emit(k, _):
        rows = pl.ds(pl.multiple_of(k * 128, 128), 128)
        h[rows, :128] = nrm[0, rows, :].astype(BF16)
        h[rows, 128:] = nrm[1, rows, :].astype(BF16)
        return 0

    lax.fori_loop(0, S * rl // 128, emit, 0)
    dx_copy = pltpu.make_async_copy(h, dx_out, local_sem.at[2])
    dx_copy.start()

    for k in range(1, nc):
        arrived(*b_col_in(k))
    total = b2[0]
    for q in range(1, nc):
        total += b2[q]
    b3[t] = total

    def b_tgt(k):
        q = lax.rem(t + k, nt)
        return b3.at[t], b3.at[t], b_tgt_send.at[k], b_tgt_recv.at[t], {"tgt": q}

    def b_tgt_in(k):
        q = lax.rem(t + k, nt)
        return b3.at[q], b3.at[q], b_tgt_send.at[k], b_tgt_recv.at[q], {"tgt": q}

    for k in range(1, nt):
        push(*b_tgt(k))

    for k in range(1, nt):
        arrived(*a_tgt_in(k))
    total = a3[0]
    for q in range(1, nt):
        total += a3[q]
    a5[flat] = total.astype(BF16)
    every(push, a_whole)

    for k in range(1, nt):
        arrived(*b_tgt_in(k))
    total = b3[0]
    for q in range(1, nt):
        total += b3[q]
    b4[r] = total

    def b_row2(k):
        q = lax.rem(r + k, nr)
        return b4.at[r], b4.at[r], b_row2_send.at[k], b_row2_recv.at[r], {"row": q}

    def b_row2_in(k):
        q = lax.rem(r + k, nr)
        return b4.at[q], b4.at[q], b_row2_send.at[k], b_row2_recv.at[q], {"row": q}

    for k in range(1, nr):
        push(*b_row2(k))

    factor = 1.0 / (nt * nr * nc * rl)
    every(arrived, a_whole_in)

    def place(d, _):
        ow_out[pl.ds(d, CH, stride=CH), :] = a5[d].astype(F32) * (factor / S)
        return 0

    lax.fori_loop(0, CH, place, 0)

    for k in range(1, nr):
        arrived(*b_row2_in(k))
    whole = b4[:, :pr, :].reshape(4 * CH, 128) * factor
    pw_out[:, :128] = whole[: 2 * CH]
    pw_out[:, 128:] = whole[2 * CH :]
    for q in range(nr):
        vec[q * vr : (q + 1) * vr, :] = b4[q, pr : pr + vr, :] * factor
    pbias_out[...] = vec[0:1, : 2 * CH]
    gain_out[...] = jnp.concatenate([vec[1:2, :], vec[2:3, :]], 1)
    shift_out[...] = jnp.concatenate([vec[3:4, :], vec[4:5, :]], 1)
    ob_out[...] = vec[5:6, :]

    dx_copy.wait()
    for k in range(2):
        sent(*gather_left(k))
        sent(*relay_left(k))
        sent(*relay_right(k))
        sent(*far_right(k))
        sent(*far_left(k))
        sent(*near_left(k))
        for part in range(2):
            sent(*gather_right(k, part))
            sent(*near_right(k, part))
            unless(z == k, lambda: sent(*first_right(k, part)))
        unless(q_at == k, lambda: sent(*scatter_right(k)))
    every(sent, a_part)
    every(sent, a_whole)
    for k in range(1, nc):
        sent(*b_col(k))
    for k in range(1, nr):
        sent(*b_row(k))
        sent(*b_row2(k))
    for k in range(1, nt):
        sent(*a_tgt(k))
        sent(*b_tgt(k))


def per_device(
    homolog_activation_matrix,
    standardizer_multiplier,
    standardizer_offset,
    side_mapping_matrices,
    side_mapping_offsets,
    final_channel_matrix,
    residue_couple_cotangent,
):
    nt, nr, nc = axis_sizes()
    rl = homolog_activation_matrix.shape[2]
    ni, nj = rl * nc, rl * nr
    pr = 4 * CH // nr + 8
    vmem = functools.partial(pl.BlockSpec, memory_space=pltpu.VMEM)
    hbm = functools.partial(pl.BlockSpec, memory_space=pl.ANY)

    def sems(*n):
        return [pltpu.SemaphoreType.DMA(n), pltpu.SemaphoreType.DMA(n)]

    results = pl.pallas_call(
        functools.partial(kernel, (nt, nr, nc, rl)),
        out_shape=(
            jax.ShapeDtypeStruct((S * rl, CM), BF16),
            jax.ShapeDtypeStruct((2 * CH, CM), F32),
            jax.ShapeDtypeStruct((1, 2 * CH), F32),
            jax.ShapeDtypeStruct((1, CM), F32),
            jax.ShapeDtypeStruct((1, CM), F32),
            jax.ShapeDtypeStruct((CH * CH, CZ), F32),
            jax.ShapeDtypeStruct((1, CZ), F32),
        ),
        in_specs=[hbm(), vmem(), vmem(), vmem(), vmem(), vmem(), hbm()],
        out_specs=(hbm(), vmem(), vmem(), vmem(), vmem(), vmem(), vmem()),
        scratch_shapes=[
            pltpu.VMEM((S * rl, CM), BF16),
            pltpu.VMEM((ni * nj, CZ), BF16),
            pltpu.VMEM((2, S * rl, 128), F32),
            pltpu.VMEM((S * rl, 128), F32),
            pltpu.VMEM((S * rl, CM), BF16),
            pltpu.VMEM((ni * CH, S), BF16),
            pltpu.VMEM((S, ni * CH), BF16),
            pltpu.VMEM((CH, 2, nj // 2, S), BF16),
            pltpu.VMEM((CH, rl, S), BF16),
            pltpu.VMEM((rl * CH, S), F32),
            pltpu.VMEM((CH * CH, CZ), F32),
            pltpu.VMEM((CH * CH, CZ), BF16),
            pltpu.VMEM((ni * CH, CH * nj), BF16),
            pltpu.VMEM((CH, 2, nj // 2, S), BF16),
            pltpu.VMEM((nc, rl * CH, S), BF16),
            pltpu.VMEM((2, CH // 2, 2, rl, S), BF16),
            pltpu.VMEM((2, CH, 2, rl, S), BF16),
            pltpu.VMEM((2, CH, rl, S), BF16),
            pltpu.VMEM((2, CH, rl, S), BF16),
            pltpu.VMEM((2, rl * CH // 2, S), BF16),
            pltpu.VMEM((2, rl * CH, S), BF16),
            pltpu.VMEM((2 * rl * CH, S), F32),
            pltpu.VMEM((CH * CH, 8 * nj), BF16),
            pltpu.VMEM((CH * CH, CZ), F32),
            pltpu.VMEM((CH * CH, CZ), BF16),
            pltpu.VMEM((8, CZ), F32),
            pltpu.VMEM((nr * nc, CH, CZ), BF16),
            pltpu.VMEM((nt, CH, CZ), F32),
            pltpu.VMEM((nr * nc, CH, CZ), BF16),
            pltpu.VMEM((S * rl, CM), F32),
            pltpu.VMEM((2 * CH, CM), F32),
            pltpu.VMEM((8, 128), F32),
            pltpu.VMEM((8, 2 * CM + 128), F32),
            pltpu.VMEM((nr, pr, 128), F32),
            pltpu.VMEM((nr, pr, 128), F32),
            pltpu.VMEM((nc, pr, 128), F32),
            pltpu.VMEM((nt, pr, 128), F32),
            pltpu.VMEM((nr, pr, 128), F32),
            pltpu.SemaphoreType.DMA((3,)),
        ]
        + sems(2)
        + sems(2)
        + 2 * sems(2, 2)
        + sems(2)
        + sems(2)
        + sems(2, 2)
        + 3 * sems(2)
        + sems(nr * nc)
        + sems(nt)
        + sems(nr * nc)
        + sems(nr)
        + sems(nc)
        + sems(nt)
        + sems(nr),
        compiler_params=pltpu.CompilerParams(
            collective_id=0, has_side_effects=True, vmem_limit_bytes=56 * 1024 * 1024
        ),
        cost_estimate=pl.CostEstimate(
            flops=10 * ni * nj * CH * CH * CZ, bytes_accessed=5 * 1024 * 1024, transcendentals=0
        ),
    )(
        homolog_activation_matrix.reshape(S * rl, CM),
        standardizer_multiplier.reshape(1, CM),
        standardizer_offset.reshape(1, CM),
        side_mapping_matrices.T,
        side_mapping_offsets.reshape(1, 2 * CH),
        final_channel_matrix,
        residue_couple_cotangent.reshape(ni * nj, CZ),
    )
    return (
        results[0].reshape(1, S, rl, CM),
        results[1].T,
        results[2].reshape(2 * CH),
        results[3].reshape(CM),
        results[4].reshape(CM),
        results[5],
        results[6].reshape(CZ),
    )


def solution(mesh):
    placed = (
        P("tgt", None, ("row", "col"), None),
        P(),
        P(),
        P(),
        P(),
        P(),
        P("tgt", "row", "col", None),
    )
    return jax.shard_map(
        per_device,
        mesh=mesh,
        in_specs=placed,
        out_specs=(P("tgt", None, ("row", "col"), None), P(), P(), P(), P(), P(), P()),
        check_vma=False,
    )
```

```python
import functools

import jax
import jax.numpy as jnp
from jax import lax
from jax.experimental import pallas as pl
from jax.experimental.pallas import tpu as pltpu
from jax.sharding import PartitionSpec as P

CM = 256
CH = 32
CZ = 128
S = 128
F32 = jnp.float32
BF16 = jnp.bfloat16
NT_DIMS = (((1,), (1,)), ((), ()))
NN_DIMS = (((1,), (0,)), ((), ()))


def mm(a, b, dims=NN_DIMS):
    return lax.dot_general(a, b, dims, preferred_element_type=F32)


def axis_sizes():
    return lax.axis_size("tgt"), lax.axis_size("row"), lax.axis_size("col")


def axis_places():
    return lax.axis_index("tgt"), lax.axis_index("row"), lax.axis_index("col")


def descriptor(src, dst, send, recv, where):
    return pltpu.make_async_remote_copy(
        src_ref=src,
        dst_ref=dst,
        send_sem=send,
        recv_sem=recv,
        device_id=where,
        device_id_type=pl.DeviceIdType.MESH,
    )


def push(*args):
    descriptor(*args).start()


def sent(*args):
    descriptor(*args).wait_send()


def arrived(*args):
    descriptor(*args).wait_recv()


def greet(nt, nr, nc, t, r, c):
    barrier = pltpu.get_barrier_semaphore()
    flat = r * nc + c
    for k in range(1, nr * nc):
        other = lax.rem(flat + k, nr * nc)
        pl.semaphore_signal(
            barrier,
            inc=1,
            device_id={"row": other // nc, "col": lax.rem(other, nc)},
            device_id_type=pl.DeviceIdType.MESH,
        )
    for k in range(1, nt):
        pl.semaphore_signal(
            barrier,
            inc=1,
            device_id={"tgt": lax.rem(t + k, nt)},
            device_id_type=pl.DeviceIdType.MESH,
        )


def meet(nt, nr, nc):
    pl.semaphore_wait(pltpu.get_barrier_semaphore(), nr * nc - 1 + nt - 1)


def kernel(
    sizes,
    h_ref,
    mult_ref,
    off_ref,
    pm_ref,
    pb_ref,
    w_ref,
    g_ref,
    dx_out,
    pw_out,
    pbias_out,
    gain_out,
    shift_out,
    ow_out,
    ob_out,
    h,
    g,
    nrm,
    inv,
    no,
    lt,
    lmat,
    rt,
    rown,
    rf,
    wf,
    wp,
    pair,
    rp,
    lp,
    ra,
    rb,
    ms,
    rr,
    la,
    lb,
    side,
    on,
    dw,
    dwb,
    obacc,
    a1,
    a3,
    a5,
    grads,
    pwt,
    vec,
    acc,
    sb,
    b1,
    b2,
    b3,
    b4,
    local_sem,
    gl_send,
    gl_recv,
    gl2_send,
    gl2_recv,
    gr1_send,
    gr1_recv,
    gr_send,
    gr_recv,
    gr2_send,
    gr2_recv,
    sr1_send,
    sr1_recv,
    sr2_send,
    sr2_recv,
    sr3_send,
    sr3_recv,
    sl1_send,
    sl1_recv,
    sl2_send,
    sl2_recv,
    a_part_send,
    a_part_recv,
    a_tgt_send,
    a_tgt_recv,
    a_whole_send,
    a_whole_recv,
    b_row_send,
    b_row_recv,
    b_col_send,
    b_col_recv,
    b_tgt_send,
    b_tgt_recv,
    b_row2_send,
    b_row2_recv,
):
    nt, nr, nc, rl = sizes
    rpc = nr // nc
    nx = nr // rpc
    assert nx == nc == 4 and rpc == 2
    ni, nj = rl * nc, rl * nr
    lrows = rl * CH
    t, r, c = axis_places()
    home = lax.div(r, rpc)
    z, x_at, q_at = lax.div(r, nx), lax.rem(r, nx), lax.rem(r, rpc)
    c_half, c_odd = lax.div(c, 2), lax.rem(c, 2)
    side_x = lax.rem(x_at + jnp.where(lax.rem(x_at, 2) == 1, 1, nx - 1), nx)
    via = jnp.where(c_odd == 1, side_x, x_at)
    own = jnp.logical_and(via == x_at, home == c)
    half, lhalf = CH // 2, lrows // 2

    h_in = pltpu.make_async_copy(h_ref, h, local_sem.at[0])
    h_in.start()
    g_in = pltpu.make_async_copy(g_ref, g, local_sem.at[1])
    g_in.start()
    greet(nt, nr, nc, t, r, c)

    mult = mult_ref[...]
    off = off_ref[...]
    pt = pm_ref[...]
    bias = jnp.broadcast_to(pb_ref[...], (S, 2 * CH)).T

    wf[...] = w_ref[...].astype(F32)

    def reorder(d, _):
        rows = wf[pl.ds(d, CH, stride=CH), :]
        wp[pl.ds(pl.multiple_of(d * CH, CH), CH), :] = rows.astype(BF16)
        return 0

    lax.fori_loop(0, CH, reorder, 0)
    h_in.wait()

    def normalise(k, _):
        rows = pl.ds(pl.multiple_of(k * 128, 128), 128)
        x = h[rows, :].astype(F32)
        centred = x - jnp.mean(x, -1, keepdims=True)
        scale = lax.rsqrt(jnp.mean(centred * centred, -1, keepdims=True) + 1e-05)
        x = centred * scale
        nrm[0, rows, :] = x[:, :128]
        nrm[1, rows, :] = x[:, 128:]
        inv[rows, :] = jnp.broadcast_to(scale, (128, 128))
        return 0

    lax.fori_loop(0, S * rl // 128, normalise, 0)

    def project(k, _):
        at = pl.ds(k, S, stride=rl)
        x = jnp.concatenate([nrm[0, at, :], nrm[1, at, :]], 1)
        row = (x * mult + off).astype(BF16)
        no[pl.ds(pl.multiple_of(k * S, S), S), :] = row
        y = (mm(pt, row, NT_DIMS) + bias).astype(BF16)
        lt[pl.ds(pl.multiple_of(c * lrows + k * CH, CH), CH), :] = y[:CH]
        rf[pl.ds(pl.multiple_of(k * CH, CH), CH), :] = y[CH:].astype(F32)
        return 0

    lax.fori_loop(0, rl, project, 0)

    def turn(d, _):
        rown[d] = rf[pl.ds(d, rl, stride=CH), :].astype(BF16)
        return 0

    lax.fori_loop(0, CH, turn, 0)
    meet(nt, nr, nc)

    def xs(k):
        return lax.rem(x_at + k, nx)

    def cs(k):
        return lax.rem(c + k, nc)

    def to_x(k):
        return {"row": z * nx + xs(1 if k == 0 else nx - 1)}

    def to_c(k):
        return {"col": cs(1 if k == 0 else nc - 1)}

    back_of = (3, 1)

    def left_block(k, part=None):
        at, size = (k * lrows, lrows) if part is None else (k * lrows + part * lhalf, lhalf)
        return lt.at[pl.ds(pl.multiple_of(at, lhalf), size), :]

    def spot(x):
        e = lax.rem(x + nx - 2 * c_odd, nx)
        return lax.div(lax.rem(e + 1, nx), 2), lax.div(e, 2)

    my_q, my_odd = spot(x_at)

    def right_block(x, part):
        q, odd = spot(x)
        return rt.at[part * half : (part + 1) * half, q, :, odd]

    def gather_left(k):
        return left_block(c), left_block(c), gl_send.at[k], gl_recv.at[k], to_c(k)

    def gather_left_in(k):
        at = left_block(cs(back_of[k]))
        return at, at, gl_send.at[k], gl_recv.at[k], to_c(k)

    def relay_left(k):
        at = left_block(cs(back_of[k]), k)
        return at, at, gl2_send.at[k], gl2_recv.at[k], to_c(k)

    def relay_left_in(k):
        at = left_block(cs(2), k)
        return at, at, gl2_send.at[k], gl2_recv.at[k], to_c(k)

    def first_right(k, part):
        rows = slice(part * half, (part + 1) * half)
        to = rt.at[rows, q_at, c_half, c_odd]
        where = {"row": k * nx + via, "col": home}
        return rown.at[rows], to, gr1_send.at[k, part], gr1_recv.at[c_half, part], where

    def first_right_in(k, part):
        rows = slice(part * half, (part + 1) * half)
        to = rt.at[rows, my_q, k, my_odd]
        where = {"row": rpc * c + my_q, "col": 2 * k + my_odd}
        return rown.at[rows], to, gr1_send.at[k, part], gr1_recv.at[k, part], where

    def gather_right(k, part):
        at = right_block(x_at, part)
        return at, at, gr_send.at[k, part], gr_recv.at[k, part], to_x(k)

    def gather_right_in(k, part):
        at = right_block(xs(back_of[k]), part)
        return at, at, gr_send.at[k, part], gr_recv.at[k, part], to_x(k)

    def relay_right(k):
        at = right_block(xs(back_of[k]), k)
        return at, at, gr2_send.at[k], gr2_recv.at[k], to_x(k)

    def relay_right_in(k):
        at = right_block(xs(2), k)
        return at, at, gr2_send.at[k], gr2_recv.at[k], to_x(k)

    def unless(same, act):
        pl.when(jnp.logical_not(jnp.logical_and(own, same)))(act)

    for part in range(2):
        for k in range(rpc):
            unless(z == k, lambda: push(*first_right(k, part)))

    @pl.when(own)
    def _():
        rt[:, q_at, c_half, c_odd] = rown[...]

    for k in range(2):
        push(*gather_left(k))

    g_in.wait()
    obacc[...] = jnp.zeros_like(obacc)

    def back(k, _):
        rows = g[pl.ds(pl.multiple_of(k * 2 * nj, 2 * nj), 2 * nj), :]
        y = mm(wp[...], rows, NT_DIMS).astype(BF16)
        for q in range(2):
            at = pl.ds(pl.multiple_of((2 * k + q) * CH, CH), CH)
            for d in range(CH):
                pair[at, d * nj : (d + 1) * nj] = y[d * CH : (d + 1) * CH, q * nj : (q + 1) * nj]
        obacc[...] += jnp.sum(rows.astype(F32).reshape(2 * nj // 8, 8, CZ), 0)
        return 0

    lax.fori_loop(0, 6 * ni // 32, back, 0, unroll=2)
    for k in range(2):
        arrived(*gather_left_in(k))
        push(*relay_left(k))
    lax.fori_loop(6 * ni // 32, 9 * ni // 32, back, 0, unroll=2)
    for k in range(rpc):
        unless(c_half == k, lambda: arrived(*first_right_in(k, 0)))
    for k in range(2):
        push(*gather_right(k, 0))
    lax.fori_loop(9 * ni // 32, 11 * ni // 32, back, 0, unroll=2)
    for k in range(rpc):
        unless(c_half == k, lambda: arrived(*first_right_in(k, 1)))
    for k in range(2):
        push(*gather_right(1 - k, 1))
    lax.fori_loop(11 * ni // 32, ni // 2, back, 0, unroll=2)
    arrived(*gather_right_in(0, 0))
    push(*relay_right(0))

    for k in range(2):
        arrived(*relay_left_in(k))
    def flip(k, _):
        at = pl.ds(pl.multiple_of(k * 128, 128), 128)
        lmat[:, at] = lt[at, :].T
        return 0

    lax.fori_loop(0, ni * CH // 128, flip, 0)

    def right_step(k, _):
        lanes = pl.ds(pl.multiple_of(k * 8 * nj, 8 * nj), 8 * nj)
        y = mm(lmat[...], pair[:, lanes]).T
        rp[pl.ds(8 * k, 8)] = y.reshape(8, 2, 2, 2, rl, S).astype(BF16)
        return 0

    def right_sum(x, part):
        q, odd = spot(x)
        return rp.at[part * half : (part + 1) * half, q, :, odd]

    def far_right(k):
        return right_sum(xs(2), k), ra.at[k], sr1_send.at[k], sr1_recv.at[k], to_x(k)

    def near_right(k, part):
        at = right_sum(xs(1 if k == 0 else 3), part)
        to = rb.at[k, part * half : (part + 1) * half]
        return at, to, sr2_send.at[k, part], sr2_recv.at[k, part], to_x(k)

    def scatter_right(k):
        where = {"row": rpc * c + my_q, "col": 2 * k + my_odd}
        return ms.at[k], rr.at[z], sr3_send.at[k], sr3_recv.at[z], where

    def scatter_right_in(k):
        where = {"row": k * nx + via, "col": home}
        return ms.at[k], rr.at[k], sr3_send.at[k], sr3_recv.at[k], where

    lax.fori_loop(0, CH // 16, right_step, 0)
    push(*far_right(0))
    push(*near_right(1, 0))
    arrived(*gather_right_in(1, 1))
    push(*relay_right(1))
    lax.fori_loop(CH // 16, CH // 8, right_step, 0)
    push(*far_right(1))
    push(*near_right(0, 1))

    for k in range(2):
        arrived(*gather_right_in(k, 1 - k))
    for k in range(2):
        arrived(*relay_right_in(k))

    def left_rows(k):
        return pl.ds(pl.multiple_of(k * lrows, lrows), lrows)

    def far_left(k):
        at = lp.at[cs(2), k * lhalf : (k + 1) * lhalf]
        return at, la.at[k], sl1_send.at[k], sl1_recv.at[k], to_c(k)

    def near_left(k):
        at = lp.at[cs(1 if k == 0 else 3)]
        return at, lb.at[k], sl2_send.at[k], sl2_recv.at[k], to_c(k)

    def left_step(k, _):
        right_all = rt[...].reshape(CH * nj, S)
        lp[k] = mm(pair[left_rows(k), :], right_all).astype(BF16)
        return 0

    left_step(cs(2), 0)
    for k in range(2):
        push(*far_left(k))
    left_step(cs(1), 0)
    for k in range(2):
        arrived(*far_right(k))
        at = right_sum(xs(1 if k == 0 else 3), k)
        at[...] = (at[...].astype(F32) + ra[k].astype(F32)).astype(BF16)
        push(*near_right(k, k))
    left_step(cs(3), 0)
    for k in range(2):
        arrived(*far_left(k))
    for k in range(2):
        at = lp.at[cs(1 if k == 0 else 3), k * lhalf : (k + 1) * lhalf]
        at[...] = (at[...].astype(F32) + la[k].astype(F32)).astype(BF16)
        push(*near_left(k))
    left_step(c, 0)

    dw[...] = jnp.zeros_like(dw)

    def weigh(k, _):
        rows = lt[pl.ds(pl.multiple_of(k * 8 * CH, 8 * CH), 8 * CH), :]
        for v in range(8):
            part = rt[v * 4 : (v + 1) * 4].reshape(4 * nj, S)
            y = mm(rows, part, NT_DIMS).astype(BF16)
            for q in range(8):
                for d in range(4):
                    on[(v * 4 + d) * CH : (v * 4 + d + 1) * CH, q * nj : (q + 1) * nj] = y[
                        q * CH : (q + 1) * CH, d * nj : (d + 1) * nj
                    ]
        dw[...] += mm(on[...], g[pl.ds(pl.multiple_of(k * 8 * nj, 8 * nj), 8 * nj), :])
        return 0

    lax.fori_loop(0, ni // 32, weigh, 0)
    for k in range(2):
        for part in range(2):
            arrived(*near_right(k, part))
    for k in range(rpc):
        total = rp[:, my_q, k, my_odd].astype(F32)
        total += rb[0, :, k].astype(F32)
        total += rb[1, :, k].astype(F32)
        ms[k] = total.astype(BF16)
    for k in range(rpc):
        unless(c_half == k, lambda: push(*scatter_right(k)))

    @pl.when(own)
    def _():
        rr[z] = ms[c_half]

    lax.fori_loop(ni // 32, ni // 8, weigh, 0)

    group = nr * nc
    flat = r * nc + c

    def member(k):
        f = lax.rem(flat + k, group)
        return f, {"row": lax.div(f, nc), "col": lax.rem(f, nc)}

    def a_part(k):
        f, where = member(k)
        src = dwb.at[pl.ds(pl.multiple_of(f * CH, CH), CH), :]
        return src, a1.at[flat], a_part_send.at[k], a_part_recv.at[flat], where

    def a_part_in(k):
        f, where = member(k)
        src = dwb.at[pl.ds(pl.multiple_of(flat * CH, CH), CH), :]
        return src, a1.at[f], a_part_send.at[k], a_part_recv.at[f], where

    def a_whole(k):
        _, where = member(k)
        return a5.at[flat], a5.at[flat], a_whole_send.at[k], a_whole_recv.at[flat], where

    def a_whole_in(k):
        f, where = member(k)
        return a5.at[f], a5.at[f], a_whole_send.at[k], a_whole_recv.at[f], where

    def every(act, copy):
        def step(k, _):
            act(*copy(k))
            return 0

        lax.fori_loop(1, group, step, 0)

    dwb[...] = dw[...].astype(BF16)
    every(push, a_part)
    a1[flat] = dwb[pl.ds(pl.multiple_of(flat * CH, CH), CH), :]

    for k in range(2):
        arrived(*near_left(k))
    for k in range(rpc):
        unless(z == k, lambda: arrived(*scatter_right_in(k)))

    def sum_left(k, _):
        at = pl.ds(pl.multiple_of(k * 128, 128), 128)
        total = lp[c, at, :].astype(F32)
        for q in range(2):
            total += lb[q, at, :].astype(F32)
        side[at, :] = total * (1.0 / S)
        return 0

    lax.fori_loop(0, lrows // 128, sum_left, 0)

    def sum_right(k, _):
        at = pl.ds(k * 8, 8)
        total = rr[0, at].astype(F32)
        for q in range(1, rpc):
            total += rr[q, at].astype(F32)
        to = pl.ds(pl.multiple_of(lrows + k * 8 * rl, 8 * rl), 8 * rl)
        side[to, :] = total.reshape(8 * rl, S) * (1.0 / S)
        return 0

    lax.fori_loop(0, CH // 8, sum_right, 0)

    pwt[...] = jnp.zeros_like(pwt)
    acc[...] = jnp.zeros_like(acc)

    def finish(k, _):
        left = side[pl.ds(pl.multiple_of(k * CH, CH), CH), :]
        right = side[pl.ds(lrows + k, CH, stride=rl), :]
        both = jnp.concatenate([left, right], 0)
        rounded = both.astype(BF16)
        turned = both.T
        acc[:, 2 * CM : 2 * CM + 2 * CH] += jnp.sum(turned.reshape(S // 8, 8, 2 * CH), 0)
        grad = mm(turned.astype(BF16), pt)
        grads[pl.ds(pl.multiple_of(k * S, S), S), :] = grad
        pwt[...] += mm(rounded, no[pl.ds(pl.multiple_of(k * S, S), S), :])
        at = pl.ds(k, S, stride=rl)
        x = jnp.concatenate([nrm[0, at, :], nrm[1, at, :]], 1)
        acc[:, :CM] += jnp.sum((grad * x).reshape(S // 8, 8, CM), 0)
        acc[:, CM : 2 * CM] += jnp.sum(grad.reshape(S // 8, 8, CM), 0)
        return 0

    lax.fori_loop(0, rl, finish, 0)

    pr = 2 * 2 * CH // nr
    vr = 8 // nr
    vec[...] = jnp.zeros_like(vec)
    small = jnp.sum(acc[...], 0, keepdims=True)
    vec[0:1, : 2 * CH] = small[:, 2 * CM : 2 * CM + 2 * CH]
    for k in range(4):
        vec[1 + k : 2 + k, :] = small[:, k * 128 : (k + 1) * 128]
    vec[5:6, :] = jnp.sum(obacc[...], 0, keepdims=True)
    weights = pwt[...]
    stacked = jnp.concatenate([weights[:, :128], weights[:, 128:]], 0)
    sb[...] = jnp.zeros_like(sb)
    for q in range(nr):
        sb[q, :pr, :] = stacked[q * pr : (q + 1) * pr]
        sb[q, pr : pr + vr, :] = vec[q * vr : (q + 1) * vr, :]

    def b_row(k):
        q = lax.rem(r + k, nr)
        return sb.at[q], b1.at[r], b_row_send.at[k], b_row_recv.at[r], {"row": q}

    def b_row_in(k):
        q = lax.rem(r + k, nr)
        return sb.at[q], b1.at[q], b_row_send.at[k], b_row_recv.at[q], {"row": q}

    for k in range(1, nr):
        push(*b_row(k))
    b1[r] = sb[r]

    every(arrived, a_part_in)
    total = a1[0].astype(F32)
    for q in range(1, group):
        total += a1[q].astype(F32)
    a3[t] = total

    def a_tgt(k):
        q = lax.rem(t + k, nt)
        return a3.at[t], a3.at[t], a_tgt_send.at[k], a_tgt_recv.at[t], {"tgt": q}

    def a_tgt_in(k):
        q = lax.rem(t + k, nt)
        return a3.at[q], a3.at[q], a_tgt_send.at[k], a_tgt_recv.at[q], {"tgt": q}

    for k in range(1, nt):
        push(*a_tgt(k))

    def descend(k, _):
        grad = grads[pl.ds(pl.multiple_of(k * S, S), S), :]
        at = pl.ds(k, S, stride=rl)
        x = jnp.concatenate([nrm[0, at, :], nrm[1, at, :]], 1)
        scale = inv[at, :]
        scaled = grad * mult
        dx = scaled - jnp.mean(scaled, -1, keepdims=True) - x * jnp.mean(scaled * x, -1, keepdims=True)
        nrm[0, at, :] = dx[:, :128] * scale
        nrm[1, at, :] = dx[:, 128:] * scale
        return 0

    lax.fori_loop(0, rl // 2, descend, 0)

    for k in range(1, nr):
        arrived(*b_row_in(k))
    total = b1[0]
    for q in range(1, nr):
        total += b1[q]
    b2[c] = total

    def b_col(k):
        q = lax.rem(c + k, nc)
        return b2.at[c], b2.at[c], b_col_send.at[k], b_col_recv.at[c], {"col": q}

    def b_col_in(k):
        q = lax.rem(c + k, nc)
        return b2.at[q], b2.at[q], b_col_send.at[k], b_col_recv.at[q], {"col": q}

    for k in range(1, nc):
        push(*b_col(k))

    lax.fori_loop(rl // 2, rl, descend, 0)

    def emit(k, _):
        rows = pl.ds(pl.multiple_of(k * 128, 128), 128)
        h[rows, :128] = nrm[0, rows, :].astype(BF16)
        h[rows, 128:] = nrm[1, rows, :].astype(BF16)
        return 0

    lax.fori_loop(0, S * rl // 128, emit, 0)
    dx_copy = pltpu.make_async_copy(h, dx_out, local_sem.at[2])
    dx_copy.start()

    for k in range(1, nc):
        arrived(*b_col_in(k))
    total = b2[0]
    for q in range(1, nc):
        total += b2[q]
    b3[t] = total

    def b_tgt(k):
        q = lax.rem(t + k, nt)
        return b3.at[t], b3.at[t], b_tgt_send.at[k], b_tgt_recv.at[t], {"tgt": q}

    def b_tgt_in(k):
        q = lax.rem(t + k, nt)
        return b3.at[q], b3.at[q], b_tgt_send.at[k], b_tgt_recv.at[q], {"tgt": q}

    for k in range(1, nt):
        push(*b_tgt(k))

    for k in range(1, nt):
        arrived(*a_tgt_in(k))
    total = a3[0]
    for q in range(1, nt):
        total += a3[q]
    a5[flat] = total.astype(BF16)
    every(push, a_whole)

    for k in range(1, nt):
        arrived(*b_tgt_in(k))
    total = b3[0]
    for q in range(1, nt):
        total += b3[q]
    b4[r] = total

    def b_row2(k):
        q = lax.rem(r + k, nr)
        return b4.at[r], b4.at[r], b_row2_send.at[k], b_row2_recv.at[r], {"row": q}

    def b_row2_in(k):
        q = lax.rem(r + k, nr)
        return b4.at[q], b4.at[q], b_row2_send.at[k], b_row2_recv.at[q], {"row": q}

    for k in range(1, nr):
        push(*b_row2(k))

    factor = 1.0 / (nt * nr * nc * rl)
    every(arrived, a_whole_in)

    def place(d, _):
        ow_out[pl.ds(d, CH, stride=CH), :] = a5[d].astype(F32) * (factor / S)
        return 0

    lax.fori_loop(0, CH, place, 0)

    for k in range(2):
        sent(*gather_left(k))
        sent(*relay_left(k))
        sent(*relay_right(k))
        sent(*far_right(k))
        sent(*far_left(k))
        sent(*near_left(k))
        for part in range(2):
            sent(*gather_right(k, part))
            sent(*near_right(k, part))
            unless(z == k, lambda: sent(*first_right(k, part)))
        unless(c_half == k, lambda: sent(*scatter_right(k)))
    every(sent, a_part)
    for k in range(1, nc):
        sent(*b_col(k))
    for k in range(1, nr):
        sent(*b_row(k))
    for k in range(1, nt):
        sent(*a_tgt(k))
        sent(*b_tgt(k))
    dx_copy.wait()
    for k in range(1, nr):
        arrived(*b_row2_in(k))
    whole = b4[:, :pr, :].reshape(4 * CH, 128) * factor
    pw_out[:, :128] = whole[: 2 * CH]
    pw_out[:, 128:] = whole[2 * CH :]
    for q in range(nr):
        vec[q * vr : (q + 1) * vr, :] = b4[q, pr : pr + vr, :] * factor
    pbias_out[...] = vec[0:1, : 2 * CH]
    gain_out[...] = jnp.concatenate([vec[1:2, :], vec[2:3, :]], 1)
    shift_out[...] = jnp.concatenate([vec[3:4, :], vec[4:5, :]], 1)
    ob_out[...] = vec[5:6, :]

    every(sent, a_whole)
    for k in range(1, nr):
        sent(*b_row2(k))


def per_device(
    homolog_activation_matrix,
    standardizer_multiplier,
    standardizer_offset,
    side_mapping_matrices,
    side_mapping_offsets,
    final_channel_matrix,
    residue_couple_cotangent,
):
    nt, nr, nc = axis_sizes()
    rl = homolog_activation_matrix.shape[2]
    ni, nj = rl * nc, rl * nr
    pr = 4 * CH // nr + 8
    vmem = functools.partial(pl.BlockSpec, memory_space=pltpu.VMEM)
    hbm = functools.partial(pl.BlockSpec, memory_space=pl.ANY)

    def sems(*n):
        return [pltpu.SemaphoreType.DMA(n), pltpu.SemaphoreType.DMA(n)]

    results = pl.pallas_call(
        functools.partial(kernel, (nt, nr, nc, rl)),
        out_shape=(
            jax.ShapeDtypeStruct((S * rl, CM), BF16),
            jax.ShapeDtypeStruct((2 * CH, CM), F32),
            jax.ShapeDtypeStruct((1, 2 * CH), F32),
            jax.ShapeDtypeStruct((1, CM), F32),
            jax.ShapeDtypeStruct((1, CM), F32),
            jax.ShapeDtypeStruct((CH * CH, CZ), F32),
            jax.ShapeDtypeStruct((1, CZ), F32),
        ),
        in_specs=[hbm(), vmem(), vmem(), vmem(), vmem(), vmem(), hbm()],
        out_specs=(hbm(), vmem(), vmem(), vmem(), vmem(), vmem(), vmem()),
        scratch_shapes=[
            pltpu.VMEM((S * rl, CM), BF16),
            pltpu.VMEM((ni * nj, CZ), BF16),
            pltpu.VMEM((2, S * rl, 128), F32),
            pltpu.VMEM((S * rl, 128), F32),
            pltpu.VMEM((S * rl, CM), BF16),
            pltpu.VMEM((ni * CH, S), BF16),
            pltpu.VMEM((S, ni * CH), BF16),
            pltpu.VMEM((CH, 2, 2, 2, rl, S), BF16),
            pltpu.VMEM((CH, rl, S), BF16),
            pltpu.VMEM((rl * CH, S), F32),
            pltpu.VMEM((CH * CH, CZ), F32),
            pltpu.VMEM((CH * CH, CZ), BF16),
            pltpu.VMEM((ni * CH, CH * nj), BF16),
            pltpu.VMEM((CH, 2, 2, 2, rl, S), BF16),
            pltpu.VMEM((nc, rl * CH, S), BF16),
            pltpu.VMEM((2, CH // 2, 2, rl, S), BF16),
            pltpu.VMEM((2, CH, 2, rl, S), BF16),
            pltpu.VMEM((2, CH, rl, S), BF16),
            pltpu.VMEM((2, CH, rl, S), BF16),
            pltpu.VMEM((2, rl * CH // 2, S), BF16),
            pltpu.VMEM((2, rl * CH, S), BF16),
            pltpu.VMEM((2 * rl * CH, S), F32),
            pltpu.VMEM((CH * CH, 8 * nj), BF16),
            pltpu.VMEM((CH * CH, CZ), F32),
            pltpu.VMEM((CH * CH, CZ), BF16),
            pltpu.VMEM((8, CZ), F32),
            pltpu.VMEM((nr * nc, CH, CZ), BF16),
            pltpu.VMEM((nt, CH, CZ), F32),
            pltpu.VMEM((nr * nc, CH, CZ), BF16),
            pltpu.VMEM((S * rl, CM), F32),
            pltpu.VMEM((2 * CH, CM), F32),
            pltpu.VMEM((8, 128), F32),
            pltpu.VMEM((8, 2 * CM + 128), F32),
            pltpu.VMEM((nr, pr, 128), F32),
            pltpu.VMEM((nr, pr, 128), F32),
            pltpu.VMEM((nc, pr, 128), F32),
            pltpu.VMEM((nt, pr, 128), F32),
            pltpu.VMEM((nr, pr, 128), F32),
            pltpu.SemaphoreType.DMA((3,)),
        ]
        + sems(2)
        + sems(2)
        + 2 * sems(2, 2)
        + sems(2)
        + sems(2)
        + sems(2, 2)
        + 3 * sems(2)
        + sems(nr * nc)
        + sems(nt)
        + sems(nr * nc)
        + sems(nr)
        + sems(nc)
        + sems(nt)
        + sems(nr),
        compiler_params=pltpu.CompilerParams(
            collective_id=0, has_side_effects=True, vmem_limit_bytes=56 * 1024 * 1024
        ),
        cost_estimate=pl.CostEstimate(
            flops=10 * ni * nj * CH * CH * CZ, bytes_accessed=5 * 1024 * 1024, transcendentals=0
        ),
    )(
        homolog_activation_matrix.reshape(S * rl, CM),
        standardizer_multiplier.reshape(1, CM),
        standardizer_offset.reshape(1, CM),
        side_mapping_matrices.T,
        side_mapping_offsets.reshape(1, 2 * CH),
        final_channel_matrix,
        residue_couple_cotangent.reshape(ni * nj, CZ),
    )
    return (
        results[0].reshape(1, S, rl, CM),
        results[1].T,
        results[2].reshape(2 * CH),
        results[3].reshape(CM),
        results[4].reshape(CM),
        results[5],
        results[6].reshape(CZ),
    )


def solution(mesh):
    placed = (
        P("tgt", None, ("row", "col"), None),
        P(),
        P(),
        P(),
        P(),
        P(),
        P("tgt", "row", "col", None),
    )
    return jax.shard_map(
        per_device,
        mesh=mesh,
        in_specs=placed,
        out_specs=(P("tgt", None, ("row", "col"), None), P(), P(), P(), P(), P(), P()),
        check_vma=False,
    )
```

```python
import functools

import jax
import jax.numpy as jnp
from jax import lax
from jax.experimental import pallas as pl
from jax.experimental.pallas import tpu as pltpu
from jax.sharding import PartitionSpec as P

CM = 256
CH = 32
CZ = 128
S = 128
F32 = jnp.float32
BF16 = jnp.bfloat16
NT_DIMS = (((1,), (1,)), ((), ()))
NN_DIMS = (((1,), (0,)), ((), ()))


def mm(a, b, dims=NN_DIMS):
    return lax.dot_general(a, b, dims, preferred_element_type=F32)


def axis_sizes():
    return lax.axis_size("tgt"), lax.axis_size("row"), lax.axis_size("col")


def axis_places():
    return lax.axis_index("tgt"), lax.axis_index("row"), lax.axis_index("col")


def descriptor(src, dst, send, recv, where):
    return pltpu.make_async_remote_copy(
        src_ref=src,
        dst_ref=dst,
        send_sem=send,
        recv_sem=recv,
        device_id=where,
        device_id_type=pl.DeviceIdType.MESH,
    )


def push(*args):
    descriptor(*args).start()


def sent(*args):
    descriptor(*args).wait_send()


def arrived(*args):
    descriptor(*args).wait_recv()


def greet(nt, nr, nc, t, r, c):
    barrier = pltpu.get_barrier_semaphore()
    flat = r * nc + c
    for k in range(1, nr * nc):
        other = lax.rem(flat + k, nr * nc)
        pl.semaphore_signal(
            barrier,
            inc=1,
            device_id={"row": other // nc, "col": lax.rem(other, nc)},
            device_id_type=pl.DeviceIdType.MESH,
        )
    for k in range(1, nt):
        pl.semaphore_signal(
            barrier,
            inc=1,
            device_id={"tgt": lax.rem(t + k, nt)},
            device_id_type=pl.DeviceIdType.MESH,
        )


def meet(nt, nr, nc):
    pl.semaphore_wait(pltpu.get_barrier_semaphore(), nr * nc - 1 + nt - 1)


def kernel(
    sizes,
    h_ref,
    mult_ref,
    off_ref,
    pm_ref,
    pb_ref,
    w_ref,
    g_ref,
    dx_out,
    pw_out,
    pbias_out,
    gain_out,
    shift_out,
    ow_out,
    ob_out,
    h,
    g,
    nrm,
    inv,
    no,
    lt,
    lmat,
    rt,
    rown,
    rf,
    wf,
    wp,
    pair,
    rp,
    lsum,
    lp,
    ra,
    rb,
    ms,
    rr,
    la,
    lb,
    side,
    on,
    dw,
    dwb,
    obacc,
    a1,
    a3,
    a5,
    grads,
    pwt,
    vec,
    acc,
    sb,
    b1,
    b2,
    b3,
    b4,
    local_sem,
    gl_send,
    gl_recv,
    gl2_send,
    gl2_recv,
    gr1_send,
    gr1_recv,
    gr_send,
    gr_recv,
    gr2_send,
    gr2_recv,
    sr1_send,
    sr1_recv,
    sr2_send,
    sr2_recv,
    sr3_send,
    sr3_recv,
    sl1_send,
    sl1_recv,
    sl2_send,
    sl2_recv,
    a_part_send,
    a_part_recv,
    a_tgt_send,
    a_tgt_recv,
    a_whole_send,
    a_whole_recv,
    b_row_send,
    b_row_recv,
    b_col_send,
    b_col_recv,
    b_tgt_send,
    b_tgt_recv,
    b_row2_send,
    b_row2_recv,
):
    nt, nr, nc, rl = sizes
    rpc = nr // nc
    nx = nr // rpc
    assert nx == nc == 4 and rpc == 2
    ni, nj = rl * nc, rl * nr
    lrows = rl * CH
    t, r, c = axis_places()
    home = lax.div(r, rpc)
    z, x_at, q_at = lax.div(r, nx), lax.rem(r, nx), lax.rem(r, rpc)
    c_half, c_odd = lax.div(c, 2), lax.rem(c, 2)
    side_x = lax.rem(x_at + jnp.where(lax.rem(x_at, 2) == 1, 1, nx - 1), nx)
    via = jnp.where(c_odd == 1, side_x, x_at)
    own = jnp.logical_and(via == x_at, home == c)
    half, lhalf = CH // 2, lrows // 2

    h_in = pltpu.make_async_copy(h_ref, h, local_sem.at[0])
    h_in.start()
    g_in = pltpu.make_async_copy(g_ref, g, local_sem.at[1])
    g_in.start()
    greet(nt, nr, nc, t, r, c)

    mult = mult_ref[...]
    off = off_ref[...]
    pt = pm_ref[...]
    bias = jnp.broadcast_to(pb_ref[...], (S, 2 * CH)).T

    wf[...] = w_ref[...].astype(F32)

    def reorder(d, _):
        rows = wf[pl.ds(d, CH, stride=CH), :]
        wp[pl.ds(pl.multiple_of(d * CH, CH), CH), :] = rows.astype(BF16)
        return 0

    lax.fori_loop(0, CH, reorder, 0, unroll=4)
    h_in.wait()

    def normalise(k, _):
        rows = pl.ds(pl.multiple_of(k * 128, 128), 128)
        x = h[rows, :].astype(F32)
        centred = x - jnp.mean(x, -1, keepdims=True)
        scale = lax.rsqrt(jnp.mean(centred * centred, -1, keepdims=True) + 1e-05)
        x = centred * scale
        nrm[0, rows, :] = x[:, :128]
        nrm[1, rows, :] = x[:, 128:]
        inv[rows, :] = jnp.broadcast_to(scale, (128, 128))
        return 0

    lax.fori_loop(0, S * rl // 128, normalise, 0, unroll=4)

    def project(k, _):
        at = pl.ds(k, S, stride=rl)
        x = jnp.concatenate([nrm[0, at, :], nrm[1, at, :]], 1)
        row = (x * mult + off).astype(BF16)
        no[pl.ds(pl.multiple_of(k * S, S), S), :] = row
        y = (mm(pt, row, NT_DIMS) + bias).astype(BF16)
        lt[pl.ds(pl.multiple_of(c * lrows + k * CH, CH), CH), :] = y[:CH]
        rf[pl.ds(pl.multiple_of(k * CH, CH), CH), :] = y[CH:].astype(F32)
        return 0

    lax.fori_loop(0, rl, project, 0, unroll=4)

    def turn(d, _):
        rown[d] = rf[pl.ds(d, rl, stride=CH), :].astype(BF16)
        return 0

    lax.fori_loop(0, CH, turn, 0, unroll=4)
    meet(nt, nr, nc)

    def xs(k):
        return lax.rem(x_at + k, nx)

    def cs(k):
        return lax.rem(c + k, nc)

    def to_x(k):
        return {"row": z * nx + xs(1 if k == 0 else nx - 1)}

    def to_c(k):
        return {"col": cs(1 if k == 0 else nc - 1)}

    back_of = (3, 1)

    def left_block(k, part=None):
        at, size = (k * lrows, lrows) if part is None else (k * lrows + part * lhalf, lhalf)
        return lt.at[pl.ds(pl.multiple_of(at, lhalf), size), :]

    def spot(x):
        e = lax.rem(x + nx - 2 * c_odd, nx)
        return lax.div(lax.rem(e + 1, nx), 2), lax.div(e, 2)

    my_q, my_odd = spot(x_at)

    def right_block(x, part):
        q, odd = spot(x)
        return rt.at[part * half : (part + 1) * half, q, :, odd]

    def gather_left(k):
        return left_block(c), left_block(c), gl_send.at[k], gl_recv.at[k], to_c(k)

    def gather_left_in(k):
        at = left_block(cs(back_of[k]))
        return at, at, gl_send.at[k], gl_recv.at[k], to_c(k)

    def relay_left(k):
        at = left_block(cs(back_of[k]), k)
        return at, at, gl2_send.at[k], gl2_recv.at[k], to_c(k)

    def relay_left_in(k):
        at = left_block(cs(2), k)
        return at, at, gl2_send.at[k], gl2_recv.at[k], to_c(k)

    def first_right(k, part):
        rows = slice(part * half, (part + 1) * half)
        to = rt.at[rows, q_at, c_half, c_odd]
        where = {"row": k * nx + via, "col": home}
        return rown.at[rows], to, gr1_send.at[k, part], gr1_recv.at[c_half, part], where

    def first_right_in(k, part):
        rows = slice(part * half, (part + 1) * half)
        to = rt.at[rows, my_q, k, my_odd]
        where = {"row": rpc * c + my_q, "col": 2 * k + my_odd}
        return rown.at[rows], to, gr1_send.at[k, part], gr1_recv.at[k, part], where

    def gather_right(k, part):
        at = right_block(x_at, part)
        return at, at, gr_send.at[k, part], gr_recv.at[k, part], to_x(k)

    def gather_right_in(k, part):
        at = right_block(xs(back_of[k]), part)
        return at, at, gr_send.at[k, part], gr_recv.at[k, part], to_x(k)

    def relay_right(k):
        at = right_block(xs(back_of[k]), k)
        return at, at, gr2_send.at[k], gr2_recv.at[k], to_x(k)

    def relay_right_in(k):
        at = right_block(xs(2), k)
        return at, at, gr2_send.at[k], gr2_recv.at[k], to_x(k)

    def unless(same, act):
        pl.when(jnp.logical_not(jnp.logical_and(own, same)))(act)

    for part in range(2):
        for k in range(rpc):
            unless(z == k, lambda: push(*first_right(k, part)))

    @pl.when(own)
    def _():
        rt[:, q_at, c_half, c_odd] = rown[...]

    for k in range(2):
        push(*gather_left(k))

    g_in.wait()
    obacc[...] = jnp.zeros_like(obacc)

    def back(k, _):
        rows = g[pl.ds(pl.multiple_of(k * 2 * nj, 2 * nj), 2 * nj), :]
        y = mm(wp[...], rows, NT_DIMS).astype(BF16)
        for q in range(2):
            at = pl.ds(pl.multiple_of((2 * k + q) * CH, CH), CH)
            for d in range(CH):
                pair[at, d * nj : (d + 1) * nj] = y[d * CH : (d + 1) * CH, q * nj : (q + 1) * nj]
        obacc[...] += jnp.sum(rows.astype(F32).reshape(2 * nj // 8, 8, CZ), 0)
        return 0

    lax.fori_loop(0, 6 * ni // 32, back, 0, unroll=2)
    for k in range(2):
        arrived(*gather_left_in(k))
        push(*relay_left(k))
    lax.fori_loop(6 * ni // 32, 9 * ni // 32, back, 0, unroll=2)
    for k in range(rpc):
        unless(c_half == k, lambda: arrived(*first_right_in(k, 0)))
    for k in range(2):
        push(*gather_right(k, 0))
    lax.fori_loop(9 * ni // 32, 11 * ni // 32, back, 0, unroll=2)
    for k in range(rpc):
        unless(c_half == k, lambda: arrived(*first_right_in(k, 1)))
    for k in range(2):
        push(*gather_right(1 - k, 1))
    lax.fori_loop(11 * ni // 32, ni // 2, back, 0, unroll=2)
    arrived(*gather_right_in(0, 0))
    push(*relay_right(0))

    for k in range(2):
        arrived(*relay_left_in(k))
    def flip(k, _):
        at = pl.ds(pl.multiple_of(k * 128, 128), 128)
        lmat[:, at] = lt[at, :].T
        return 0

    lax.fori_loop(0, ni * CH // 128, flip, 0, unroll=4)

    def right_step(k, _):
        lanes = pl.ds(pl.multiple_of(k * 8 * nj, 8 * nj), 8 * nj)
        y = mm(lmat[...], pair[:, lanes]).T
        rp[pl.ds(8 * k, 8)] = y.reshape(8, 2, 2, 2, rl, S).astype(BF16)
        return 0

    def right_sum(x, part):
        q, odd = spot(x)
        return rp.at[part * half : (part + 1) * half, q, :, odd]

    def far_right(k):
        return right_sum(xs(2), k), ra.at[k], sr1_send.at[k], sr1_recv.at[k], to_x(k)

    def near_right(k, part):
        at = right_sum(xs(1 if k == 0 else 3), part)
        to = rb.at[k, part * half : (part + 1) * half]
        return at, to, sr2_send.at[k, part], sr2_recv.at[k, part], to_x(k)

    def scatter_right(k):
        where = {"row": rpc * c + my_q, "col": 2 * k + my_odd}
        return ms.at[k], rr.at[z], sr3_send.at[k], sr3_recv.at[z], where

    def scatter_right_in(k):
        where = {"row": k * nx + via, "col": home}
        return ms.at[k], rr.at[k], sr3_send.at[k], sr3_recv.at[k], where

    lax.fori_loop(0, CH // 16, right_step, 0)
    push(*far_right(0))
    push(*near_right(1, 0))
    arrived(*gather_right_in(1, 1))
    push(*relay_right(1))
    lax.fori_loop(CH // 16, CH // 8, right_step, 0)
    push(*far_right(1))
    push(*near_right(0, 1))

    arrived(*gather_right_in(1, 0))
    arrived(*relay_right_in(0))

    def left_rows(k):
        return pl.ds(pl.multiple_of(k * lrows, lrows), lrows)

    def far_left(k):
        at = lp.at[cs(2), k * lhalf : (k + 1) * lhalf]
        return at, la.at[k], sl1_send.at[k], sl1_recv.at[k], to_c(k)

    def near_left(k):
        at = lp.at[cs(1 if k == 0 else 3)]
        return at, lb.at[k], sl2_send.at[k], sl2_recv.at[k], to_c(k)

    def left_first(k, _):
        lsum[k] = mm(pair[left_rows(k), : half * nj], rt[:half].reshape(half * nj, S))
        return 0

    lax.fori_loop(0, nc, left_first, 0)
    for k in range(2):
        arrived(*far_right(k))
        at = right_sum(xs(1 if k == 0 else 3), k)
        at[...] = (at[...].astype(F32) + ra[k].astype(F32)).astype(BF16)
        push(*near_right(k, k))
    arrived(*gather_right_in(0, 1))
    arrived(*relay_right_in(1))

    def left_step(k, _):
        more = mm(pair[left_rows(k), half * nj :], rt[half:].reshape(half * nj, S))
        lp[k] = (lsum[k] + more).astype(BF16)
        return 0

    left_step(cs(2), 0)
    for k in range(2):
        push(*far_left(k))
    left_step(cs(1), 0)
    left_step(cs(3), 0)
    for k in range(2):
        arrived(*far_left(k))
    for k in range(2):
        at = lp.at[cs(1 if k == 0 else 3), k * lhalf : (k + 1) * lhalf]
        at[...] = (at[...].astype(F32) + la[k].astype(F32)).astype(BF16)
        push(*near_left(k))
    left_step(c, 0)

    dw[...] = jnp.zeros_like(dw)

    def weigh(k, _):
        rows = lt[pl.ds(pl.multiple_of(k * 8 * CH, 8 * CH), 8 * CH), :]
        for v in range(8):
            part = rt[v * 4 : (v + 1) * 4].reshape(4 * nj, S)
            y = mm(rows, part, NT_DIMS).astype(BF16)
            for q in range(8):
                for d in range(4):
                    on[(v * 4 + d) * CH : (v * 4 + d + 1) * CH, q * nj : (q + 1) * nj] = y[
                        q * CH : (q + 1) * CH, d * nj : (d + 1) * nj
                    ]
        dw[...] += mm(on[...], g[pl.ds(pl.multiple_of(k * 8 * nj, 8 * nj), 8 * nj), :])
        return 0

    lax.fori_loop(0, ni // 32, weigh, 0)
    for k in range(2):
        for part in range(2):
            arrived(*near_right(k, part))
    for k in range(rpc):
        total = rp[:, my_q, k, my_odd].astype(F32)
        total += rb[0, :, k].astype(F32)
        total += rb[1, :, k].astype(F32)
        ms[k] = total.astype(BF16)
    for k in range(rpc):
        unless(c_half == k, lambda: push(*scatter_right(k)))

    @pl.when(own)
    def _():
        rr[z] = ms[c_half]

    lax.fori_loop(ni // 32, ni // 8, weigh, 0)

    group = nr * nc
    flat = r * nc + c

    def member(k):
        f = lax.rem(flat + k, group)
        return f, {"row": lax.div(f, nc), "col": lax.rem(f, nc)}

    def a_part(k):
        f, where = member(k)
        src = dwb.at[pl.ds(pl.multiple_of(f * CH, CH), CH), :]
        return src, a1.at[flat], a_part_send.at[k], a_part_recv.at[flat], where

    def a_part_in(k):
        f, where = member(k)
        src = dwb.at[pl.ds(pl.multiple_of(flat * CH, CH), CH), :]
        return src, a1.at[f], a_part_send.at[k], a_part_recv.at[f], where

    def a_whole(k):
        _, where = member(k)
        return a5.at[flat], a5.at[flat], a_whole_send.at[k], a_whole_recv.at[flat], where

    def a_whole_in(k):
        f, where = member(k)
        return a5.at[f], a5.at[f], a_whole_send.at[k], a_whole_recv.at[f], where

    def every(act, copy):
        def step(k, _):
            act(*copy(k))
            return 0

        lax.fori_loop(1, group, step, 0)

    dwb[...] = dw[...].astype(BF16)
    every(push, a_part)
    a1[flat] = dwb[pl.ds(pl.multiple_of(flat * CH, CH), CH), :]

    for k in range(2):
        arrived(*near_left(k))
    for k in range(rpc):
        unless(z == k, lambda: arrived(*scatter_right_in(k)))

    def sum_left(k, _):
        at = pl.ds(pl.multiple_of(k * 128, 128), 128)
        total = lp[c, at, :].astype(F32)
        for q in range(2):
            total += lb[q, at, :].astype(F32)
        side[at, :] = total * (1.0 / S)
        return 0

    lax.fori_loop(0, lrows // 128, sum_left, 0, unroll=4)

    def sum_right(k, _):
        at = pl.ds(k * 8, 8)
        total = rr[0, at].astype(F32)
        for q in range(1, rpc):
            total += rr[q, at].astype(F32)
        to = pl.ds(pl.multiple_of(lrows + k * 8 * rl, 8 * rl), 8 * rl)
        side[to, :] = total.reshape(8 * rl, S) * (1.0 / S)
        return 0

    lax.fori_loop(0, CH // 8, sum_right, 0, unroll=4)

    pwt[...] = jnp.zeros_like(pwt)
    acc[...] = jnp.zeros_like(acc)

    def finish(k, _):
        left = side[pl.ds(pl.multiple_of(k * CH, CH), CH), :]
        right = side[pl.ds(lrows + k, CH, stride=rl), :]
        both = jnp.concatenate([left, right], 0)
        rounded = both.astype(BF16)
        turned = both.T
        acc[:, 2 * CM : 2 * CM + 2 * CH] += jnp.sum(turned.reshape(S // 8, 8, 2 * CH), 0)
        grad = mm(turned.astype(BF16), pt)
        grads[pl.ds(pl.multiple_of(k * S, S), S), :] = grad
        pwt[...] += mm(rounded, no[pl.ds(pl.multiple_of(k * S, S), S), :])
        at = pl.ds(k, S, stride=rl)
        x = jnp.concatenate([nrm[0, at, :], nrm[1, at, :]], 1)
        acc[:, :CM] += jnp.sum((grad * x).reshape(S // 8, 8, CM), 0)
        acc[:, CM : 2 * CM] += jnp.sum(grad.reshape(S // 8, 8, CM), 0)
        return 0

    lax.fori_loop(0, rl, finish, 0, unroll=4)

    pr = 2 * 2 * CH // nr
    vr = 8 // nr
    vec[...] = jnp.zeros_like(vec)
    small = jnp.sum(acc[...], 0, keepdims=True)
    vec[0:1, : 2 * CH] = small[:, 2 * CM : 2 * CM + 2 * CH]
    for k in range(4):
        vec[1 + k : 2 + k, :] = small[:, k * 128 : (k + 1) * 128]
    vec[5:6, :] = jnp.sum(obacc[...], 0, keepdims=True)
    weights = pwt[...]
    stacked = jnp.concatenate([weights[:, :128], weights[:, 128:]], 0)
    sb[...] = jnp.zeros_like(sb)
    for q in range(nr):
        sb[q, :pr, :] = stacked[q * pr : (q + 1) * pr]
        sb[q, pr : pr + vr, :] = vec[q * vr : (q + 1) * vr, :]

    def b_row(k):
        q = lax.rem(r + k, nr)
        return sb.at[q], b1.at[r], b_row_send.at[k], b_row_recv.at[r], {"row": q}

    def b_row_in(k):
        q = lax.rem(r + k, nr)
        return sb.at[q], b1.at[q], b_row_send.at[k], b_row_recv.at[q], {"row": q}

    for k in range(1, nr):
        push(*b_row(k))
    b1[r] = sb[r]

    every(arrived, a_part_in)
    total = a1[0].astype(F32)
    for q in range(1, group):
        total += a1[q].astype(F32)
    a3[t] = total

    def a_tgt(k):
        q = lax.rem(t + k, nt)
        return a3.at[t], a3.at[t], a_tgt_send.at[k], a_tgt_recv.at[t], {"tgt": q}

    def a_tgt_in(k):
        q = lax.rem(t + k, nt)
        return a3.at[q], a3.at[q], a_tgt_send.at[k], a_tgt_recv.at[q], {"tgt": q}

    for k in range(1, nt):
        push(*a_tgt(k))

    def descend(k, _):
        grad = grads[pl.ds(pl.multiple_of(k * S, S), S), :]
        at = pl.ds(k, S, stride=rl)
        x = jnp.concatenate([nrm[0, at, :], nrm[1, at, :]], 1)
        scale = inv[at, :]
        scaled = grad * mult
        dx = scaled - jnp.mean(scaled, -1, keepdims=True) - x * jnp.mean(scaled * x, -1, keepdims=True)
        nrm[0, at, :] = dx[:, :128] * scale
        nrm[1, at, :] = dx[:, 128:] * scale
        return 0

    lax.fori_loop(0, rl // 2, descend, 0, unroll=4)

    for k in range(1, nr):
        arrived(*b_row_in(k))
    total = b1[0]
    for q in range(1, nr):
        total += b1[q]
    b2[c] = total

    def b_col(k):
        q = lax.rem(c + k, nc)
        return b2.at[c], b2.at[c], b_col_send.at[k], b_col_recv.at[c], {"col": q}

    def b_col_in(k):
        q = lax.rem(c + k, nc)
        return b2.at[q], b2.at[q], b_col_send.at[k], b_col_recv.at[q], {"col": q}

    for k in range(1, nc):
        push(*b_col(k))

    lax.fori_loop(rl // 2, rl, descend, 0, unroll=4)

    def emit(k, _):
        rows = pl.ds(pl.multiple_of(k * 128, 128), 128)
        h[rows, :128] = nrm[0, rows, :].astype(BF16)
        h[rows, 128:] = nrm[1, rows, :].astype(BF16)
        return 0

    lax.fori_loop(0, S * rl // 128, emit, 0, unroll=4)
    dx_copy = pltpu.make_async_copy(h, dx_out, local_sem.at[2])
    dx_copy.start()

    for k in range(1, nt):
        arrived(*a_tgt_in(k))
    total = a3[0]
    for q in range(1, nt):
        total += a3[q]
    a5[flat] = total.astype(BF16)
    every(push, a_whole)

    for k in range(1, nc):
        arrived(*b_col_in(k))
    total = b2[0]
    for q in range(1, nc):
        total += b2[q]
    b3[t] = total

    def b_tgt(k):
        q = lax.rem(t + k, nt)
        return b3.at[t], b3.at[t], b_tgt_send.at[k], b_tgt_recv.at[t], {"tgt": q}

    def b_tgt_in(k):
        q = lax.rem(t + k, nt)
        return b3.at[q], b3.at[q], b_tgt_send.at[k], b_tgt_recv.at[q], {"tgt": q}

    for k in range(1, nt):
        push(*b_tgt(k))

    for k in range(1, nt):
        arrived(*b_tgt_in(k))
    total = b3[0]
    for q in range(1, nt):
        total += b3[q]
    b4[r] = total

    def b_row2(k):
        q = lax.rem(r + k, nr)
        return b4.at[r], b4.at[r], b_row2_send.at[k], b_row2_recv.at[r], {"row": q}

    def b_row2_in(k):
        q = lax.rem(r + k, nr)
        return b4.at[q], b4.at[q], b_row2_send.at[k], b_row2_recv.at[q], {"row": q}

    for k in range(1, nr):
        push(*b_row2(k))

    factor = 1.0 / (nt * nr * nc * rl)
    every(arrived, a_whole_in)

    def place(d, _):
        ow_out[pl.ds(d, CH, stride=CH), :] = a5[d].astype(F32) * (factor / S)
        return 0

    lax.fori_loop(0, CH, place, 0, unroll=4)

    for k in range(2):
        sent(*gather_left(k))
        sent(*relay_left(k))
        sent(*relay_right(k))
        sent(*far_right(k))
        sent(*far_left(k))
        sent(*near_left(k))
        for part in range(2):
            sent(*gather_right(k, part))
            sent(*near_right(k, part))
            unless(z == k, lambda: sent(*first_right(k, part)))
        unless(c_half == k, lambda: sent(*scatter_right(k)))
    every(sent, a_part)
    for k in range(1, nc):
        sent(*b_col(k))
    for k in range(1, nr):
        sent(*b_row(k))
    for k in range(1, nt):
        sent(*a_tgt(k))
        sent(*b_tgt(k))
    dx_copy.wait()
    for k in range(1, nr):
        arrived(*b_row2_in(k))
    whole = b4[:, :pr, :].reshape(4 * CH, 128) * factor
    pw_out[:, :128] = whole[: 2 * CH]
    pw_out[:, 128:] = whole[2 * CH :]
    for q in range(nr):
        vec[q * vr : (q + 1) * vr, :] = b4[q, pr : pr + vr, :] * factor
    pbias_out[...] = vec[0:1, : 2 * CH]
    gain_out[...] = jnp.concatenate([vec[1:2, :], vec[2:3, :]], 1)
    shift_out[...] = jnp.concatenate([vec[3:4, :], vec[4:5, :]], 1)
    ob_out[...] = vec[5:6, :]

    every(sent, a_whole)
    for k in range(1, nr):
        sent(*b_row2(k))


def per_device(
    homolog_activation_matrix,
    standardizer_multiplier,
    standardizer_offset,
    side_mapping_matrices,
    side_mapping_offsets,
    final_channel_matrix,
    residue_couple_cotangent,
):
    nt, nr, nc = axis_sizes()
    rl = homolog_activation_matrix.shape[2]
    ni, nj = rl * nc, rl * nr
    pr = 4 * CH // nr + 8
    vmem = functools.partial(pl.BlockSpec, memory_space=pltpu.VMEM)
    hbm = functools.partial(pl.BlockSpec, memory_space=pl.ANY)

    def sems(*n):
        return [pltpu.SemaphoreType.DMA(n), pltpu.SemaphoreType.DMA(n)]

    results = pl.pallas_call(
        functools.partial(kernel, (nt, nr, nc, rl)),
        out_shape=(
            jax.ShapeDtypeStruct((S * rl, CM), BF16),
            jax.ShapeDtypeStruct((2 * CH, CM), F32),
            jax.ShapeDtypeStruct((1, 2 * CH), F32),
            jax.ShapeDtypeStruct((1, CM), F32),
            jax.ShapeDtypeStruct((1, CM), F32),
            jax.ShapeDtypeStruct((CH * CH, CZ), F32),
            jax.ShapeDtypeStruct((1, CZ), F32),
        ),
        in_specs=[hbm(), vmem(), vmem(), vmem(), vmem(), vmem(), hbm()],
        out_specs=(hbm(), vmem(), vmem(), vmem(), vmem(), vmem(), vmem()),
        scratch_shapes=[
            pltpu.VMEM((S * rl, CM), BF16),
            pltpu.VMEM((ni * nj, CZ), BF16),
            pltpu.VMEM((2, S * rl, 128), F32),
            pltpu.VMEM((S * rl, 128), F32),
            pltpu.VMEM((S * rl, CM), BF16),
            pltpu.VMEM((ni * CH, S), BF16),
            pltpu.VMEM((S, ni * CH), BF16),
            pltpu.VMEM((CH, 2, 2, 2, rl, S), BF16),
            pltpu.VMEM((CH, rl, S), BF16),
            pltpu.VMEM((rl * CH, S), F32),
            pltpu.VMEM((CH * CH, CZ), F32),
            pltpu.VMEM((CH * CH, CZ), BF16),
            pltpu.VMEM((ni * CH, CH * nj), BF16),
            pltpu.VMEM((CH, 2, 2, 2, rl, S), BF16),
            pltpu.VMEM((nc, rl * CH, S), F32),
            pltpu.VMEM((nc, rl * CH, S), BF16),
            pltpu.VMEM((2, CH // 2, 2, rl, S), BF16),
            pltpu.VMEM((2, CH, 2, rl, S), BF16),
            pltpu.VMEM((2, CH, rl, S), BF16),
            pltpu.VMEM((2, CH, rl, S), BF16),
            pltpu.VMEM((2, rl * CH // 2, S), BF16),
            pltpu.VMEM((2, rl * CH, S), BF16),
            pltpu.VMEM((2 * rl * CH, S), F32),
            pltpu.VMEM((CH * CH, 8 * nj), BF16),
            pltpu.VMEM((CH * CH, CZ), F32),
            pltpu.VMEM((CH * CH, CZ), BF16),
            pltpu.VMEM((8, CZ), F32),
            pltpu.VMEM((nr * nc, CH, CZ), BF16),
            pltpu.VMEM((nt, CH, CZ), F32),
            pltpu.VMEM((nr * nc, CH, CZ), BF16),
            pltpu.VMEM((S * rl, CM), F32),
            pltpu.VMEM((2 * CH, CM), F32),
            pltpu.VMEM((8, 128), F32),
            pltpu.VMEM((8, 2 * CM + 128), F32),
            pltpu.VMEM((nr, pr, 128), F32),
            pltpu.VMEM((nr, pr, 128), F32),
            pltpu.VMEM((nc, pr, 128), F32),
            pltpu.VMEM((nt, pr, 128), F32),
            pltpu.VMEM((nr, pr, 128), F32),
            pltpu.SemaphoreType.DMA((3,)),
        ]
        + sems(2)
        + sems(2)
        + 2 * sems(2, 2)
        + sems(2)
        + sems(2)
        + sems(2, 2)
        + 3 * sems(2)
        + sems(nr * nc)
        + sems(nt)
        + sems(nr * nc)
        + sems(nr)
        + sems(nc)
        + sems(nt)
        + sems(nr),
        compiler_params=pltpu.CompilerParams(
            collective_id=0, has_side_effects=True, vmem_limit_bytes=56 * 1024 * 1024
        ),
        cost_estimate=pl.CostEstimate(
            flops=10 * ni * nj * CH * CH * CZ, bytes_accessed=5 * 1024 * 1024, transcendentals=0
        ),
    )(
        homolog_activation_matrix.reshape(S * rl, CM),
        standardizer_multiplier.reshape(1, CM),
        standardizer_offset.reshape(1, CM),
        side_mapping_matrices.T,
        side_mapping_offsets.reshape(1, 2 * CH),
        final_channel_matrix,
        residue_couple_cotangent.reshape(ni * nj, CZ),
    )
    return (
        results[0].reshape(1, S, rl, CM),
        results[1].T,
        results[2].reshape(2 * CH),
        results[3].reshape(CM),
        results[4].reshape(CM),
        results[5],
        results[6].reshape(CZ),
    )


def solution(mesh):
    placed = (
        P("tgt", None, ("row", "col"), None),
        P(),
        P(),
        P(),
        P(),
        P(),
        P("tgt", "row", "col", None),
    )
    return jax.shard_map(
        per_device,
        mesh=mesh,
        in_specs=placed,
        out_specs=(P("tgt", None, ("row", "col"), None), P(), P(), P(), P(), P(), P()),
        check_vma=False,
    )
```

```python
import functools

import jax
import jax.numpy as jnp
from jax import lax
from jax.experimental import pallas as pl
from jax.experimental.pallas import tpu as pltpu
from jax.sharding import PartitionSpec as P

CM = 256
CH = 32
CZ = 128
S = 128
F32 = jnp.float32
BF16 = jnp.bfloat16
NT_DIMS = (((1,), (1,)), ((), ()))
NN_DIMS = (((1,), (0,)), ((), ()))


def mm(a, b, dims=NN_DIMS):
    return lax.dot_general(a, b, dims, preferred_element_type=F32)


def axis_sizes():
    return lax.axis_size("tgt"), lax.axis_size("row"), lax.axis_size("col")


def axis_places():
    return lax.axis_index("tgt"), lax.axis_index("row"), lax.axis_index("col")


def descriptor(src, dst, send, recv, where):
    return pltpu.make_async_remote_copy(
        src_ref=src,
        dst_ref=dst,
        send_sem=send,
        recv_sem=recv,
        device_id=where,
        device_id_type=pl.DeviceIdType.MESH,
    )


def push(*args):
    descriptor(*args).start()


def sent(*args):
    descriptor(*args).wait_send()


def arrived(*args):
    descriptor(*args).wait_recv()


def greet(nt, nr, nc, t, r, c):
    barrier = pltpu.get_barrier_semaphore()
    flat = r * nc + c
    for k in range(1, nr * nc):
        other = lax.rem(flat + k, nr * nc)
        pl.semaphore_signal(
            barrier,
            inc=1,
            device_id={"row": other // nc, "col": lax.rem(other, nc)},
            device_id_type=pl.DeviceIdType.MESH,
        )
    for k in range(1, nt):
        pl.semaphore_signal(
            barrier,
            inc=1,
            device_id={"tgt": lax.rem(t + k, nt)},
            device_id_type=pl.DeviceIdType.MESH,
        )


def meet(nt, nr, nc):
    pl.semaphore_wait(pltpu.get_barrier_semaphore(), nr * nc - 1 + nt - 1)


def kernel(
    sizes,
    h_ref,
    mult_ref,
    off_ref,
    pm_ref,
    pb_ref,
    w_ref,
    g_ref,
    dx_out,
    pw_out,
    pbias_out,
    gain_out,
    shift_out,
    ow_out,
    ob_out,
    h,
    g,
    nrm,
    inv,
    no,
    lt,
    lmat,
    rt,
    rown,
    rf,
    wf,
    wp,
    pair,
    rp,
    lsum,
    lp,
    ra,
    rb,
    ms,
    rr,
    la,
    lb,
    side,
    on,
    dw,
    dwb,
    obacc,
    a1,
    a3,
    a5,
    grads,
    pwt,
    vec,
    acc,
    sb,
    b1,
    b2,
    b3,
    b4,
    local_sem,
    gl_send,
    gl_recv,
    gl2_send,
    gl2_recv,
    gr1_send,
    gr1_recv,
    gr_send,
    gr_recv,
    gr2_send,
    gr2_recv,
    sr1_send,
    sr1_recv,
    sr2_send,
    sr2_recv,
    sr3_send,
    sr3_recv,
    sl1_send,
    sl1_recv,
    sl2_send,
    sl2_recv,
    a_part_send,
    a_part_recv,
    a_tgt_send,
    a_tgt_recv,
    a_whole_send,
    a_whole_recv,
    b_row_send,
    b_row_recv,
    b_col_send,
    b_col_recv,
    b_tgt_send,
    b_tgt_recv,
    b_row2_send,
    b_row2_recv,
):
    nt, nr, nc, rl = sizes
    rpc = nr // nc
    nx = nr // rpc
    assert nx == nc == 4 and rpc == 2
    ni, nj = rl * nc, rl * nr
    lrows = rl * CH
    t, r, c = axis_places()
    home = lax.div(r, rpc)
    z, x_at, q_at = lax.div(r, nx), lax.rem(r, nx), lax.rem(r, rpc)
    c_half, c_odd = lax.div(c, 2), lax.rem(c, 2)
    side_x = lax.rem(x_at + jnp.where(lax.rem(x_at, 2) == 1, 1, nx - 1), nx)
    via = jnp.where(c_odd == 1, side_x, x_at)
    own = jnp.logical_and(via == x_at, home == c)
    half, lhalf = CH // 2, lrows // 2

    h_in = pltpu.make_async_copy(h_ref, h, local_sem.at[0])
    h_in.start()
    g_in = pltpu.make_async_copy(g_ref, g, local_sem.at[1])
    g_in.start()
    greet(nt, nr, nc, t, r, c)

    mult = mult_ref[...]
    off = off_ref[...]
    pt = pm_ref[...]
    bias = jnp.broadcast_to(pb_ref[...], (S, 2 * CH)).T

    h_in.wait()

    def normalise(k, _):
        rows = pl.ds(pl.multiple_of(k * 128, 128), 128)
        x = h[rows, :].astype(F32)
        centred = x - jnp.mean(x, -1, keepdims=True)
        scale = lax.rsqrt(jnp.mean(centred * centred, -1, keepdims=True) + 1e-05)
        x = centred * scale
        nrm[0, rows, :] = x[:, :128]
        nrm[1, rows, :] = x[:, 128:]
        inv[rows, :] = jnp.broadcast_to(scale, (128, 128))
        return 0

    lax.fori_loop(0, S * rl // 128, normalise, 0, unroll=4)

    def project(k, _):
        at = pl.ds(k, S, stride=rl)
        x = jnp.concatenate([nrm[0, at, :], nrm[1, at, :]], 1)
        row = (x * mult + off).astype(BF16)
        no[pl.ds(pl.multiple_of(k * S, S), S), :] = row
        y = (mm(pt, row, NT_DIMS) + bias).astype(BF16)
        lt[pl.ds(pl.multiple_of(c * lrows + k * CH, CH), CH), :] = y[:CH]
        rf[pl.ds(pl.multiple_of(k * CH, CH), CH), :] = y[CH:].astype(F32)
        return 0

    lax.fori_loop(0, rl, project, 0, unroll=4)

    def turn(d, _):
        rown[d] = rf[pl.ds(d, rl, stride=CH), :].astype(BF16)
        return 0

    lax.fori_loop(0, CH, turn, 0, unroll=4)
    meet(nt, nr, nc)

    def xs(k):
        return lax.rem(x_at + k, nx)

    def cs(k):
        return lax.rem(c + k, nc)

    def to_x(k):
        return {"row": z * nx + xs(1 if k == 0 else nx - 1)}

    def to_c(k):
        return {"col": cs(1 if k == 0 else nc - 1)}

    back_of = (3, 1)

    def left_block(k, part=None):
        at, size = (k * lrows, lrows) if part is None else (k * lrows + part * lhalf, lhalf)
        return lt.at[pl.ds(pl.multiple_of(at, lhalf), size), :]

    def spot(x):
        e = lax.rem(x + nx - 2 * c_odd, nx)
        return lax.div(lax.rem(e + 1, nx), 2), lax.div(e, 2)

    my_q, my_odd = spot(x_at)

    def right_block(x, part):
        q, odd = spot(x)
        return rt.at[part * half : (part + 1) * half, q, :, odd]

    def gather_left(k):
        return left_block(c), left_block(c), gl_send.at[k], gl_recv.at[k], to_c(k)

    def gather_left_in(k):
        at = left_block(cs(back_of[k]))
        return at, at, gl_send.at[k], gl_recv.at[k], to_c(k)

    def relay_left(k):
        at = left_block(cs(back_of[k]), k)
        return at, at, gl2_send.at[k], gl2_recv.at[k], to_c(k)

    def relay_left_in(k):
        at = left_block(cs(2), k)
        return at, at, gl2_send.at[k], gl2_recv.at[k], to_c(k)

    def first_right(k, part):
        rows = slice(part * half, (part + 1) * half)
        to = rt.at[rows, q_at, c_half, c_odd]
        where = {"row": k * nx + via, "col": home}
        return rown.at[rows], to, gr1_send.at[k, part], gr1_recv.at[c_half, part], where

    def first_right_in(k, part):
        rows = slice(part * half, (part + 1) * half)
        to = rt.at[rows, my_q, k, my_odd]
        where = {"row": rpc * c + my_q, "col": 2 * k + my_odd}
        return rown.at[rows], to, gr1_send.at[k, part], gr1_recv.at[k, part], where

    def gather_right(k, part):
        at = right_block(x_at, part)
        return at, at, gr_send.at[k, part], gr_recv.at[k, part], to_x(k)

    def gather_right_in(k, part):
        at = right_block(xs(back_of[k]), part)
        return at, at, gr_send.at[k, part], gr_recv.at[k, part], to_x(k)

    def relay_right(k):
        at = right_block(xs(back_of[k]), k)
        return at, at, gr2_send.at[k], gr2_recv.at[k], to_x(k)

    def relay_right_in(k):
        at = right_block(xs(2), k)
        return at, at, gr2_send.at[k], gr2_recv.at[k], to_x(k)

    def unless(same, act):
        pl.when(jnp.logical_not(jnp.logical_and(own, same)))(act)

    for part in range(2):
        for k in range(rpc):
            unless(z == k, lambda: push(*first_right(k, part)))

    @pl.when(own)
    def _():
        rt[:, q_at, c_half, c_odd] = rown[...]

    for k in range(2):
        push(*gather_left(k))

    wf[...] = w_ref[...].astype(F32)

    def reorder(d, _):
        rows = wf[pl.ds(d, CH, stride=CH), :]
        wp[pl.ds(pl.multiple_of(d * CH, CH), CH), :] = rows.astype(BF16)
        return 0

    lax.fori_loop(0, CH, reorder, 0, unroll=4)
    g_in.wait()
    obacc[...] = jnp.zeros_like(obacc)

    def back(k, _):
        rows = g[pl.ds(pl.multiple_of(k * 2 * nj, 2 * nj), 2 * nj), :]
        y = mm(wp[...], rows, NT_DIMS).astype(BF16)
        for q in range(2):
            at = pl.ds(pl.multiple_of((2 * k + q) * CH, CH), CH)
            for d in range(CH):
                pair[at, d * nj : (d + 1) * nj] = y[d * CH : (d + 1) * CH, q * nj : (q + 1) * nj]
        obacc[...] += jnp.sum(rows.astype(F32).reshape(2 * nj // 8, 8, CZ), 0)
        return 0

    lax.fori_loop(0, 6 * ni // 32, back, 0, unroll=2)
    for k in range(2):
        arrived(*gather_left_in(k))
        push(*relay_left(k))
    lax.fori_loop(6 * ni // 32, 9 * ni // 32, back, 0, unroll=2)
    for k in range(rpc):
        unless(c_half == k, lambda: arrived(*first_right_in(k, 0)))
    for k in range(2):
        push(*gather_right(k, 0))
    lax.fori_loop(9 * ni // 32, 11 * ni // 32, back, 0, unroll=2)
    for k in range(rpc):
        unless(c_half == k, lambda: arrived(*first_right_in(k, 1)))
    for k in range(2):
        push(*gather_right(1 - k, 1))
    lax.fori_loop(11 * ni // 32, ni // 2, back, 0, unroll=2)
    arrived(*gather_right_in(0, 0))
    push(*relay_right(0))

    for k in range(2):
        arrived(*relay_left_in(k))
    def flip(k, _):
        at = pl.ds(pl.multiple_of(k * 128, 128), 128)
        lmat[:, at] = lt[at, :].T
        return 0

    lax.fori_loop(0, ni * CH // 128, flip, 0, unroll=4)

    def right_step(k, _):
        lanes = pl.ds(pl.multiple_of(k * 8 * nj, 8 * nj), 8 * nj)
        y = mm(lmat[...], pair[:, lanes]).T
        rp[pl.ds(8 * k, 8)] = y.reshape(8, 2, 2, 2, rl, S).astype(BF16)
        return 0

    def right_sum(x, part):
        q, odd = spot(x)
        return rp.at[part * half : (part + 1) * half, q, :, odd]

    def far_right(k):
        return right_sum(xs(2), k), ra.at[k], sr1_send.at[k], sr1_recv.at[k], to_x(k)

    def near_right(k, part):
        at = right_sum(xs(1 if k == 0 else 3), part)
        to = rb.at[k, part * half : (part + 1) * half]
        return at, to, sr2_send.at[k, part], sr2_recv.at[k, part], to_x(k)

    def scatter_right(k):
        where = {"row": rpc * c + my_q, "col": 2 * k + my_odd}
        return ms.at[k], rr.at[z], sr3_send.at[k], sr3_recv.at[z], where

    def scatter_right_in(k):
        where = {"row": k * nx + via, "col": home}
        return ms.at[k], rr.at[k], sr3_send.at[k], sr3_recv.at[k], where

    lax.fori_loop(0, CH // 16, right_step, 0)
    push(*far_right(0))
    push(*near_right(1, 0))
    arrived(*gather_right_in(1, 1))
    push(*relay_right(1))
    lax.fori_loop(CH // 16, CH // 8, right_step, 0)
    push(*far_right(1))
    push(*near_right(0, 1))

    arrived(*gather_right_in(1, 0))
    arrived(*relay_right_in(0))

    def left_rows(k):
        return pl.ds(pl.multiple_of(k * lrows, lrows), lrows)

    def far_left(k):
        at = lp.at[cs(2), k * lhalf : (k + 1) * lhalf]
        return at, la.at[k], sl1_send.at[k], sl1_recv.at[k], to_c(k)

    def near_left(k):
        at = lp.at[cs(1 if k == 0 else 3)]
        return at, lb.at[k], sl2_send.at[k], sl2_recv.at[k], to_c(k)

    def left_first(k, _):
        lsum[k] = mm(pair[left_rows(k), : half * nj], rt[:half].reshape(half * nj, S))
        return 0

    lax.fori_loop(0, nc, left_first, 0)
    for k in range(2):
        arrived(*far_right(k))
        at = right_sum(xs(1 if k == 0 else 3), k)
        at[...] = (at[...].astype(F32) + ra[k].astype(F32)).astype(BF16)
        push(*near_right(k, k))
    arrived(*gather_right_in(0, 1))
    arrived(*relay_right_in(1))

    def left_step(k, _):
        more = mm(pair[left_rows(k), half * nj :], rt[half:].reshape(half * nj, S))
        lp[k] = (lsum[k] + more).astype(BF16)
        return 0

    left_step(cs(2), 0)
    for k in range(2):
        push(*far_left(k))
    left_step(cs(1), 0)
    left_step(cs(3), 0)
    for k in range(2):
        arrived(*far_left(k))
    for k in range(2):
        at = lp.at[cs(1 if k == 0 else 3), k * lhalf : (k + 1) * lhalf]
        at[...] = (at[...].astype(F32) + la[k].astype(F32)).astype(BF16)
        push(*near_left(k))
    left_step(c, 0)

    dw[...] = jnp.zeros_like(dw)

    def weigh(k, _):
        rows = lt[pl.ds(pl.multiple_of(k * 8 * CH, 8 * CH), 8 * CH), :]
        for v in range(8):
            part = rt[v * 4 : (v + 1) * 4].reshape(4 * nj, S)
            y = mm(rows, part, NT_DIMS).astype(BF16)
            for q in range(8):
                for d in range(4):
                    on[(v * 4 + d) * CH : (v * 4 + d + 1) * CH, q * nj : (q + 1) * nj] = y[
                        q * CH : (q + 1) * CH, d * nj : (d + 1) * nj
                    ]
        dw[...] += mm(on[...], g[pl.ds(pl.multiple_of(k * 8 * nj, 8 * nj), 8 * nj), :])
        return 0

    lax.fori_loop(0, ni // 32, weigh, 0)
    for k in range(2):
        for part in range(2):
            arrived(*near_right(k, part))
    for k in range(rpc):
        total = rp[:, my_q, k, my_odd].astype(F32)
        total += rb[0, :, k].astype(F32)
        total += rb[1, :, k].astype(F32)
        ms[k] = total.astype(BF16)
    for k in range(rpc):
        unless(c_half == k, lambda: push(*scatter_right(k)))

    @pl.when(own)
    def _():
        rr[z] = ms[c_half]

    lax.fori_loop(ni // 32, ni // 8, weigh, 0)

    group = nr * nc
    flat = r * nc + c

    def member(k):
        f = lax.rem(flat + k, group)
        return f, {"row": lax.div(f, nc), "col": lax.rem(f, nc)}

    def a_part(k):
        f, where = member(k)
        src = dwb.at[pl.ds(pl.multiple_of(f * CH, CH), CH), :]
        return src, a1.at[flat], a_part_send.at[k], a_part_recv.at[flat], where

    def a_part_in(k):
        f, where = member(k)
        src = dwb.at[pl.ds(pl.multiple_of(flat * CH, CH), CH), :]
        return src, a1.at[f], a_part_send.at[k], a_part_recv.at[f], where

    def a_whole(k):
        _, where = member(k)
        return a5.at[flat], a5.at[flat], a_whole_send.at[k], a_whole_recv.at[flat], where

    def a_whole_in(k):
        f, where = member(k)
        return a5.at[f], a5.at[f], a_whole_send.at[k], a_whole_recv.at[f], where

    def every(act, copy):
        def step(k, _):
            act(*copy(k))
            return 0

        lax.fori_loop(1, group, step, 0)

    dwb[...] = dw[...].astype(BF16)
    every(push, a_part)
    a1[flat] = dwb[pl.ds(pl.multiple_of(flat * CH, CH), CH), :]

    for k in range(2):
        arrived(*near_left(k))
    def sum_left(k, _):
        at = pl.ds(pl.multiple_of(k * 128, 128), 128)
        total = lp[c, at, :].astype(F32)
        for q in range(2):
            total += lb[q, at, :].astype(F32)
        side[at, :] = total * (1.0 / S)
        return 0

    lax.fori_loop(0, lrows // 128, sum_left, 0, unroll=4)

    for k in range(rpc):
        unless(z == k, lambda: arrived(*scatter_right_in(k)))

    def sum_right(k, _):
        at = pl.ds(k * 8, 8)
        total = rr[0, at].astype(F32)
        for q in range(1, rpc):
            total += rr[q, at].astype(F32)
        to = pl.ds(pl.multiple_of(lrows + k * 8 * rl, 8 * rl), 8 * rl)
        side[to, :] = total.reshape(8 * rl, S) * (1.0 / S)
        return 0

    lax.fori_loop(0, CH // 8, sum_right, 0, unroll=4)

    pwt[...] = jnp.zeros_like(pwt)
    acc[...] = jnp.zeros_like(acc)

    def finish(k, _):
        left = side[pl.ds(pl.multiple_of(k * CH, CH), CH), :]
        right = side[pl.ds(lrows + k, CH, stride=rl), :]
        both = jnp.concatenate([left, right], 0)
        rounded = both.astype(BF16)
        turned = both.T
        acc[:, 2 * CM : 2 * CM + 2 * CH] += jnp.sum(turned.reshape(S // 8, 8, 2 * CH), 0)
        grad = mm(turned.astype(BF16), pt)
        grads[pl.ds(pl.multiple_of(k * S, S), S), :] = grad
        pwt[...] += mm(rounded, no[pl.ds(pl.multiple_of(k * S, S), S), :])
        at = pl.ds(k, S, stride=rl)
        x = jnp.concatenate([nrm[0, at, :], nrm[1, at, :]], 1)
        acc[:, :CM] += jnp.sum((grad * x).reshape(S // 8, 8, CM), 0)
        acc[:, CM : 2 * CM] += jnp.sum(grad.reshape(S // 8, 8, CM), 0)
        return 0

    lax.fori_loop(0, rl, finish, 0, unroll=4)

    pr = 2 * 2 * CH // nr
    vr = 8 // nr
    vec[...] = jnp.zeros_like(vec)
    small = jnp.sum(acc[...], 0, keepdims=True)
    vec[0:1, : 2 * CH] = small[:, 2 * CM : 2 * CM + 2 * CH]
    for k in range(4):
        vec[1 + k : 2 + k, :] = small[:, k * 128 : (k + 1) * 128]
    vec[5:6, :] = jnp.sum(obacc[...], 0, keepdims=True)
    weights = pwt[...]
    stacked = jnp.concatenate([weights[:, :128], weights[:, 128:]], 0)
    sb[...] = jnp.zeros_like(sb)
    for q in range(nr):
        sb[q, :pr, :] = stacked[q * pr : (q + 1) * pr]
        sb[q, pr : pr + vr, :] = vec[q * vr : (q + 1) * vr, :]

    def b_row(k):
        q = lax.rem(r + k, nr)
        return sb.at[q], b1.at[r], b_row_send.at[k], b_row_recv.at[r], {"row": q}

    def b_row_in(k):
        q = lax.rem(r + k, nr)
        return sb.at[q], b1.at[q], b_row_send.at[k], b_row_recv.at[q], {"row": q}

    for k in range(1, nr):
        push(*b_row(k))
    b1[r] = sb[r]

    def descend(k, _):
        grad = grads[pl.ds(pl.multiple_of(k * S, S), S), :]
        at = pl.ds(k, S, stride=rl)
        x = jnp.concatenate([nrm[0, at, :], nrm[1, at, :]], 1)
        scale = inv[at, :]
        scaled = grad * mult
        dx = scaled - jnp.mean(scaled, -1, keepdims=True) - x * jnp.mean(scaled * x, -1, keepdims=True)
        nrm[0, at, :] = dx[:, :128] * scale
        nrm[1, at, :] = dx[:, 128:] * scale
        return 0

    lax.fori_loop(0, rl // 2, descend, 0, unroll=4)

    every(arrived, a_part_in)
    total = a1[0].astype(F32)
    for q in range(1, group):
        total += a1[q].astype(F32)
    a3[t] = total

    def a_tgt(k):
        q = lax.rem(t + k, nt)
        return a3.at[t], a3.at[t], a_tgt_send.at[k], a_tgt_recv.at[t], {"tgt": q}

    def a_tgt_in(k):
        q = lax.rem(t + k, nt)
        return a3.at[q], a3.at[q], a_tgt_send.at[k], a_tgt_recv.at[q], {"tgt": q}

    for k in range(1, nt):
        push(*a_tgt(k))


    for k in range(1, nr):
        arrived(*b_row_in(k))
    total = b1[0]
    for q in range(1, nr):
        total += b1[q]
    b2[c] = total

    def b_col(k):
        q = lax.rem(c + k, nc)
        return b2.at[c], b2.at[c], b_col_send.at[k], b_col_recv.at[c], {"col": q}

    def b_col_in(k):
        q = lax.rem(c + k, nc)
        return b2.at[q], b2.at[q], b_col_send.at[k], b_col_recv.at[q], {"col": q}

    for k in range(1, nc):
        push(*b_col(k))

    lax.fori_loop(rl // 2, rl, descend, 0, unroll=4)

    def emit(k, _):
        rows = pl.ds(pl.multiple_of(k * 128, 128), 128)
        h[rows, :128] = nrm[0, rows, :].astype(BF16)
        h[rows, 128:] = nrm[1, rows, :].astype(BF16)
        return 0

    lax.fori_loop(0, S * rl // 128, emit, 0, unroll=4)
    dx_copy = pltpu.make_async_copy(h, dx_out, local_sem.at[2])
    dx_copy.start()

    for k in range(1, nc):
        arrived(*b_col_in(k))
    total = b2[0]
    for q in range(1, nc):
        total += b2[q]
    b3[t] = total

    def b_tgt(k):
        q = lax.rem(t + k, nt)
        return b3.at[t], b3.at[t], b_tgt_send.at[k], b_tgt_recv.at[t], {"tgt": q}

    def b_tgt_in(k):
        q = lax.rem(t + k, nt)
        return b3.at[q], b3.at[q], b_tgt_send.at[k], b_tgt_recv.at[q], {"tgt": q}

    for k in range(1, nt):
        push(*b_tgt(k))

    for k in range(1, nt):
        arrived(*a_tgt_in(k))
    total = a3[0]
    for q in range(1, nt):
        total += a3[q]
    a5[flat] = total.astype(BF16)
    every(push, a_whole)

    for k in range(1, nt):
        arrived(*b_tgt_in(k))
    total = b3[0]
    for q in range(1, nt):
        total += b3[q]
    b4[r] = total

    def b_row2(k):
        q = lax.rem(r + k, nr)
        return b4.at[r], b4.at[r], b_row2_send.at[k], b_row2_recv.at[r], {"row": q}

    def b_row2_in(k):
        q = lax.rem(r + k, nr)
        return b4.at[q], b4.at[q], b_row2_send.at[k], b_row2_recv.at[q], {"row": q}

    for k in range(1, nr):
        push(*b_row2(k))

    factor = 1.0 / (nt * nr * nc * rl)
    every(arrived, a_whole_in)

    def place(d, _):
        ow_out[pl.ds(d, CH, stride=CH), :] = a5[d].astype(F32) * (factor / S)
        return 0

    lax.fori_loop(0, CH, place, 0, unroll=4)

    for k in range(2):
        sent(*gather_left(k))
        sent(*relay_left(k))
        sent(*relay_right(k))
        sent(*far_right(k))
        sent(*far_left(k))
        sent(*near_left(k))
        for part in range(2):
            sent(*gather_right(k, part))
            sent(*near_right(k, part))
            unless(z == k, lambda: sent(*first_right(k, part)))
        unless(c_half == k, lambda: sent(*scatter_right(k)))
    every(sent, a_part)
    for k in range(1, nc):
        sent(*b_col(k))
    for k in range(1, nr):
        sent(*b_row(k))
    for k in range(1, nt):
        sent(*a_tgt(k))
        sent(*b_tgt(k))
    dx_copy.wait()
    for k in range(1, nr):
        arrived(*b_row2_in(k))
    whole = b4[:, :pr, :].reshape(4 * CH, 128) * factor
    pw_out[:, :128] = whole[: 2 * CH]
    pw_out[:, 128:] = whole[2 * CH :]
    for q in range(nr):
        vec[q * vr : (q + 1) * vr, :] = b4[q, pr : pr + vr, :] * factor
    pbias_out[...] = vec[0:1, : 2 * CH]
    gain_out[...] = jnp.concatenate([vec[1:2, :], vec[2:3, :]], 1)
    shift_out[...] = jnp.concatenate([vec[3:4, :], vec[4:5, :]], 1)
    ob_out[...] = vec[5:6, :]

    every(sent, a_whole)
    for k in range(1, nr):
        sent(*b_row2(k))


def per_device(
    homolog_activation_matrix,
    standardizer_multiplier,
    standardizer_offset,
    side_mapping_matrices,
    side_mapping_offsets,
    final_channel_matrix,
    residue_couple_cotangent,
):
    nt, nr, nc = axis_sizes()
    rl = homolog_activation_matrix.shape[2]
    ni, nj = rl * nc, rl * nr
    pr = 4 * CH // nr + 8
    vmem = functools.partial(pl.BlockSpec, memory_space=pltpu.VMEM)
    hbm = functools.partial(pl.BlockSpec, memory_space=pl.ANY)

    def sems(*n):
        return [pltpu.SemaphoreType.DMA(n), pltpu.SemaphoreType.DMA(n)]

    results = pl.pallas_call(
        functools.partial(kernel, (nt, nr, nc, rl)),
        out_shape=(
            jax.ShapeDtypeStruct((S * rl, CM), BF16),
            jax.ShapeDtypeStruct((2 * CH, CM), F32),
            jax.ShapeDtypeStruct((1, 2 * CH), F32),
            jax.ShapeDtypeStruct((1, CM), F32),
            jax.ShapeDtypeStruct((1, CM), F32),
            jax.ShapeDtypeStruct((CH * CH, CZ), F32),
            jax.ShapeDtypeStruct((1, CZ), F32),
        ),
        in_specs=[hbm(), vmem(), vmem(), vmem(), vmem(), vmem(), hbm()],
        out_specs=(hbm(), vmem(), vmem(), vmem(), vmem(), vmem(), vmem()),
        scratch_shapes=[
            pltpu.VMEM((S * rl, CM), BF16),
            pltpu.VMEM((ni * nj, CZ), BF16),
            pltpu.VMEM((2, S * rl, 128), F32),
            pltpu.VMEM((S * rl, 128), F32),
            pltpu.VMEM((S * rl, CM), BF16),
            pltpu.VMEM((ni * CH, S), BF16),
            pltpu.VMEM((S, ni * CH), BF16),
            pltpu.VMEM((CH, 2, 2, 2, rl, S), BF16),
            pltpu.VMEM((CH, rl, S), BF16),
            pltpu.VMEM((rl * CH, S), F32),
            pltpu.VMEM((CH * CH, CZ), F32),
            pltpu.VMEM((CH * CH, CZ), BF16),
            pltpu.VMEM((ni * CH, CH * nj), BF16),
            pltpu.VMEM((CH, 2, 2, 2, rl, S), BF16),
            pltpu.VMEM((nc, rl * CH, S), F32),
            pltpu.VMEM((nc, rl * CH, S), BF16),
            pltpu.VMEM((2, CH // 2, 2, rl, S), BF16),
            pltpu.VMEM((2, CH, 2, rl, S), BF16),
            pltpu.VMEM((2, CH, rl, S), BF16),
            pltpu.VMEM((2, CH, rl, S), BF16),
            pltpu.VMEM((2, rl * CH // 2, S), BF16),
            pltpu.VMEM((2, rl * CH, S), BF16),
            pltpu.VMEM((2 * rl * CH, S), F32),
            pltpu.VMEM((CH * CH, 8 * nj), BF16),
            pltpu.VMEM((CH * CH, CZ), F32),
            pltpu.VMEM((CH * CH, CZ), BF16),
            pltpu.VMEM((8, CZ), F32),
            pltpu.VMEM((nr * nc, CH, CZ), BF16),
            pltpu.VMEM((nt, CH, CZ), F32),
            pltpu.VMEM((nr * nc, CH, CZ), BF16),
            pltpu.VMEM((S * rl, CM), F32),
            pltpu.VMEM((2 * CH, CM), F32),
            pltpu.VMEM((8, 128), F32),
            pltpu.VMEM((8, 2 * CM + 128), F32),
            pltpu.VMEM((nr, pr, 128), F32),
            pltpu.VMEM((nr, pr, 128), F32),
            pltpu.VMEM((nc, pr, 128), F32),
            pltpu.VMEM((nt, pr, 128), F32),
            pltpu.VMEM((nr, pr, 128), F32),
            pltpu.SemaphoreType.DMA((3,)),
        ]
        + sems(2)
        + sems(2)
        + 2 * sems(2, 2)
        + sems(2)
        + sems(2)
        + sems(2, 2)
        + 3 * sems(2)
        + sems(nr * nc)
        + sems(nt)
        + sems(nr * nc)
        + sems(nr)
        + sems(nc)
        + sems(nt)
        + sems(nr),
        compiler_params=pltpu.CompilerParams(
            collective_id=0, has_side_effects=True, vmem_limit_bytes=56 * 1024 * 1024
        ),
        cost_estimate=pl.CostEstimate(
            flops=10 * ni * nj * CH * CH * CZ, bytes_accessed=5 * 1024 * 1024, transcendentals=0
        ),
    )(
        homolog_activation_matrix.reshape(S * rl, CM),
        standardizer_multiplier.reshape(1, CM),
        standardizer_offset.reshape(1, CM),
        side_mapping_matrices.T,
        side_mapping_offsets.reshape(1, 2 * CH),
        final_channel_matrix,
        residue_couple_cotangent.reshape(ni * nj, CZ),
    )
    return (
        results[0].reshape(1, S, rl, CM),
        results[1].T,
        results[2].reshape(2 * CH),
        results[3].reshape(CM),
        results[4].reshape(CM),
        results[5],
        results[6].reshape(CZ),
    )


def solution(mesh):
    placed = (
        P("tgt", None, ("row", "col"), None),
        P(),
        P(),
        P(),
        P(),
        P(),
        P("tgt", "row", "col", None),
    )
    return jax.shard_map(
        per_device,
        mesh=mesh,
        in_specs=placed,
        out_specs=(P("tgt", None, ("row", "col"), None), P(), P(), P(), P(), P(), P()),
        check_vma=False,
    )
```

```python
import functools

import jax
import jax.numpy as jnp
from jax import lax
from jax.experimental import pallas as pl
from jax.experimental.pallas import tpu as pltpu
from jax.sharding import PartitionSpec as P

CM = 256
CH = 32
CZ = 128
S = 128
F32 = jnp.float32
BF16 = jnp.bfloat16
NT_DIMS = (((1,), (1,)), ((), ()))
NN_DIMS = (((1,), (0,)), ((), ()))


def mm(a, b, dims=NN_DIMS):
    return lax.dot_general(a, b, dims, preferred_element_type=F32)


def axis_sizes():
    return lax.axis_size("tgt"), lax.axis_size("row"), lax.axis_size("col")


def axis_places():
    return lax.axis_index("tgt"), lax.axis_index("row"), lax.axis_index("col")


def descriptor(src, dst, send, recv, where):
    return pltpu.make_async_remote_copy(
        src_ref=src,
        dst_ref=dst,
        send_sem=send,
        recv_sem=recv,
        device_id=where,
        device_id_type=pl.DeviceIdType.MESH,
    )


def push(*args):
    descriptor(*args).start()


def sent(*args):
    descriptor(*args).wait_send()


def arrived(*args):
    descriptor(*args).wait_recv()


def greet(nt, nr, nc, t, r, c):
    barrier = pltpu.get_barrier_semaphore()
    flat = r * nc + c
    for k in range(1, nr * nc):
        other = lax.rem(flat + k, nr * nc)
        pl.semaphore_signal(
            barrier,
            inc=1,
            device_id={"row": other // nc, "col": lax.rem(other, nc)},
            device_id_type=pl.DeviceIdType.MESH,
        )
    for k in range(1, nt):
        pl.semaphore_signal(
            barrier,
            inc=1,
            device_id={"tgt": lax.rem(t + k, nt)},
            device_id_type=pl.DeviceIdType.MESH,
        )


def meet(nt, nr, nc):
    pl.semaphore_wait(pltpu.get_barrier_semaphore(), nr * nc - 1 + nt - 1)


def kernel(
    sizes,
    h_ref,
    mult_ref,
    off_ref,
    pm_ref,
    pb_ref,
    w_ref,
    g_ref,
    dx_out,
    pw_out,
    pbias_out,
    gain_out,
    shift_out,
    ow_out,
    ob_out,
    h,
    g,
    nrm,
    inv,
    no,
    lt,
    lmat,
    rt,
    rown,
    rf,
    wf,
    wp,
    pair,
    rp,
    lsum,
    lp,
    ra,
    rb,
    ms,
    rr,
    la,
    lb,
    side,
    on,
    dw,
    dwb,
    obacc,
    a1,
    a3,
    a5,
    grads,
    pwt,
    vec,
    acc,
    sb,
    b1,
    b2,
    b3,
    b4,
    local_sem,
    gl_send,
    gl_recv,
    gl2_send,
    gl2_recv,
    gr1_send,
    gr1_recv,
    gr_send,
    gr_recv,
    gr2_send,
    gr2_recv,
    sr1_send,
    sr1_recv,
    sr2_send,
    sr2_recv,
    sr3_send,
    sr3_recv,
    sl1_send,
    sl1_recv,
    sl2_send,
    sl2_recv,
    a_part_send,
    a_part_recv,
    a_tgt_send,
    a_tgt_recv,
    a_whole_send,
    a_whole_recv,
    b_row_send,
    b_row_recv,
    b_col_send,
    b_col_recv,
    b_tgt_send,
    b_tgt_recv,
    b_row2_send,
    b_row2_recv,
):
    nt, nr, nc, rl = sizes
    rpc = nr // nc
    nx = nr // rpc
    assert nx == nc == 4 and rpc == 2
    ni, nj = rl * nc, rl * nr
    lrows = rl * CH
    t, r, c = axis_places()
    home = lax.div(r, rpc)
    z, x_at, q_at = lax.div(r, nx), lax.rem(r, nx), lax.rem(r, rpc)
    c_half, c_odd = lax.div(c, 2), lax.rem(c, 2)
    side_x = lax.rem(x_at + jnp.where(lax.rem(x_at, 2) == 1, 1, nx - 1), nx)
    via = jnp.where(c_odd == 1, side_x, x_at)
    own = jnp.logical_and(via == x_at, home == c)
    half, lhalf = CH // 2, lrows // 2

    h_in = pltpu.make_async_copy(h_ref, h, local_sem.at[0])
    h_in.start()
    g_in = pltpu.make_async_copy(g_ref, g, local_sem.at[1])
    g_in.start()
    greet(nt, nr, nc, t, r, c)

    mult = mult_ref[...]
    off = off_ref[...]
    pt = pm_ref[...]
    bias = jnp.broadcast_to(pb_ref[...], (S, 2 * CH)).T

    h_in.wait()

    def normalise(k, _):
        rows = pl.ds(pl.multiple_of(k * 128, 128), 128)
        x = h[rows, :].astype(F32)
        centred = x - jnp.mean(x, -1, keepdims=True)
        scale = lax.rsqrt(jnp.mean(centred * centred, -1, keepdims=True) + 1e-05)
        x = centred * scale
        nrm[0, rows, :] = x[:, :128]
        nrm[1, rows, :] = x[:, 128:]
        inv[rows, :] = jnp.broadcast_to(scale, (128, 128))
        return 0

    lax.fori_loop(0, S * rl // 128, normalise, 0, unroll=8)

    def project(k, _):
        at = pl.ds(k, S, stride=rl)
        x = jnp.concatenate([nrm[0, at, :], nrm[1, at, :]], 1)
        row = (x * mult + off).astype(BF16)
        no[pl.ds(pl.multiple_of(k * S, S), S), :] = row
        y = (mm(pt, row, NT_DIMS) + bias).astype(BF16)
        lt[pl.ds(pl.multiple_of(c * lrows + k * CH, CH), CH), :] = y[:CH]
        rf[pl.ds(pl.multiple_of(k * CH, CH), CH), :] = y[CH:].astype(F32)
        return 0

    lax.fori_loop(0, rl, project, 0, unroll=8)

    def turn(d, _):
        rown[d] = rf[pl.ds(d, rl, stride=CH), :].astype(BF16)
        return 0

    lax.fori_loop(0, CH, turn, 0, unroll=8)
    meet(nt, nr, nc)

    def xs(k):
        return lax.rem(x_at + k, nx)

    def cs(k):
        return lax.rem(c + k, nc)

    def to_x(k):
        return {"row": z * nx + xs(1 if k == 0 else nx - 1)}

    def to_c(k):
        return {"col": cs(1 if k == 0 else nc - 1)}

    back_of = (3, 1)

    def left_block(k, part=None):
        at, size = (k * lrows, lrows) if part is None else (k * lrows + part * lhalf, lhalf)
        return lt.at[pl.ds(pl.multiple_of(at, lhalf), size), :]

    def spot(x):
        e = lax.rem(x + nx - 2 * c_odd, nx)
        return lax.div(lax.rem(e + 1, nx), 2), lax.div(e, 2)

    my_q, my_odd = spot(x_at)

    def right_block(x, part):
        q, odd = spot(x)
        return rt.at[part * half : (part + 1) * half, q, :, odd]

    def gather_left(k):
        return left_block(c), left_block(c), gl_send.at[k], gl_recv.at[k], to_c(k)

    def gather_left_in(k):
        at = left_block(cs(back_of[k]))
        return at, at, gl_send.at[k], gl_recv.at[k], to_c(k)

    def relay_left(k):
        at = left_block(cs(back_of[k]), k)
        return at, at, gl2_send.at[k], gl2_recv.at[k], to_c(k)

    def relay_left_in(k):
        at = left_block(cs(2), k)
        return at, at, gl2_send.at[k], gl2_recv.at[k], to_c(k)

    def first_right(k, part):
        rows = slice(part * half, (part + 1) * half)
        to = rt.at[rows, q_at, c_half, c_odd]
        where = {"row": k * nx + via, "col": home}
        return rown.at[rows], to, gr1_send.at[k, part], gr1_recv.at[c_half, part], where

    def first_right_in(k, part):
        rows = slice(part * half, (part + 1) * half)
        to = rt.at[rows, my_q, k, my_odd]
        where = {"row": rpc * c + my_q, "col": 2 * k + my_odd}
        return rown.at[rows], to, gr1_send.at[k, part], gr1_recv.at[k, part], where

    def gather_right(k, part):
        at = right_block(x_at, part)
        return at, at, gr_send.at[k, part], gr_recv.at[k, part], to_x(k)

    def gather_right_in(k, part):
        at = right_block(xs(back_of[k]), part)
        return at, at, gr_send.at[k, part], gr_recv.at[k, part], to_x(k)

    def relay_right(k):
        at = right_block(xs(back_of[k]), k)
        return at, at, gr2_send.at[k], gr2_recv.at[k], to_x(k)

    def relay_right_in(k):
        at = right_block(xs(2), k)
        return at, at, gr2_send.at[k], gr2_recv.at[k], to_x(k)

    def unless(same, act):
        pl.when(jnp.logical_not(jnp.logical_and(own, same)))(act)

    for part in range(2):
        for k in range(rpc):
            unless(z == k, lambda: push(*first_right(k, part)))

    @pl.when(own)
    def _():
        rt[:, q_at, c_half, c_odd] = rown[...]

    for k in range(2):
        push(*gather_left(k))

    wf[...] = w_ref[...].astype(F32)

    def reorder(d, _):
        rows = wf[pl.ds(d, CH, stride=CH), :]
        wp[pl.ds(pl.multiple_of(d * CH, CH), CH), :] = rows.astype(BF16)
        return 0

    lax.fori_loop(0, CH, reorder, 0, unroll=4)
    g_in.wait()
    obacc[...] = jnp.zeros_like(obacc)

    def back(k, _):
        rows = g[pl.ds(pl.multiple_of(k * 2 * nj, 2 * nj), 2 * nj), :]
        y = mm(wp[...], rows, NT_DIMS).astype(BF16)
        for q in range(2):
            at = pl.ds(pl.multiple_of((2 * k + q) * CH, CH), CH)
            for d in range(CH):
                pair[at, d * nj : (d + 1) * nj] = y[d * CH : (d + 1) * CH, q * nj : (q + 1) * nj]
        obacc[...] += jnp.sum(rows.astype(F32).reshape(2 * nj // 8, 8, CZ), 0)
        return 0

    lax.fori_loop(0, 6 * ni // 32, back, 0, unroll=2)
    for k in range(2):
        arrived(*gather_left_in(k))
        push(*relay_left(k))
    lax.fori_loop(6 * ni // 32, 9 * ni // 32, back, 0, unroll=2)
    for k in range(rpc):
        unless(c_half == k, lambda: arrived(*first_right_in(k, 0)))
    for k in range(2):
        push(*gather_right(k, 0))
    lax.fori_loop(9 * ni // 32, 11 * ni // 32, back, 0, unroll=2)
    for k in range(rpc):
        unless(c_half == k, lambda: arrived(*first_right_in(k, 1)))
    for k in range(2):
        push(*gather_right(1 - k, 1))
    lax.fori_loop(11 * ni // 32, ni // 2, back, 0, unroll=2)
    arrived(*gather_right_in(0, 0))
    push(*relay_right(0))

    for k in range(2):
        arrived(*relay_left_in(k))
    def flip(k, _):
        at = pl.ds(pl.multiple_of(k * 128, 128), 128)
        lmat[:, at] = lt[at, :].T
        return 0

    lax.fori_loop(0, ni * CH // 128, flip, 0, unroll=8)

    def right_step(k, _):
        lanes = pl.ds(pl.multiple_of(k * 8 * nj, 8 * nj), 8 * nj)
        y = mm(lmat[...], pair[:, lanes]).T
        rp[pl.ds(8 * k, 8)] = y.reshape(8, 2, 2, 2, rl, S).astype(BF16)
        return 0

    def right_sum(x, part):
        q, odd = spot(x)
        return rp.at[part * half : (part + 1) * half, q, :, odd]

    def far_right(k):
        return right_sum(xs(2), k), ra.at[k], sr1_send.at[k], sr1_recv.at[k], to_x(k)

    def near_right(k, part):
        at = right_sum(xs(1 if k == 0 else 3), part)
        to = rb.at[k, part * half : (part + 1) * half]
        return at, to, sr2_send.at[k, part], sr2_recv.at[k, part], to_x(k)

    def scatter_right(k):
        where = {"row": rpc * c + my_q, "col": 2 * k + my_odd}
        return ms.at[k], rr.at[z], sr3_send.at[k], sr3_recv.at[z], where

    def scatter_right_in(k):
        where = {"row": k * nx + via, "col": home}
        return ms.at[k], rr.at[k], sr3_send.at[k], sr3_recv.at[k], where

    lax.fori_loop(0, CH // 16, right_step, 0)
    push(*far_right(0))
    push(*near_right(1, 0))
    arrived(*gather_right_in(1, 1))
    push(*relay_right(1))
    lax.fori_loop(CH // 16, CH // 8, right_step, 0)
    push(*far_right(1))
    push(*near_right(0, 1))

    arrived(*gather_right_in(1, 0))
    arrived(*relay_right_in(0))

    def left_rows(k):
        return pl.ds(pl.multiple_of(k * lrows, lrows), lrows)

    def far_left(k):
        at = lp.at[cs(2), k * lhalf : (k + 1) * lhalf]
        return at, la.at[k], sl1_send.at[k], sl1_recv.at[k], to_c(k)

    def near_left(k):
        at = lp.at[cs(1 if k == 0 else 3)]
        return at, lb.at[k], sl2_send.at[k], sl2_recv.at[k], to_c(k)

    def left_first(k, _):
        lsum[k] = mm(pair[left_rows(k), : half * nj], rt[:half].reshape(half * nj, S))
        return 0

    lax.fori_loop(0, nc, left_first, 0)
    for k in range(2):
        arrived(*far_right(k))
        at = right_sum(xs(1 if k == 0 else 3), k)
        at[...] = (at[...].astype(F32) + ra[k].astype(F32)).astype(BF16)
        push(*near_right(k, k))
    arrived(*gather_right_in(0, 1))
    arrived(*relay_right_in(1))

    def left_step(k, _):
        more = mm(pair[left_rows(k), half * nj :], rt[half:].reshape(half * nj, S))
        lp[k] = (lsum[k] + more).astype(BF16)
        return 0

    left_step(cs(2), 0)
    for k in range(2):
        push(*far_left(k))
    left_step(cs(1), 0)
    left_step(cs(3), 0)
    for k in range(2):
        arrived(*far_left(k))
    for k in range(2):
        at = lp.at[cs(1 if k == 0 else 3), k * lhalf : (k + 1) * lhalf]
        at[...] = (at[...].astype(F32) + la[k].astype(F32)).astype(BF16)
        push(*near_left(k))
    left_step(c, 0)

    dw[...] = jnp.zeros_like(dw)

    def weigh(k, _):
        rows = lt[pl.ds(pl.multiple_of(k * 8 * CH, 8 * CH), 8 * CH), :]
        for v in range(8):
            part = rt[v * 4 : (v + 1) * 4].reshape(4 * nj, S)
            y = mm(rows, part, NT_DIMS).astype(BF16)
            for q in range(8):
                for d in range(4):
                    on[(v * 4 + d) * CH : (v * 4 + d + 1) * CH, q * nj : (q + 1) * nj] = y[
                        q * CH : (q + 1) * CH, d * nj : (d + 1) * nj
                    ]
        dw[...] += mm(on[...], g[pl.ds(pl.multiple_of(k * 8 * nj, 8 * nj), 8 * nj), :])
        return 0

    lax.fori_loop(0, ni // 32, weigh, 0)
    for k in range(2):
        for part in range(2):
            arrived(*near_right(k, part))
    for k in range(rpc):
        total = rp[:, my_q, k, my_odd].astype(F32)
        total += rb[0, :, k].astype(F32)
        total += rb[1, :, k].astype(F32)
        ms[k] = total.astype(BF16)
    for k in range(rpc):
        unless(c_half == k, lambda: push(*scatter_right(k)))

    @pl.when(own)
    def _():
        rr[z] = ms[c_half]

    lax.fori_loop(ni // 32, ni // 8, weigh, 0)

    group = nr * nc
    flat = r * nc + c

    def member(k):
        f = lax.rem(flat + k, group)
        return f, {"row": lax.div(f, nc), "col": lax.rem(f, nc)}

    def a_part(k):
        f, where = member(k)
        src = dwb.at[pl.ds(pl.multiple_of(f * CH, CH), CH), :]
        return src, a1.at[flat], a_part_send.at[k], a_part_recv.at[flat], where

    def a_part_in(k):
        f, where = member(k)
        src = dwb.at[pl.ds(pl.multiple_of(flat * CH, CH), CH), :]
        return src, a1.at[f], a_part_send.at[k], a_part_recv.at[f], where

    def a_whole(k):
        _, where = member(k)
        return a5.at[flat], a5.at[flat], a_whole_send.at[k], a_whole_recv.at[flat], where

    def a_whole_in(k):
        f, where = member(k)
        return a5.at[f], a5.at[f], a_whole_send.at[k], a_whole_recv.at[f], where

    def every(act, copy):
        def step(k, _):
            act(*copy(k))
            return 0

        lax.fori_loop(1, group, step, 0)

    dwb[...] = dw[...].astype(BF16)
    every(push, a_part)
    a1[flat] = dwb[pl.ds(pl.multiple_of(flat * CH, CH), CH), :]

    for k in range(2):
        arrived(*near_left(k))
    def sum_left(k, _):
        at = pl.ds(pl.multiple_of(k * 128, 128), 128)
        total = lp[c, at, :].astype(F32)
        for q in range(2):
            total += lb[q, at, :].astype(F32)
        side[at, :] = total * (1.0 / S)
        return 0

    lax.fori_loop(0, lrows // 128, sum_left, 0, unroll=4)

    for k in range(rpc):
        unless(z == k, lambda: arrived(*scatter_right_in(k)))

    def sum_right(k, _):
        at = pl.ds(k * 8, 8)
        total = rr[0, at].astype(F32)
        for q in range(1, rpc):
            total += rr[q, at].astype(F32)
        to = pl.ds(pl.multiple_of(lrows + k * 8 * rl, 8 * rl), 8 * rl)
        side[to, :] = total.reshape(8 * rl, S) * (1.0 / S)
        return 0

    lax.fori_loop(0, CH // 8, sum_right, 0, unroll=4)

    pwt[...] = jnp.zeros_like(pwt)
    acc[...] = jnp.zeros_like(acc)

    def finish(k, _):
        left = side[pl.ds(pl.multiple_of(k * CH, CH), CH), :]
        right = side[pl.ds(lrows + k, CH, stride=rl), :]
        both = jnp.concatenate([left, right], 0)
        rounded = both.astype(BF16)
        turned = both.T
        acc[:, 2 * CM : 2 * CM + 2 * CH] += jnp.sum(turned.reshape(S // 8, 8, 2 * CH), 0)
        grad = mm(turned.astype(BF16), pt)
        grads[pl.ds(pl.multiple_of(k * S, S), S), :] = grad
        pwt[...] += mm(rounded, no[pl.ds(pl.multiple_of(k * S, S), S), :])
        at = pl.ds(k, S, stride=rl)
        x = jnp.concatenate([nrm[0, at, :], nrm[1, at, :]], 1)
        acc[:, :CM] += jnp.sum((grad * x).reshape(S // 8, 8, CM), 0)
        acc[:, CM : 2 * CM] += jnp.sum(grad.reshape(S // 8, 8, CM), 0)
        return 0

    lax.fori_loop(0, rl, finish, 0, unroll=8)

    pr = 2 * 2 * CH // nr
    vr = 8 // nr
    vec[...] = jnp.zeros_like(vec)
    small = jnp.sum(acc[...], 0, keepdims=True)
    vec[0:1, : 2 * CH] = small[:, 2 * CM : 2 * CM + 2 * CH]
    for k in range(4):
        vec[1 + k : 2 + k, :] = small[:, k * 128 : (k + 1) * 128]
    vec[5:6, :] = jnp.sum(obacc[...], 0, keepdims=True)
    weights = pwt[...]
    stacked = jnp.concatenate([weights[:, :128], weights[:, 128:]], 0)
    sb[...] = jnp.zeros_like(sb)
    for q in range(nr):
        sb[q, :pr, :] = stacked[q * pr : (q + 1) * pr]
        sb[q, pr : pr + vr, :] = vec[q * vr : (q + 1) * vr, :]

    def b_row(k):
        q = lax.rem(r + k, nr)
        return sb.at[q], b1.at[r], b_row_send.at[k], b_row_recv.at[r], {"row": q}

    def b_row_in(k):
        q = lax.rem(r + k, nr)
        return sb.at[q], b1.at[q], b_row_send.at[k], b_row_recv.at[q], {"row": q}

    for k in range(1, nr):
        push(*b_row(k))
    b1[r] = sb[r]

    def descend(k, _):
        grad = grads[pl.ds(pl.multiple_of(k * S, S), S), :]
        at = pl.ds(k, S, stride=rl)
        x = jnp.concatenate([nrm[0, at, :], nrm[1, at, :]], 1)
        scale = inv[at, :]
        scaled = grad * mult
        dx = scaled - jnp.mean(scaled, -1, keepdims=True) - x * jnp.mean(scaled * x, -1, keepdims=True)
        nrm[0, at, :] = dx[:, :128] * scale
        nrm[1, at, :] = dx[:, 128:] * scale
        return 0

    lax.fori_loop(0, rl // 2, descend, 0, unroll=8)

    every(arrived, a_part_in)
    total = a1[0].astype(F32)
    for q in range(1, group):
        total += a1[q].astype(F32)
    a3[t] = total

    def a_tgt(k):
        q = lax.rem(t + k, nt)
        return a3.at[t], a3.at[t], a_tgt_send.at[k], a_tgt_recv.at[t], {"tgt": q}

    def a_tgt_in(k):
        q = lax.rem(t + k, nt)
        return a3.at[q], a3.at[q], a_tgt_send.at[k], a_tgt_recv.at[q], {"tgt": q}

    for k in range(1, nt):
        push(*a_tgt(k))


    for k in range(1, nr):
        arrived(*b_row_in(k))
    total = b1[0]
    for q in range(1, nr):
        total += b1[q]
    b2[c] = total

    def b_col(k):
        q = lax.rem(c + k, nc)
        return b2.at[c], b2.at[c], b_col_send.at[k], b_col_recv.at[c], {"col": q}

    def b_col_in(k):
        q = lax.rem(c + k, nc)
        return b2.at[q], b2.at[q], b_col_send.at[k], b_col_recv.at[q], {"col": q}

    for k in range(1, nc):
        push(*b_col(k))

    lax.fori_loop(rl // 2, rl, descend, 0, unroll=8)

    def emit(k, _):
        rows = pl.ds(pl.multiple_of(k * 128, 128), 128)
        h[rows, :128] = nrm[0, rows, :].astype(BF16)
        h[rows, 128:] = nrm[1, rows, :].astype(BF16)
        return 0

    lax.fori_loop(0, S * rl // 128, emit, 0, unroll=4)
    dx_copy = pltpu.make_async_copy(h, dx_out, local_sem.at[2])
    dx_copy.start()

    for k in range(1, nc):
        arrived(*b_col_in(k))
    total = b2[0]
    for q in range(1, nc):
        total += b2[q]
    b3[t] = total

    def b_tgt(k):
        q = lax.rem(t + k, nt)
        return b3.at[t], b3.at[t], b_tgt_send.at[k], b_tgt_recv.at[t], {"tgt": q}

    def b_tgt_in(k):
        q = lax.rem(t + k, nt)
        return b3.at[q], b3.at[q], b_tgt_send.at[k], b_tgt_recv.at[q], {"tgt": q}

    for k in range(1, nt):
        push(*b_tgt(k))

    for k in range(1, nt):
        arrived(*a_tgt_in(k))
    total = a3[0]
    for q in range(1, nt):
        total += a3[q]
    a5[flat] = total.astype(BF16)
    every(push, a_whole)

    for k in range(1, nt):
        arrived(*b_tgt_in(k))
    total = b3[0]
    for q in range(1, nt):
        total += b3[q]
    b4[r] = total

    def b_row2(k):
        q = lax.rem(r + k, nr)
        return b4.at[r], b4.at[r], b_row2_send.at[k], b_row2_recv.at[r], {"row": q}

    def b_row2_in(k):
        q = lax.rem(r + k, nr)
        return b4.at[q], b4.at[q], b_row2_send.at[k], b_row2_recv.at[q], {"row": q}

    for k in range(1, nr):
        push(*b_row2(k))

    factor = 1.0 / (nt * nr * nc * rl)
    every(arrived, a_whole_in)

    def place(d, _):
        ow_out[pl.ds(d, CH, stride=CH), :] = a5[d].astype(F32) * (factor / S)
        return 0

    lax.fori_loop(0, CH, place, 0, unroll=4)

    for k in range(2):
        sent(*gather_left(k))
        sent(*relay_left(k))
        sent(*relay_right(k))
        sent(*far_right(k))
        sent(*far_left(k))
        sent(*near_left(k))
        for part in range(2):
            sent(*gather_right(k, part))
            sent(*near_right(k, part))
            unless(z == k, lambda: sent(*first_right(k, part)))
        unless(c_half == k, lambda: sent(*scatter_right(k)))
    every(sent, a_part)
    for k in range(1, nc):
        sent(*b_col(k))
    for k in range(1, nr):
        sent(*b_row(k))
    for k in range(1, nt):
        sent(*a_tgt(k))
        sent(*b_tgt(k))
    dx_copy.wait()
    for k in range(1, nr):
        arrived(*b_row2_in(k))
    whole = b4[:, :pr, :].reshape(4 * CH, 128) * factor
    pw_out[:, :128] = whole[: 2 * CH]
    pw_out[:, 128:] = whole[2 * CH :]
    for q in range(nr):
        vec[q * vr : (q + 1) * vr, :] = b4[q, pr : pr + vr, :] * factor
    pbias_out[...] = vec[0:1, : 2 * CH]
    gain_out[...] = jnp.concatenate([vec[1:2, :], vec[2:3, :]], 1)
    shift_out[...] = jnp.concatenate([vec[3:4, :], vec[4:5, :]], 1)
    ob_out[...] = vec[5:6, :]

    every(sent, a_whole)
    for k in range(1, nr):
        sent(*b_row2(k))


def per_device(
    homolog_activation_matrix,
    standardizer_multiplier,
    standardizer_offset,
    side_mapping_matrices,
    side_mapping_offsets,
    final_channel_matrix,
    residue_couple_cotangent,
):
    nt, nr, nc = axis_sizes()
    rl = homolog_activation_matrix.shape[2]
    ni, nj = rl * nc, rl * nr
    pr = 4 * CH // nr + 8
    vmem = functools.partial(pl.BlockSpec, memory_space=pltpu.VMEM)
    hbm = functools.partial(pl.BlockSpec, memory_space=pl.ANY)

    def sems(*n):
        return [pltpu.SemaphoreType.DMA(n), pltpu.SemaphoreType.DMA(n)]

    results = pl.pallas_call(
        functools.partial(kernel, (nt, nr, nc, rl)),
        out_shape=(
            jax.ShapeDtypeStruct((S * rl, CM), BF16),
            jax.ShapeDtypeStruct((2 * CH, CM), F32),
            jax.ShapeDtypeStruct((1, 2 * CH), F32),
            jax.ShapeDtypeStruct((1, CM), F32),
            jax.ShapeDtypeStruct((1, CM), F32),
            jax.ShapeDtypeStruct((CH * CH, CZ), F32),
            jax.ShapeDtypeStruct((1, CZ), F32),
        ),
        in_specs=[hbm(), vmem(), vmem(), vmem(), vmem(), vmem(), hbm()],
        out_specs=(hbm(), vmem(), vmem(), vmem(), vmem(), vmem(), vmem()),
        scratch_shapes=[
            pltpu.VMEM((S * rl, CM), BF16),
            pltpu.VMEM((ni * nj, CZ), BF16),
            pltpu.VMEM((2, S * rl, 128), F32),
            pltpu.VMEM((S * rl, 128), F32),
            pltpu.VMEM((S * rl, CM), BF16),
            pltpu.VMEM((ni * CH, S), BF16),
            pltpu.VMEM((S, ni * CH), BF16),
            pltpu.VMEM((CH, 2, 2, 2, rl, S), BF16),
            pltpu.VMEM((CH, rl, S), BF16),
            pltpu.VMEM((rl * CH, S), F32),
            pltpu.VMEM((CH * CH, CZ), F32),
            pltpu.VMEM((CH * CH, CZ), BF16),
            pltpu.VMEM((ni * CH, CH * nj), BF16),
            pltpu.VMEM((CH, 2, 2, 2, rl, S), BF16),
            pltpu.VMEM((nc, rl * CH, S), F32),
            pltpu.VMEM((nc, rl * CH, S), BF16),
            pltpu.VMEM((2, CH // 2, 2, rl, S), BF16),
            pltpu.VMEM((2, CH, 2, rl, S), BF16),
            pltpu.VMEM((2, CH, rl, S), BF16),
            pltpu.VMEM((2, CH, rl, S), BF16),
            pltpu.VMEM((2, rl * CH // 2, S), BF16),
            pltpu.VMEM((2, rl * CH, S), BF16),
            pltpu.VMEM((2 * rl * CH, S), F32),
            pltpu.VMEM((CH * CH, 8 * nj), BF16),
            pltpu.VMEM((CH * CH, CZ), F32),
            pltpu.VMEM((CH * CH, CZ), BF16),
            pltpu.VMEM((8, CZ), F32),
            pltpu.VMEM((nr * nc, CH, CZ), BF16),
            pltpu.VMEM((nt, CH, CZ), F32),
            pltpu.VMEM((nr * nc, CH, CZ), BF16),
            pltpu.VMEM((S * rl, CM), F32),
            pltpu.VMEM((2 * CH, CM), F32),
            pltpu.VMEM((8, 128), F32),
            pltpu.VMEM((8, 2 * CM + 128), F32),
            pltpu.VMEM((nr, pr, 128), F32),
            pltpu.VMEM((nr, pr, 128), F32),
            pltpu.VMEM((nc, pr, 128), F32),
            pltpu.VMEM((nt, pr, 128), F32),
            pltpu.VMEM((nr, pr, 128), F32),
            pltpu.SemaphoreType.DMA((3,)),
        ]
        + sems(2)
        + sems(2)
        + 2 * sems(2, 2)
        + sems(2)
        + sems(2)
        + sems(2, 2)
        + 3 * sems(2)
        + sems(nr * nc)
        + sems(nt)
        + sems(nr * nc)
        + sems(nr)
        + sems(nc)
        + sems(nt)
        + sems(nr),
        compiler_params=pltpu.CompilerParams(
            collective_id=0, has_side_effects=True, vmem_limit_bytes=56 * 1024 * 1024
        ),
        cost_estimate=pl.CostEstimate(
            flops=10 * ni * nj * CH * CH * CZ, bytes_accessed=5 * 1024 * 1024, transcendentals=0
        ),
    )(
        homolog_activation_matrix.reshape(S * rl, CM),
        standardizer_multiplier.reshape(1, CM),
        standardizer_offset.reshape(1, CM),
        side_mapping_matrices.T,
        side_mapping_offsets.reshape(1, 2 * CH),
        final_channel_matrix,
        residue_couple_cotangent.reshape(ni * nj, CZ),
    )
    return (
        results[0].reshape(1, S, rl, CM),
        results[1].T,
        results[2].reshape(2 * CH),
        results[3].reshape(CM),
        results[4].reshape(CM),
        results[5],
        results[6].reshape(CZ),
    )


def solution(mesh):
    placed = (
        P("tgt", None, ("row", "col"), None),
        P(),
        P(),
        P(),
        P(),
        P(),
        P("tgt", "row", "col", None),
    )
    return jax.shard_map(
        per_device,
        mesh=mesh,
        in_specs=placed,
        out_specs=(P("tgt", None, ("row", "col"), None), P(), P(), P(), P(), P(), P()),
        check_vma=False,
    )
```
